32 devices in a mesh: img: 8 (over z, y), blk: 4 (over x, core).
Axes of the slice: x: 2, y: 2, z: 4, core: 2. Of those that a mesh axis runs over, the one named last changes fastest.
Arguments:
- x_small: bfloat16 [32, 196, 768], P('img', 'blk'), may hold values from -6 to 6
- x_large: bfloat16 [48, 576, 768], P('img', 'blk'), may hold values from -6 to 6
- live_counts: int32 [8, 2], P('img'), may hold values from 1 to 6, as said below
- ln1_gain: float32 [768], replicated, may hold values from 0.1 to 1.9
- ln1_bias: float32 [768], replicated, may hold values from -1.5 to 1.5
- tok_w1_small: bfloat16 [196, 384], P('blk'), may hold values from -0.4375 to 0.4375
- tok_b1_small: float32 [384], replicated, may hold values from -2.5 to 2.5
- tok_w2_small: bfloat16 [384, 196], P(None, 'blk'), may hold values from -0.3125 to 0.3125
- tok_b2_small: float32 [196], P('blk'), may hold values from -2.5 to 2.5
- tok_w1_large: bfloat16 [576, 384], P('blk'), may hold values from -0.25 to 0.25
- tok_b1_large: float32 [384], replicated, may hold values from -2.5 to 2.5
- tok_w2_large: bfloat16 [384, 576], P(None, 'blk'), may hold values from -0.3125 to 0.3125
- tok_b2_large: float32 [576], P('blk'), may hold values from -2.5 to 2.5
- ln2_gain: float32 [768], replicated, may hold values from 0.1 to 1.9
- ln2_bias: float32 [768], replicated, may hold values from -1.5 to 1.5
- ch_w1: bfloat16 [768, 3072], replicated, may hold values from -0.21875 to 0.21875
- ch_b1: float32 [3072], replicated, may hold values from -2.5 to 2.5
- ch_w2: bfloat16 [3072, 768], replicated, may hold values from -0.109375 to 0.109375
- ch_b2: float32 [768], replicated, may hold values from -2.5 to 2.5
- cot_small: bfloat16 [32, 196, 768], P('img', 'blk'), may hold values from -6 to 6
- cot_large: bfloat16 [48, 576, 768], P('img', 'blk'), may hold values from -6 to 6
Outputs:
- out_small: bfloat16 [32, 196, 768], P('img', 'blk')
- out_large: bfloat16 [48, 576, 768], P('img', 'blk')
- grad_x_small: float32 [32, 196, 768], P('img', 'blk')
- grad_x_large: float32 [48, 576, 768], P('img', 'blk')
- grad_ln1_gain: float32 [768], replicated
- grad_ln1_bias: float32 [768], replicated
- grad_tok_w1_small: float32 [196, 384], P('blk')
- grad_tok_b1_small: float32 [384], replicated
- grad_tok_w2_small: float32 [384, 196], P(None, 'blk')
- grad_tok_b2_small: float32 [196], P('blk')
- grad_tok_w1_large: float32 [576, 384], P('blk')
- grad_tok_b1_large: float32 [384], replicated
- grad_tok_w2_large: float32 [384, 576], P(None, 'blk')
- grad_tok_b2_large: float32 [576], P('blk')
- grad_ln2_gain: float32 [768], replicated
- grad_ln2_bias: float32 [768], replicated
- grad_ch_w1: float32 [768, 3072], replicated
- grad_ch_b1: float32 [3072], replicated
- grad_ch_w2: float32 [3072, 768], replicated
- grad_ch_b2: float32 [768], replicated
The draws below stay inside these ranges and needn't reach their ends.
Inputs may be any that keep to these rules, and one draw needn't show every extreme that they name: `live_counts`: row i gives how many of the 4 224 px slots and of the 6 384 px slots of img index i hold live images; live slots come first, the others are empty. In every draw some index has all slots of both groups live and another has one of each.
All inputs are finite; a program needn't handle non-finite values.
Results may differ from the reference program's by a relative error of at most 0.007.
Values may be sent and summed in bfloat16 or wider, within the bound.
A program may use at most 192 MiB of HBM per device.

```python
import jax
import jax.numpy as jnp
from jax import lax

D = 768
DS = 384
DC = 3072
PS = 196
PL = 576
CS = 4
CL = 6
NS = 32
NL = 48
N_IMG = 8


def draw_live_counts(key, part):
    key = jax.random.fold_in(key, 11)
    key_small, key_large, key_order = jax.random.split(key, 3)
    small_live = jax.random.randint(key_small, (N_IMG,), 1, CS + 1)
    large_live = jax.random.randint(key_large, (N_IMG,), 1, CL + 1)
    order = jax.random.permutation(key_order, N_IMG)
    small_live = small_live.at[order[0]].set(CS).at[order[1]].set(1)
    large_live = large_live.at[order[0]].set(CL).at[order[1]].set(1)
    return jnp.stack([small_live, large_live], axis=1).astype(jnp.int32)


def block_scale(own_key, extent, cuts, low, largest):
    def one(axis_at, parts):
        heights = jax.random.uniform(jax.random.fold_in(jax.random.fold_in(own_key, 6), axis_at), (parts,), jnp.float32, low / len(cuts), largest / len(cuts))
        return jnp.repeat(jnp.exp(heights), extent[axis_at] // parts).reshape((-1,) + (1,) * (len(extent) - axis_at - 1))

    factor_of = one(*cuts[0])
    for cut in cuts[1:]:
        factor_of = factor_of * one(*cut)
    return factor_of


def bell_draw(own_key, extent, scale, reach, cuts=(), kind=jnp.bfloat16):
    loudness = block_scale(own_key, extent, cuts, -0.22, 0.18) if cuts else 1.0
    values = jax.random.normal(own_key, extent, jnp.float32) * scale * loudness
    return jnp.minimum(jnp.maximum(values, -reach), reach).astype(kind)


def setup_inputs(seed: int = 0) -> dict:
    arg_keys = jax.random.split(jax.random.key(seed), 22)
    return {
        "x_small": bell_draw(arg_keys[0], (NS, PS, D), 1.0, 6.0, ((0, 8), (1, 4))),
        "x_large": bell_draw(arg_keys[1], (NL, PL, D), 1.0, 6.0, ((0, 8), (1, 4))),
        "live_counts": draw_live_counts(jax.random.fold_in(arg_keys[21], 71), 0),
        "ln1_gain": jnp.clip(1.0 + 0.18 * jax.random.normal(arg_keys[3], (D,), jnp.float32), 0.1, 1.9),
        "ln1_bias": bell_draw(arg_keys[4], (D,), 0.3, 1.5, (), jnp.float32),
        "tok_w1_small": bell_draw(arg_keys[5], (PS, DS), PS ** -0.5, 0.4375, ((0, 4),)),
        "tok_b1_small": bell_draw(arg_keys[6], (DS,), 0.5, 2.5, (), jnp.float32),
        "tok_w2_small": bell_draw(arg_keys[7], (DS, PS), DS ** -0.5, 0.3125, ((1, 4),)),
        "tok_b2_small": bell_draw(arg_keys[8], (PS,), 0.5, 2.5, ((0, 4),), jnp.float32),
        "tok_w1_large": bell_draw(arg_keys[9], (PL, DS), PL ** -0.5, 0.25, ((0, 4),)),
        "tok_b1_large": bell_draw(arg_keys[10], (DS,), 0.5, 2.5, (), jnp.float32),
        "tok_w2_large": bell_draw(arg_keys[11], (DS, PL), DS ** -0.5, 0.3125, ((1, 4),)),
        "tok_b2_large": bell_draw(arg_keys[12], (PL,), 0.5, 2.5, ((0, 4),), jnp.float32),
        "ln2_gain": jnp.clip(1.0 + 0.18 * jax.random.normal(arg_keys[13], (D,), jnp.float32), 0.1, 1.9),
        "ln2_bias": bell_draw(arg_keys[14], (D,), 0.3, 1.5, (), jnp.float32),
        "ch_w1": bell_draw(arg_keys[15], (D, DC), D ** -0.5, 0.21875),
        "ch_b1": bell_draw(arg_keys[16], (DC,), 0.5, 2.5, (), jnp.float32),
        "ch_w2": bell_draw(arg_keys[17], (DC, D), DC ** -0.5, 0.109375),
        "ch_b2": bell_draw(arg_keys[18], (D,), 0.5, 2.5, (), jnp.float32),
        "cot_small": bell_draw(arg_keys[19], (NS, PS, D), 1.0, 6.0, ((0, 8), (1, 4))),
        "cot_large": bell_draw(arg_keys[20], (NL, PL, D), 1.0, 6.0, ((0, 8), (1, 4))),
    }


@jax.custom_vjp
def low(v):
    return lax.optimization_barrier(v.astype(jnp.bfloat16)).astype(jnp.float32)

@jax.custom_vjp
def low_back(v):
    return v

def low_keep(v):
    return (low(v), None)

def low_pass(kept, grad):
    return (grad,)

def back_keep(v):
    return (v, None)

def back_low(kept, grad):
    return (low(grad),)
low.defvjp(low_keep, low_pass)
low_back.defvjp(back_keep, back_low)
EPSILON = 1e-06

def norm_rows(values, scales, shifts):
    row_mean = lax.optimization_barrier(jnp.mean(values, axis=-1, keepdims=True))
    centered = values - row_mean
    row_var = lax.optimization_barrier(jnp.mean(centered * centered, axis=-1, keepdims=True))
    return centered * lax.rsqrt(row_var + EPSILON) * scales + shifts

def token_branch(normed, w_first, b_first, w_second, b_second):
    preact = low_back(jnp.einsum('nsd,sj->ndj', low(normed), w_first, precision=lax.Precision.HIGHEST) + b_first)
    hidden = low(jax.nn.gelu(preact))
    mixed = jnp.einsum('ndj,js->nsd', hidden, w_second, precision=lax.Precision.HIGHEST) + b_second[:, None]
    return low_back(mixed)

def channel_branch(rows_in, w_first, b_first, w_second, b_second):
    activation = low_back(jnp.dot(low(rows_in), w_first, precision=lax.Precision.HIGHEST) + b_first)
    hidden = low(jax.nn.gelu(activation))
    return low_back(jnp.dot(hidden, w_second, precision=lax.Precision.HIGHEST) + b_second)

def device_block(params, small_in, large_in, mask_small, mask_large):
    gain_one, shift_one, w1_small, b1_small, w2_small, b2_small, w1_large, b1_large, w2_large, b2_large, gain_two, shift_two, chan_w1, chan_b1, chan_w2, chan_b2 = params
    mid_small = small_in + token_branch(norm_rows(small_in, gain_one, shift_one), w1_small, b1_small, w2_small, b2_small)
    mid_large = large_in + token_branch(norm_rows(large_in, gain_one, shift_one), w1_large, b1_large, w2_large, b2_large)
    model_width = small_in.shape[2]
    rows_mid = jnp.concatenate([mid_small.reshape(-1, model_width), mid_large.reshape(-1, model_width)], axis=0)
    result = rows_mid + channel_branch(norm_rows(rows_mid, gain_two, shift_two), chan_w1, chan_b1, chan_w2, chan_b2)
    row_mask = jnp.concatenate([jnp.repeat(mask_small, PS), jnp.repeat(mask_large, PL)])
    result = result * row_mask[:, None]
    split_at = mask_small.shape[0] * PS
    return (result[:split_at].reshape(mid_small.shape), result[split_at:].reshape(mid_large.shape))

def reference(x_small, x_large, live_counts, ln1_gain, ln1_bias, tok_w1_small, tok_b1_small, tok_w2_small, tok_b2_small, tok_w1_large, tok_b1_large, tok_w2_large, tok_b2_large, ln2_gain, ln2_bias, ch_w1, ch_b1, ch_w2, ch_b2, cot_small, cot_large):
    params = tuple((weight.astype(jnp.float32) for weight in (ln1_gain, ln1_bias, tok_w1_small, tok_b1_small, tok_w2_small, tok_b2_small, tok_w1_large, tok_b1_large, tok_w2_large, tok_b2_large, ln2_gain, ln2_bias, ch_w1, ch_b1, ch_w2, ch_b2)))
    mask_small = (jnp.arange(CS, dtype=jnp.int32)[None, :] < live_counts[:, 0:1]).astype(jnp.float32)
    mask_large = (jnp.arange(CL, dtype=jnp.int32)[None, :] < live_counts[:, 1:2]).astype(jnp.float32)
    small_in = x_small.astype(jnp.float32).reshape(N_IMG, CS, PS, D)
    large_in = x_large.astype(jnp.float32).reshape(N_IMG, CL, PL, D)

    def forward(weights, small_all, large_all):

        def one_device(pieces):
            return jax.checkpoint(device_block)(weights, pieces[0], pieces[1], pieces[2], pieces[3])
        return lax.map(one_device, (small_all, large_all, mask_small, mask_large))
    outputs, pullback = jax.vjp(forward, params, small_in, large_in)
    cotangents = (cot_small.astype(jnp.float32).reshape(N_IMG, CS, PS, D), cot_large.astype(jnp.float32).reshape(N_IMG, CL, PL, D))
    grads, grad_small, grad_large = pullback(cotangents)
    return (outputs[0].reshape(NS, PS, D).astype(jnp.bfloat16), outputs[1].reshape(NL, PL, D).astype(jnp.bfloat16), grad_small.reshape(NS, PS, D), grad_large.reshape(NL, PL, D), grads[0], grads[1], grads[2], grads[3], grads[4], grads[5], grads[6], grads[7], grads[8], grads[9], grads[10], grads[11], grads[12], grads[13], grads[14], grads[15])
```

```python
import jax
import jax.numpy as jnp
from jax import lax
from jax.sharding import PartitionSpec as P

EPSILON = 1e-06
LANES = 128
BF = jnp.bfloat16
F32 = jnp.float32


def norm_rows(values, scales, shifts):
    row_mean = jnp.mean(values, axis=-1, keepdims=True)
    centered = values - row_mean
    row_var = jnp.mean(centered * centered, axis=-1, keepdims=True)
    return centered * lax.rsqrt(row_var + EPSILON) * scales + shifts


def gelu_back(preact, upstream):
    unused, pullback = jax.vjp(jax.nn.gelu, preact)
    return pullback(upstream)[0]


def to_columns(rows):
    count, patches, width = rows.shape
    blocks = rows.reshape(count, patches, width // LANES, LANES).transpose(0, 2, 1, 3)
    blocks = blocks.reshape(count * (width // LANES), patches, LANES)
    size = lax.axis_size("blk")
    moved = lax.all_to_all(blocks, "blk", 0, 0, tiled=True)
    share = moved.shape[0] // size
    moved = moved.reshape(size, share, patches, LANES).transpose(0, 2, 1, 3)
    return moved.reshape(size * patches, share * LANES)


def to_rows(columns, shape):
    count, patches, width = shape
    size = lax.axis_size("blk")
    share = columns.shape[1] // LANES
    blocks = columns.reshape(size, patches, share, LANES).transpose(0, 2, 1, 3)
    blocks = blocks.reshape(size * share, patches, LANES)
    moved = lax.all_to_all(blocks, "blk", 0, 0, tiled=True)
    moved = moved.reshape(count, width // LANES, patches, LANES).transpose(0, 2, 1, 3)
    return moved.reshape(shape)


def mm(spec, left, right):
    return jnp.einsum(spec, left, right, preferred_element_type=F32)


def sum_low(values, axes):
    return lax.psum(values.astype(BF), axes).astype(F32)


def local(
    x_small, x_large, live_counts, ln1_gain, ln1_bias,
    tok_w1_small, tok_b1_small, tok_w2_small, tok_b2_small,
    tok_w1_large, tok_b1_large, tok_w2_large, tok_b2_large,
    ln2_gain, ln2_bias, ch_w1, ch_b1, ch_w2, ch_b2, cot_small, cot_large,
):
    width = x_small.shape[2]
    mask_small = (jnp.arange(x_small.shape[0]) < live_counts[0, 0]).astype(F32)
    mask_large = (jnp.arange(x_large.shape[0]) < live_counts[0, 1]).astype(F32)
    groups = []
    for x, w1, b1, w2, b2 in (
        (x_small, tok_w1_small, tok_b1_small, tok_w2_small, tok_b2_small),
        (x_large, tok_w1_large, tok_b1_large, tok_w2_large, tok_b2_large),
    ):
        wide = x.astype(F32)
        normed, back = jax.vjp(norm_rows, wide, ln1_gain, ln1_bias)
        w1_all = lax.all_gather(w1, "blk", axis=0, tiled=True)
        w2_all = lax.all_gather(w2, "blk", axis=1, tiled=True)
        u_cols = to_columns(normed.astype(BF))
        preact = mm("sj,sd->jd", w1_all, u_cols) + b1[:, None]
        hidden = jax.nn.gelu(preact).astype(BF)
        mixed = to_rows(mm("js,jd->sd", w2_all, hidden).astype(BF), x.shape)
        mid = wide + mixed.astype(F32) + b2[:, None]
        groups.append((x, mid, back, w1_all, w2_all, u_cols, preact, hidden))
    rows_mid = jnp.concatenate([g[1].reshape(-1, width) for g in groups], axis=0)
    row_mask = jnp.concatenate(
        [jnp.repeat(mask_small, x_small.shape[1]), jnp.repeat(mask_large, x_large.shape[1])]
    )
    split_at = x_small.shape[0] * x_small.shape[1]
    normed_two, back_two = jax.vjp(norm_rows, rows_mid, ln2_gain, ln2_bias)
    v = normed_two.astype(BF)
    activation = mm("rd,dk->rk", v, ch_w1) + ch_b1
    g = jax.nn.gelu(activation).astype(BF)
    result = (rows_mid + mm("rk,kd->rd", g, ch_w2) + ch_b2) * row_mask[:, None]
    out_small = result[:split_at].reshape(x_small.shape).astype(BF)
    out_large = result[split_at:].reshape(x_large.shape).astype(BF)
    e = (
        jnp.concatenate([cot_small.reshape(-1, width), cot_large.reshape(-1, width)]).astype(F32)
        * row_mask[:, None]
    )
    ec = e.astype(BF)
    grad_ch_w2 = mm("rk,rd->kd", g, ec)
    grad_ch_b2 = jnp.sum(ec.astype(F32), axis=0)
    ea = gelu_back(activation, mm("rd,kd->rk", ec, ch_w2)).astype(BF)
    grad_ch_w1 = mm("rd,rk->dk", v, ea)
    grad_ch_b1 = jnp.sum(ea.astype(F32), axis=0)
    rows_norm, grad_gain2, grad_bias2 = back_two(mm("rk,dk->rd", ea, ch_w1))
    ey = e + rows_norm
    grads = []
    gain1 = 0.0
    bias1 = 0.0
    for (x, mid, back, w1_all, w2_all, u_cols, preact, hidden), part in zip(
        groups, (ey[:split_at], ey[split_at:])
    ):
        part = part.reshape(x.shape)
        et = part.astype(BF)
        grad_b2 = jnp.sum(et.astype(F32), axis=(0, 2))
        et_cols = to_columns(et)
        grad_w2 = mm("jd,sd->js", hidden, et_cols)
        ep = gelu_back(preact, mm("js,sd->jd", w2_all, et_cols)).astype(BF)
        grad_b1 = jnp.sum(ep.astype(F32), axis=1)
        grad_w1 = mm("sd,jd->sj", u_cols, ep)
        eu = to_rows(mm("sj,jd->sd", w1_all, ep).astype(BF), x.shape)
        norm_grad, gain_part, bias_part = back(eu.astype(F32))
        gain1 = gain1 + gain_part
        bias1 = bias1 + bias_part
        grads.append((part + norm_grad, grad_w1, grad_b1, grad_w2, grad_b2))
    scattered = [
        (
            lax.psum_scatter(grad_w1, "blk", scatter_dimension=0, tiled=True),
            lax.psum_scatter(grad_w2, "blk", scatter_dimension=1, tiled=True),
        )
        for _, grad_w1, _, grad_w2, _ in grads
    ]
    (w1_s, w2_s), (w1_l, w2_l) = lax.psum(scattered, "img")
    b2_s, b2_l = lax.psum((grads[0][4], grads[1][4]), "img")
    both = ("img", "blk")
    grad_ch_w1 = sum_low(grad_ch_w1, both)
    grad_ch_w2 = sum_low(grad_ch_w2, both)
    gain1, bias1, b1_s, b1_l, grad_gain2, grad_bias2, grad_ch_b1, grad_ch_b2 = lax.psum(
        (gain1, bias1, grads[0][2], grads[1][2], grad_gain2, grad_bias2, grad_ch_b1, grad_ch_b2), both
    )
    return (
        out_small, out_large, grads[0][0], grads[1][0], gain1, bias1,
        w1_s, b1_s, w2_s, b2_s, w1_l, b1_l, w2_l, b2_l,
        grad_gain2, grad_bias2, grad_ch_w1, grad_ch_b1, grad_ch_w2, grad_ch_b2,
    )


def solution(mesh):
    image = P("img", "blk", None)
    whole = P()
    rows = P("blk", None)
    columns = P(None, "blk")
    vector = P("blk")
    in_specs = (
        image, image, P("img", None), whole, whole,
        rows, whole, columns, vector, rows, whole, columns, vector,
        whole, whole, whole, whole, whole, whole, image, image,
    )
    out_specs = (
        image, image, image, image, whole, whole,
        rows, whole, columns, vector, rows, whole, columns, vector,
        whole, whole, whole, whole, whole, whole,
    )
    return jax.shard_map(local, mesh=mesh, in_specs=in_specs, out_specs=out_specs, check_vma=False)
```

```python
import functools

import jax
import jax.numpy as jnp
from jax import lax
from jax.experimental import pallas as pl
from jax.experimental.pallas import tpu as pltpu
from jax.sharding import PartitionSpec as P

EPSILON = 1e-06
LANES = 128
BF = jnp.bfloat16
F32 = jnp.float32


def norm_rows(values, scales, shifts):
    row_mean = jnp.mean(values, axis=-1, keepdims=True)
    centered = values - row_mean
    row_var = jnp.mean(centered * centered, axis=-1, keepdims=True)
    return centered * lax.rsqrt(row_var + EPSILON) * scales + shifts


def gelu_back(preact, upstream):
    unused, pullback = jax.vjp(jax.nn.gelu, preact)
    return pullback(upstream)[0]


def to_columns(rows):
    count, patches, width = rows.shape
    blocks = rows.reshape(count, patches, width // LANES, LANES).transpose(0, 2, 1, 3)
    blocks = blocks.reshape(count * (width // LANES), patches, LANES)
    size = lax.axis_size("blk")
    moved = lax.all_to_all(blocks, "blk", 0, 0, tiled=True)
    share = moved.shape[0] // size
    moved = moved.reshape(size, share, patches, LANES).transpose(0, 2, 1, 3)
    return moved.reshape(size * patches, share * LANES)


def to_rows(columns, shape):
    count, patches, width = shape
    size = lax.axis_size("blk")
    share = columns.shape[1] // LANES
    blocks = columns.reshape(size, patches, share, LANES).transpose(0, 2, 1, 3)
    blocks = blocks.reshape(size * share, patches, LANES)
    moved = lax.all_to_all(blocks, "blk", 0, 0, tiled=True)
    moved = moved.reshape(count, width // LANES, patches, LANES).transpose(0, 2, 1, 3)
    return moved.reshape(shape)


def mm(spec, left, right):
    return jnp.einsum(spec, left, right, preferred_element_type=F32)


MESH = pl.DeviceIdType.MESH
ANY = pl.BlockSpec(memory_space=pl.ANY)
TILE = 256
TOP = 62 * 1024 * 1024


def img_split(size):
    near = 2 if size <= 8 else 8
    return near, size // near


def gelu_pair(a):
    square = a * a
    slope = 0.7978845608028654
    t = jnp.tanh(a * (slope + (slope * 0.044715) * square))
    half = 0.5 + 0.5 * t
    inner = slope + (3.0 * slope * 0.044715) * square
    return a * half, half + (0.5 * a) * (1.0 - t * t) * inner


class Peers:
    def __init__(self, near_count):
        self.img = lax.axis_index("img")
        self.blk = lax.axis_index("blk")
        self.core = lax.rem(self.blk, 2)
        self.x = self.blk // 2
        self.near_count = near_count
        self.near = lax.rem(self.img, near_count)
        self.far = self.img // near_count

    def at(self, axis, place):
        if axis == "core":
            return (self.img, self.x * 2 + place)
        if axis == "x":
            return (self.img, place * 2 + self.core)
        if axis == "near":
            return (self.far * self.near_count + place, self.blk)
        return (place * self.near_count + self.near, self.blk)

    def mine(self, axis):
        return {"core": self.core, "x": self.x, "near": self.near, "far": self.far}[axis]


def greet(peers, axes):
    barrier = pltpu.get_barrier_semaphore()
    total = 0
    for axis, count in axes:
        for j in range(1, count):
            there = lax.rem(peers.mine(axis) + j, count)
            pl.semaphore_signal(barrier, inc=1, device_id=peers.at(axis, there), device_id_type=MESH)
            total += 1
    pl.semaphore_wait(barrier, total)


def channel_kernel(
    near, far, far_inside,
    y_hbm, ec_hbm, w1_hbm, w2_hbm, b1_ref, gain_ref, bias_ref, b2_ref,
    out_hbm, ey_hbm, chunk_ref, small_ref,
    y, ec, v, lt, rt, w1, w2, acc_out, acc_ev, out_low,
    keep, core_tx, core_rx, keep_n, near_tx, near_rx, keep_f, far_tx, far_rx, keep_x, x_tx, x_rx,
    in_sem, w_sem, out_sem, core_ss, core_rs, near_ss, near_rs, far_ss, far_rs, x_ss, x_rs,
):
    rows, width = y.shape
    tiles = w1.shape[0]
    peers = Peers(near)
    core = peers.core
    part = 128
    parts = rows // part

    def w_copies(t):
        return (
            pltpu.make_async_copy(w1_hbm.at[:, pl.ds(t * TILE, TILE)], w1.at[t], w_sem.at[0, t]),
            pltpu.make_async_copy(w2_hbm.at[pl.ds(t * TILE, TILE)], w2.at[t], w_sem.at[1, t]),
        )

    y_in = pltpu.make_async_copy(y_hbm, y, in_sem.at[0])
    ec_in = pltpu.make_async_copy(ec_hbm, ec, in_sem.at[1])
    y_in.start()
    ec_in.start()

    def start_w(t, carry):
        for copy in w_copies(t):
            copy.start()
        return carry

    lax.fori_loop(0, tiles, start_w, 0)
    axes = [("core", 2), ("near", near)] + ([("far", far)] if far_inside else []) + [("x", 2)]
    greet(peers, axes)
    y_in.wait()
    ec_in.wait()
    small_ref[...] = jnp.zeros_like(small_ref)

    def prepare(p, carry):
        at = pl.ds(pl.multiple_of(p * part, part), part)
        row = y[at, :]
        mean = jnp.mean(row, axis=-1, keepdims=True)
        centered = row - mean
        var = jnp.mean(centered * centered, axis=-1, keepdims=True)
        normed = centered * lax.rsqrt(var + EPSILON) * gain_ref[...] + bias_ref[...]
        low = normed.astype(BF)
        v[at, :] = low
        lt[0, :, at] = low.T
        own = ec[at, :]
        lt[1, :, at] = own.T
        small_ref[4:5, :] += jnp.sum(own.astype(F32), axis=0, keepdims=True)
        acc_out[at, :] = jnp.zeros((part, width), F32)
        acc_ev[at, :] = jnp.zeros((part, width), F32)
        return carry

    lax.fori_loop(0, parts, prepare, 0)

    def send(src, dst, ss, rs, device):
        return pltpu.make_async_remote_copy(
            src_ref=src, dst_ref=dst, send_sem=ss, recv_sem=rs, device_id=device, device_id_type=MESH
        )

    def core_copy(t):
        slot = lax.rem(t, 2)
        return send(core_tx.at[slot], core_rx.at[t], core_ss.at[slot], core_rs.at[t], peers.at("core", 1 - core))

    def near_copy(t, j):
        slot = lax.rem(t, 2)
        there = lax.rem(peers.near + j, near)
        return send(
            near_tx.at[slot, j - 1], near_rx.at[t, j - 1], near_ss.at[slot, j - 1], near_rs.at[t, j - 1],
            peers.at("near", there),
        )

    def far_copy(t, j):
        slot = lax.rem(t, 2)
        there = lax.rem(peers.far + j, far)
        return send(
            far_tx.at[slot, j - 1], far_rx.at[t, j - 1], far_ss.at[slot, j - 1], far_rs.at[t, j - 1],
            peers.at("far", there),
        )

    def x_copy(t):
        slot = lax.rem(t, 2)
        return send(x_tx.at[slot], x_rx.at[t], x_ss.at[slot], x_rs.at[t], peers.at("x", 1 - peers.x))

    step_rows = rows // 3

    def tile_step(t):
        for copy in w_copies(t):
            copy.wait()
        columns = pl.ds(pl.multiple_of(t * TILE, TILE), TILE)
        bias = b1_ref[:, columns]

        def act(p, total):
            at = pl.ds(pl.multiple_of(p * step_rows, step_rows), step_rows)
            a = jnp.dot(v[at, :], w1[t], preferred_element_type=F32) + bias
            gh = lax.dot_general(ec[at, :], w2[t], (((1,), (1,)), ((), ())), preferred_element_type=F32)
            g, slope = gelu_pair(a)
            ea = (slope * gh).astype(BF)
            rt[1, at, :] = g.astype(BF)
            rt[0, at, :] = ea
            return total + jnp.sum(ea.astype(F32), axis=0, keepdims=True)

        total = lax.fori_loop(0, rows // step_rows, act, jnp.zeros((1, TILE), F32))
        small_ref[lax.div(t, 3), pl.ds(pl.multiple_of(lax.rem(t, 3) * TILE, TILE), TILE)] = total[0]

        slot = lax.rem(t, 2)

        @pl.when(t >= 2)
        def _():
            core_copy(t - 2).wait_send()

        core_tx[slot] = jnp.dot(lt[1 - core], rt[1 - core], preferred_element_type=F32).astype(BF)
        core_copy(t).start()
        keep[slot] = jnp.dot(lt[core], rt[core], preferred_element_type=F32)
        def add(p, carry):
            at = pl.ds(pl.multiple_of(p * step_rows, step_rows), step_rows)
            acc_out[at, :] += jnp.dot(rt[1, at, :], w2[t], preferred_element_type=F32)
            acc_ev[at, :] += lax.dot_general(
                rt[0, at, :], w1[t], (((1,), (1,)), ((), ())), preferred_element_type=F32
            )
            return carry

        lax.fori_loop(0, rows // step_rows, add, 0)

    share = rows // 4
    piece = share // 3

    def out_copies(p):
        at = pl.ds(pl.multiple_of(p * share, share), share)
        return (
            pltpu.make_async_copy(out_low.at[at], out_hbm.at[at], out_sem.at[0, p]),
            pltpu.make_async_copy(acc_ev.at[at], ey_hbm.at[at], out_sem.at[1, p]),
        )

    def finish(p):
        def one(q, carry):
            at = pl.ds(pl.multiple_of(p * share + q * piece, piece), piece)
            row = y[at, :]
            out_low[at, :] = (row + acc_out[at, :] + b2_ref[...]).astype(BF)
            mean = jnp.mean(row, axis=-1, keepdims=True)
            centered = row - mean
            var = jnp.mean(centered * centered, axis=-1, keepdims=True)
            scale = lax.rsqrt(var + EPSILON)
            unit = centered * scale
            ev = acc_ev[at, :]
            small_ref[5:6, :] += jnp.sum(ev * unit, axis=0, keepdims=True)
            small_ref[6:7, :] += jnp.sum(ev, axis=0, keepdims=True)
            d = ev * gain_ref[...]
            m1 = jnp.mean(d, axis=-1, keepdims=True)
            m2 = jnp.mean(d * unit, axis=-1, keepdims=True)
            acc_ev[at, :] = ec[at, :].astype(F32) + scale * (d - m1 - unit * m2)
            return carry

        lax.fori_loop(0, 3, one, 0)
        for copy in out_copies(p):
            copy.start()

    def core_sum(t):
        slot = lax.rem(t, 2)
        core_copy(t).wait_recv()

        @pl.when(t >= 2)
        def _():
            for j in range(1, near):
                near_copy(t - 2, j).wait_send()

        each = width // near
        for j in range(near):
            there = lax.rem(peers.near + j, near)
            at = pl.ds(pl.multiple_of(there * each, each), each)
            value = keep[slot, at, :] + core_rx[t, at, :].astype(F32)
            if j == 0:
                keep_n[slot] = value
            else:
                near_tx[slot, j - 1] = value.astype(BF)
                near_copy(t, j).start()

    def near_sum(t):
        slot = lax.rem(t, 2)
        for j in range(1, near):
            near_copy(t, j).wait_recv()

        if far_inside:
            @pl.when(t >= 2)
            def _():
                for j in range(1, far):
                    far_copy(t - 2, j).wait_send()

            each = width // near // far
            for j in range(1, far + 1):
                there = lax.rem(peers.far + j, far)
                at = pl.ds(pl.multiple_of(there * each, each), each)
                value = keep_n[slot, at, :]
                for k in range(near - 1):
                    value += near_rx[t, k, at, :].astype(F32)
                if j == far:
                    keep_f[slot] = value
                else:
                    far_tx[slot, j - 1] = value.astype(BF)
                    far_copy(t, j).start()
        else:
            value = keep_n[slot]
            for k in range(near - 1):
                value += near_rx[t, k].astype(F32)
            keep_f[slot] = value

    def far_sum(t):
        slot = lax.rem(t, 2)
        if far_inside:
            for j in range(1, far):
                far_copy(t, j).wait_recv()

        @pl.when(t >= 2)
        def _():
            x_copy(t - 2).wait_send()

        each = chunk_ref.shape[0]
        for there, own in ((peers.x, True), (1 - peers.x, False)):
            at = pl.ds(pl.multiple_of(there * each, each), each)
            value = keep_f[slot, at, :]
            if far_inside:
                for k in range(far - 1):
                    value += far_rx[t, k, at, :].astype(F32)
            if own:
                keep_x[slot] = value
            else:
                x_tx[slot] = value.astype(BF)
                x_copy(t).start()

    def x_sum(t):
        slot = lax.rem(t, 2)
        x_copy(t).wait_recv()
        columns = pl.ds(pl.multiple_of(t * TILE, TILE), TILE)
        chunk_ref[:, columns] = (keep_x[slot] + x_rx[t].astype(F32)).astype(BF)

    stages = (core_sum, near_sum, far_sum, x_sum)

    def step(s, carry):
        @pl.when(s < tiles)
        def _():
            tile_step(s)

        for lag, stage in enumerate(stages):
            t = s - lag
            @pl.when((t >= 0) & (t < tiles))
            def _(t=t, stage=stage):
                stage(t)

        @pl.when(s >= tiles)
        def _():
            finish(s - tiles)

        return carry

    lax.fori_loop(0, tiles + 4, step, 0)
    for t in (tiles - 2, tiles - 1):
        core_copy(t).wait_send()
        for j in range(1, near):
            near_copy(t, j).wait_send()
        if far_inside:
            for j in range(1, far):
                far_copy(t, j).wait_send()
        x_copy(t).wait_send()
    for p in range(4):
        for copy in out_copies(p):
            copy.wait()


def channel(y, ec, w1, w2, b1, gain, bias, b2):
    rows, width = y.shape
    hidden = w1.shape[1]
    tiles = hidden // TILE
    near, far = img_split(lax.axis_size("img"))
    far_inside = width % (near * far * 2 * 16) == 0
    f = far if far_inside else 1
    chunk = width // near // f // 2
    vmem = pl.BlockSpec(memory_space=pltpu.VMEM)
    V = pltpu.VMEM
    DMA = pltpu.SemaphoreType.DMA
    fm = max(f - 1, 1)
    return pl.pallas_call(
        functools.partial(channel_kernel, near, far, far_inside),
        out_shape=(
            jax.ShapeDtypeStruct((rows, width), BF),
            jax.ShapeDtypeStruct((rows, width), F32),
            jax.ShapeDtypeStruct((chunk, hidden), BF),
            jax.ShapeDtypeStruct((8, width), F32),
        ),
        in_specs=[ANY] * 4 + [vmem] * 4,
        out_specs=(ANY, ANY, vmem, vmem),
        scratch_shapes=[
            V((rows, width), F32), V((rows, width), BF), V((rows, width), BF),
            V((2, width, rows), BF), V((2, rows, TILE), BF),
            V((tiles, width, TILE), BF), V((tiles, TILE, width), BF),
            V((rows, width), F32), V((rows, width), F32), V((rows, width), BF),
            V((2, width, TILE), F32), V((2, width, TILE), BF), V((tiles, width, TILE), BF),
            V((2, width // near, TILE), F32), V((2, near - 1, width // near, TILE), BF),
            V((tiles, near - 1, width // near, TILE), BF),
            V((2, chunk * 2, TILE), F32), V((2, fm, chunk * 2, TILE), BF), V((tiles, fm, chunk * 2, TILE), BF),
            V((2, chunk, TILE), F32), V((2, chunk, TILE), BF), V((tiles, chunk, TILE), BF),
            DMA((2,)), DMA((2, tiles)), DMA((2, 4)),
            DMA((2,)), DMA((tiles,)),
            DMA((2, near - 1)), DMA((tiles, near - 1)),
            DMA((2, fm)), DMA((tiles, fm)),
            DMA((2,)), DMA((tiles,)),
        ],
        compiler_params=pltpu.CompilerParams(
            collective_id=0, has_side_effects=True, vmem_limit_bytes=TOP
        ),
    )(y, ec, w1, w2, b1.reshape(1, -1), gain.reshape(1, -1), bias.reshape(1, -1), b2.reshape(1, -1))


GROUPS = 6


def gather_kernel(near, far, far_inside, chunk_hbm, full_hbm, own_sem, x_ss, x_rs, far_ss, far_rs, near_ss, near_rs, core_ss, core_rs):
    each, hidden = chunk_hbm.shape
    peers = Peers(near)
    f = far if far_inside else 1
    f_place = peers.far if far_inside else 0
    cols = hidden // GROUPS
    axes = [("core", 2), ("near", near)] + ([("far", far)] if far_inside else []) + [("x", 2)]
    base_n = peers.near * (each * 2 * f)
    base_f = base_n + f_place * (each * 2)
    base_x = base_f + peers.x * each

    def block(start, size, k):
        return full_hbm.at[peers.core, pl.ds(pl.multiple_of(start, each), size), pl.ds(k * cols, cols)]

    def send(src, dst, ss, rs, device):
        return pltpu.make_async_remote_copy(
            src_ref=src, dst_ref=dst, send_sem=ss, recv_sem=rs, device_id=device, device_id_type=MESH
        )

    def own(k):
        return pltpu.make_async_copy(chunk_hbm.at[:, pl.ds(k * cols, cols)], block(base_x, each, k), own_sem.at[k])

    def x_copy(k):
        return send(chunk_hbm.at[:, pl.ds(k * cols, cols)], block(base_x, each, k), x_ss.at[k], x_rs.at[k], peers.at("x", 1 - peers.x))

    def far_copy(k, j):
        there = lax.rem(peers.far + j, far)
        span = block(base_f, each * 2, k)
        return send(span, span, far_ss.at[k, j - 1], far_rs.at[k, j - 1], peers.at("far", there))

    def near_copy(k, j):
        there = lax.rem(peers.near + j, near)
        span = block(base_n, each * 2 * f, k)
        return send(span, span, near_ss.at[k, j - 1], near_rs.at[k, j - 1], peers.at("near", there))

    def core_copy(k):
        span = block(0, each * 2 * f * near, k)
        return send(span, span, core_ss.at[k], core_rs.at[k], peers.at("core", 1 - peers.core))

    greet(peers, axes)
    for k in range(GROUPS):
        x_copy(k).start()
        own(k).start()
    for s in range(GROUPS + 2):
        k = s
        if 0 <= k < GROUPS:
            own(k).wait()
            x_copy(k).wait_recv()
            if far_inside:
                for j in range(1, far):
                    far_copy(k, j).start()
        k = s - 1
        if 0 <= k < GROUPS:
            if far_inside:
                for j in range(1, far):
                    far_copy(k, j).wait_recv()
            for j in range(1, near):
                near_copy(k, j).start()
        k = s - 2
        if 0 <= k < GROUPS:
            for j in range(1, near):
                near_copy(k, j).wait_recv()
            core_copy(k).start()
    for k in range(GROUPS):
        core_copy(k).wait_recv()
    for k in range(GROUPS):
        x_copy(k).wait_send()
        if far_inside:
            for j in range(1, far):
                far_copy(k, j).wait_send()
        for j in range(1, near):
            near_copy(k, j).wait_send()
        core_copy(k).wait_send()


def gather(chunk, width):
    each, hidden = chunk.shape
    near, far = img_split(lax.axis_size("img"))
    far_inside = width % (near * far * 2 * 16) == 0
    fm = far - 1
    DMA = pltpu.SemaphoreType.DMA
    return pl.pallas_call(
        functools.partial(gather_kernel, near, far, far_inside),
        out_shape=jax.ShapeDtypeStruct((2, width, hidden), BF),
        in_specs=[ANY],
        out_specs=ANY,
        scratch_shapes=[
            DMA((GROUPS,)), DMA((GROUPS,)), DMA((GROUPS,)), DMA((GROUPS, fm)), DMA((GROUPS, fm)),
            DMA((GROUPS, near - 1)), DMA((GROUPS, near - 1)), DMA((GROUPS,)), DMA((GROUPS,)),
        ],
        compiler_params=pltpu.CompilerParams(collective_id=1, has_side_effects=True),
    )(chunk)


def local(
    x_small, x_large, live_counts, ln1_gain, ln1_bias,
    tok_w1_small, tok_b1_small, tok_w2_small, tok_b2_small,
    tok_w1_large, tok_b1_large, tok_w2_large, tok_b2_large,
    ln2_gain, ln2_bias, ch_w1, ch_b1, ch_w2, ch_b2, cot_small, cot_large,
):
    width = x_small.shape[2]
    mask_small = (jnp.arange(x_small.shape[0]) < live_counts[0, 0]).astype(F32)
    mask_large = (jnp.arange(x_large.shape[0]) < live_counts[0, 1]).astype(F32)
    groups = []
    for x, w1, b1, w2, b2 in (
        (x_small, tok_w1_small, tok_b1_small, tok_w2_small, tok_b2_small),
        (x_large, tok_w1_large, tok_b1_large, tok_w2_large, tok_b2_large),
    ):
        wide = x.astype(F32)
        normed, back = jax.vjp(norm_rows, wide, ln1_gain, ln1_bias)
        w1_all = lax.all_gather(w1, "blk", axis=0, tiled=True)
        w2_all = lax.all_gather(w2, "blk", axis=1, tiled=True)
        u_cols = to_columns(normed.astype(BF))
        preact = mm("sj,sd->jd", w1_all, u_cols) + b1[:, None]
        hidden = jax.nn.gelu(preact).astype(BF)
        mixed = to_rows(mm("js,jd->sd", w2_all, hidden).astype(BF), x.shape)
        mid = wide + mixed.astype(F32) + b2[:, None]
        groups.append((x, mid, back, w1_all, w2_all, u_cols, preact, hidden))
    pad_small = -x_small.shape[1] % 64
    small_rows = x_small.shape[0] * (x_small.shape[1] + pad_small)
    large_rows = x_large.shape[0] * x_large.shape[1]
    spare = -(small_rows + large_rows) % (3 * LANES)

    def join(small, large):
        small = jnp.pad(small, ((0, 0), (0, pad_small), (0, 0))).reshape(-1, width)
        return jnp.concatenate([small, large.reshape(-1, width), jnp.zeros((spare, width), small.dtype)])

    def part(joined):
        small = joined[:small_rows].reshape(x_small.shape[0], -1, width)[:, : x_small.shape[1]]
        return small, joined[small_rows : small_rows + large_rows].reshape(x_large.shape)

    mask_small = mask_small[:, None, None]
    mask_large = mask_large[:, None, None]
    ec = join(cot_small * mask_small.astype(BF), cot_large * mask_large.astype(BF))
    out, ey, chunk, small_grads = channel(
        join(groups[0][1], groups[1][1]), ec, ch_w1, ch_w2, ch_b1, ln2_gain, ln2_bias, ch_b2
    )
    out_small, out_large = part(out)
    out_small = out_small * mask_small.astype(BF)
    out_large = out_large * mask_large.astype(BF)
    grad_ch_b1 = small_grads[:4].reshape(-1)
    grad_ch_b2, grad_gain2, grad_bias2 = small_grads[4], small_grads[5], small_grads[6]
    near, far = img_split(lax.axis_size("img"))
    if width % (near * far * 2 * 16):
        same = [[a * near + b for a in range(far)] for b in range(near)]
        chunk = lax.psum(chunk.astype(F32), "img", axis_index_groups=same).astype(BF)
    full = gather(chunk, width)
    grad_ch_w1 = full[0].astype(F32)
    grad_ch_w2 = full[1].T.astype(F32)
    grads = []
    gain1 = 0.0
    bias1 = 0.0
    for (x, mid, back, w1_all, w2_all, u_cols, preact, hidden), part_ey in zip(
        groups, part(ey)
    ):
        et = part_ey.astype(BF)
        grad_b2 = jnp.sum(et.astype(F32), axis=(0, 2))
        et_cols = to_columns(et)
        grad_w2 = mm("jd,sd->js", hidden, et_cols)
        ep = gelu_back(preact, mm("js,sd->jd", w2_all, et_cols)).astype(BF)
        grad_b1 = jnp.sum(ep.astype(F32), axis=1)
        grad_w1 = mm("sd,jd->sj", u_cols, ep)
        eu = to_rows(mm("sj,jd->sd", w1_all, ep).astype(BF), x.shape)
        norm_grad, gain_part, bias_part = back(eu.astype(F32))
        gain1 = gain1 + gain_part
        bias1 = bias1 + bias_part
        grads.append((part_ey + norm_grad, grad_w1, grad_b1, grad_w2, grad_b2))
    scattered = [
        (
            lax.psum_scatter(grad_w1, "blk", scatter_dimension=0, tiled=True),
            lax.psum_scatter(grad_w2, "blk", scatter_dimension=1, tiled=True),
        )
        for _, grad_w1, _, grad_w2, _ in grads
    ]
    (w1_s, w2_s), (w1_l, w2_l) = lax.psum(scattered, "img")
    b2_s, b2_l = lax.psum((grads[0][4], grads[1][4]), "img")
    both = ("img", "blk")
    gain1, bias1, b1_s, b1_l, grad_gain2, grad_bias2, grad_ch_b1, grad_ch_b2 = lax.psum(
        (gain1, bias1, grads[0][2], grads[1][2], grad_gain2, grad_bias2, grad_ch_b1, grad_ch_b2), both
    )
    return (
        out_small, out_large, grads[0][0], grads[1][0], gain1, bias1,
        w1_s, b1_s, w2_s, b2_s, w1_l, b1_l, w2_l, b2_l,
        grad_gain2, grad_bias2, grad_ch_w1, grad_ch_b1, grad_ch_w2, grad_ch_b2,
    )


def solution(mesh):
    image = P("img", "blk", None)
    whole = P()
    rows = P("blk", None)
    columns = P(None, "blk")
    vector = P("blk")
    in_specs = (
        image, image, P("img", None), whole, whole,
        rows, whole, columns, vector, rows, whole, columns, vector,
        whole, whole, whole, whole, whole, whole, image, image,
    )
    out_specs = (
        image, image, image, image, whole, whole,
        rows, whole, columns, vector, rows, whole, columns, vector,
        whole, whole, whole, whole, whole, whole,
    )
    return jax.shard_map(local, mesh=mesh, in_specs=in_specs, out_specs=out_specs, check_vma=False)
```

```python
import functools

import jax
import jax.numpy as jnp
from jax import lax
from jax.experimental import pallas as pl
from jax.experimental.pallas import tpu as pltpu
from jax.sharding import PartitionSpec as P

EPSILON = 1e-06
LANES = 128
BF = jnp.bfloat16
F32 = jnp.float32


MESH = pl.DeviceIdType.MESH
ANY = pl.BlockSpec(memory_space=pl.ANY)
TILE = 256
TOP = 62 * 1024 * 1024


def img_split(size):
    near = 2 if size <= 8 else 8
    return near, size // near


def gelu_pair(a):
    square = a * a
    slope = 0.7978845608028654
    t = jnp.tanh(a * (slope + (slope * 0.044715) * square))
    half = 0.5 + 0.5 * t
    inner = slope + (3.0 * slope * 0.044715) * square
    return a * half, half + (0.5 * a) * (1.0 - t * t) * inner


class Peers:
    def __init__(self, near_count):
        self.img = lax.axis_index("img")
        self.blk = lax.axis_index("blk")
        self.core = lax.rem(self.blk, 2)
        self.x = self.blk // 2
        self.near_count = near_count
        self.near = lax.rem(self.img, near_count)
        self.far = self.img // near_count

    def at(self, axis, place):
        if axis == "core":
            return (self.img, self.x * 2 + place)
        if axis == "x":
            return (self.img, place * 2 + self.core)
        if axis == "near":
            return (self.far * self.near_count + place, self.blk)
        return (place * self.near_count + self.near, self.blk)

    def mine(self, axis):
        return {"core": self.core, "x": self.x, "near": self.near, "far": self.far}[axis]


def greet(peers, axes):
    barrier = pltpu.get_barrier_semaphore()
    total = 0
    for axis, count in axes:
        for j in range(1, count):
            there = lax.rem(peers.mine(axis) + j, count)
            pl.semaphore_signal(barrier, inc=1, device_id=peers.at(axis, there), device_id_type=MESH)
            total += 1
    pl.semaphore_wait(barrier, total)


def channel_kernel(
    near, far, far_inside,
    y_hbm, ec_hbm, w1_hbm, w2_hbm, b1_ref, gain_ref, bias_ref, b2_ref,
    out_hbm, ey_hbm, chunk_ref, small_ref,
    y, ec, v, lt, rt, w1, w2, acc_out, acc_ev, out_low,
    keep, core_tx, core_rx, keep_n, near_tx, near_rx, keep_f, far_tx, far_rx, keep_x, x_tx, x_rx,
    in_sem, w_sem, out_sem, core_ss, core_rs, near_ss, near_rs, far_ss, far_rs, x_ss, x_rs,
):
    rows, width = y.shape
    tiles = w1.shape[0]
    peers = Peers(near)
    core = peers.core
    part = 128
    parts = rows // part

    def w_copies(t):
        return (
            pltpu.make_async_copy(w1_hbm.at[:, pl.ds(t * TILE, TILE)], w1.at[t], w_sem.at[0, t]),
            pltpu.make_async_copy(w2_hbm.at[pl.ds(t * TILE, TILE)], w2.at[t], w_sem.at[1, t]),
        )

    y_in = pltpu.make_async_copy(y_hbm, y, in_sem.at[0])
    ec_in = pltpu.make_async_copy(ec_hbm, ec, in_sem.at[1])
    y_in.start()
    ec_in.start()

    def start_w(t, carry):
        for copy in w_copies(t):
            copy.start()
        return carry

    lax.fori_loop(0, tiles, start_w, 0)
    axes = [("core", 2), ("near", near)] + ([("far", far)] if far_inside else []) + [("x", 2)]
    greet(peers, axes)
    y_in.wait()
    ec_in.wait()
    small_ref[...] = jnp.zeros_like(small_ref)

    def prepare(p, carry):
        at = pl.ds(pl.multiple_of(p * part, part), part)
        row = y[at, :]
        mean = jnp.mean(row, axis=-1, keepdims=True)
        centered = row - mean
        var = jnp.mean(centered * centered, axis=-1, keepdims=True)
        normed = centered * lax.rsqrt(var + EPSILON) * gain_ref[...] + bias_ref[...]
        low = normed.astype(BF)
        v[at, :] = low
        lt[0, :, at] = low.T
        own = ec[at, :]
        lt[1, :, at] = own.T
        small_ref[4:5, :] += jnp.sum(own.astype(F32), axis=0, keepdims=True)
        acc_out[at, :] = jnp.zeros((part, width), F32)
        acc_ev[at, :] = jnp.zeros((part, width), F32)
        return carry

    lax.fori_loop(0, parts, prepare, 0)

    def send(src, dst, ss, rs, device):
        return pltpu.make_async_remote_copy(
            src_ref=src, dst_ref=dst, send_sem=ss, recv_sem=rs, device_id=device, device_id_type=MESH
        )

    def core_copy(t):
        slot = lax.rem(t, 2)
        return send(core_tx.at[slot], core_rx.at[t], core_ss.at[slot], core_rs.at[t], peers.at("core", 1 - core))

    def near_copy(t, j):
        slot = lax.rem(t, 2)
        there = lax.rem(peers.near + j, near)
        return send(
            near_tx.at[slot, j - 1], near_rx.at[t, j - 1], near_ss.at[slot, j - 1], near_rs.at[t, j - 1],
            peers.at("near", there),
        )

    def far_copy(t, j):
        slot = lax.rem(t, 2)
        there = lax.rem(peers.far + j, far)
        return send(
            far_tx.at[slot, j - 1], far_rx.at[t, j - 1], far_ss.at[slot, j - 1], far_rs.at[t, j - 1],
            peers.at("far", there),
        )

    def x_copy(t):
        slot = lax.rem(t, 2)
        return send(x_tx.at[slot], x_rx.at[t], x_ss.at[slot], x_rs.at[t], peers.at("x", 1 - peers.x))

    step_rows = rows

    def tile_step(t):
        for copy in w_copies(t):
            copy.wait()
        columns = pl.ds(pl.multiple_of(t * TILE, TILE), TILE)
        bias = b1_ref[:, columns]

        def act(p, total):
            at = pl.ds(pl.multiple_of(p * step_rows, step_rows), step_rows)
            a = jnp.dot(v[at, :], w1[t], preferred_element_type=F32) + bias
            gh = lax.dot_general(ec[at, :], w2[t], (((1,), (1,)), ((), ())), preferred_element_type=F32)
            g, slope = gelu_pair(a)
            ea = (slope * gh).astype(BF)
            rt[1, at, :] = g.astype(BF)
            rt[0, at, :] = ea
            return total + jnp.sum(ea.astype(F32), axis=0, keepdims=True)

        total = lax.fori_loop(0, rows // step_rows, act, jnp.zeros((1, TILE), F32))
        small_ref[lax.div(t, 3), pl.ds(pl.multiple_of(lax.rem(t, 3) * TILE, TILE), TILE)] = total[0]

        slot = lax.rem(t, 2)

        @pl.when(t >= 2)
        def _():
            core_copy(t - 2).wait_send()

        core_tx[slot] = jnp.dot(lt[1 - core], rt[1 - core], preferred_element_type=F32).astype(BF)
        core_copy(t).start()
        keep[slot] = jnp.dot(lt[core], rt[core], preferred_element_type=F32)
        def add(p, carry):
            at = pl.ds(pl.multiple_of(p * step_rows, step_rows), step_rows)
            acc_out[at, :] += jnp.dot(rt[1, at, :], w2[t], preferred_element_type=F32)
            acc_ev[at, :] += lax.dot_general(
                rt[0, at, :], w1[t], (((1,), (1,)), ((), ())), preferred_element_type=F32
            )
            return carry

        lax.fori_loop(0, rows // step_rows, add, 0)

    share = rows // 4
    piece = share // 3

    def out_copies(p):
        at = pl.ds(pl.multiple_of(p * share, share), share)
        return (
            pltpu.make_async_copy(out_low.at[at], out_hbm.at[at], out_sem.at[0, p]),
            pltpu.make_async_copy(acc_ev.at[at], ey_hbm.at[at], out_sem.at[1, p]),
        )

    def finish(p):
        def one(q, carry):
            at = pl.ds(pl.multiple_of(p * share + q * piece, piece), piece)
            row = y[at, :]
            out_low[at, :] = (row + acc_out[at, :] + b2_ref[...]).astype(BF)
            mean = jnp.mean(row, axis=-1, keepdims=True)
            centered = row - mean
            var = jnp.mean(centered * centered, axis=-1, keepdims=True)
            scale = lax.rsqrt(var + EPSILON)
            unit = centered * scale
            ev = acc_ev[at, :]
            small_ref[5:6, :] += jnp.sum(ev * unit, axis=0, keepdims=True)
            small_ref[6:7, :] += jnp.sum(ev, axis=0, keepdims=True)
            d = ev * gain_ref[...]
            m1 = jnp.mean(d, axis=-1, keepdims=True)
            m2 = jnp.mean(d * unit, axis=-1, keepdims=True)
            acc_ev[at, :] = ec[at, :].astype(F32) + scale * (d - m1 - unit * m2)
            return carry

        lax.fori_loop(0, 3, one, 0)
        for copy in out_copies(p):
            copy.start()

    def core_sum(t):
        slot = lax.rem(t, 2)
        core_copy(t).wait_recv()

        @pl.when(t >= 2)
        def _():
            for j in range(1, near):
                near_copy(t - 2, j).wait_send()

        each = width // near
        for j in range(near):
            there = lax.rem(peers.near + j, near)
            at = pl.ds(pl.multiple_of(there * each, each), each)
            value = keep[slot, at, :] + core_rx[t, at, :].astype(F32)
            if j == 0:
                keep_n[slot] = value
            else:
                near_tx[slot, j - 1] = value.astype(BF)
                near_copy(t, j).start()

    def near_sum(t):
        slot = lax.rem(t, 2)
        for j in range(1, near):
            near_copy(t, j).wait_recv()

        if far_inside:
            @pl.when(t >= 2)
            def _():
                for j in range(1, far):
                    far_copy(t - 2, j).wait_send()

            each = width // near // far
            for j in range(1, far + 1):
                there = lax.rem(peers.far + j, far)
                at = pl.ds(pl.multiple_of(there * each, each), each)
                value = keep_n[slot, at, :]
                for k in range(near - 1):
                    value += near_rx[t, k, at, :].astype(F32)
                if j == far:
                    keep_f[slot] = value
                else:
                    far_tx[slot, j - 1] = value.astype(BF)
                    far_copy(t, j).start()
        else:
            value = keep_n[slot]
            for k in range(near - 1):
                value += near_rx[t, k].astype(F32)
            keep_f[slot] = value

    def far_sum(t):
        slot = lax.rem(t, 2)
        if far_inside:
            for j in range(1, far):
                far_copy(t, j).wait_recv()

        @pl.when(t >= 2)
        def _():
            x_copy(t - 2).wait_send()

        each = chunk_ref.shape[0]
        for there, own in ((peers.x, True), (1 - peers.x, False)):
            at = pl.ds(pl.multiple_of(there * each, each), each)
            value = keep_f[slot, at, :]
            if far_inside:
                for k in range(far - 1):
                    value += far_rx[t, k, at, :].astype(F32)
            if own:
                keep_x[slot] = value
            else:
                x_tx[slot] = value.astype(BF)
                x_copy(t).start()

    def x_sum(t):
        slot = lax.rem(t, 2)
        x_copy(t).wait_recv()
        columns = pl.ds(pl.multiple_of(t * TILE, TILE), TILE)
        chunk_ref[:, columns] = (keep_x[slot] + x_rx[t].astype(F32)).astype(BF)

    stages = (core_sum, near_sum, far_sum, x_sum)

    def step(s, carry):
        @pl.when(s < tiles)
        def _():
            tile_step(s)

        for lag, stage in enumerate(stages):
            t = s - lag
            @pl.when((t >= 0) & (t < tiles))
            def _(t=t, stage=stage):
                stage(t)

        @pl.when(s >= tiles)
        def _():
            finish(s - tiles)

        return carry

    lax.fori_loop(0, tiles + 4, step, 0)
    for t in (tiles - 2, tiles - 1):
        core_copy(t).wait_send()
        for j in range(1, near):
            near_copy(t, j).wait_send()
        if far_inside:
            for j in range(1, far):
                far_copy(t, j).wait_send()
        x_copy(t).wait_send()
    for p in range(4):
        for copy in out_copies(p):
            copy.wait()


def channel(y, ec, w1, w2, b1, gain, bias, b2):
    rows, width = y.shape
    hidden = w1.shape[1]
    tiles = hidden // TILE
    near, far = img_split(lax.axis_size("img"))
    far_inside = width % (near * far * 2 * 16) == 0
    f = far if far_inside else 1
    chunk = width // near // f // 2
    vmem = pl.BlockSpec(memory_space=pltpu.VMEM)
    V = pltpu.VMEM
    DMA = pltpu.SemaphoreType.DMA
    fm = max(f - 1, 1)
    return pl.pallas_call(
        functools.partial(channel_kernel, near, far, far_inside),
        out_shape=(
            jax.ShapeDtypeStruct((rows, width), BF),
            jax.ShapeDtypeStruct((rows, width), F32),
            jax.ShapeDtypeStruct((chunk, hidden), BF),
            jax.ShapeDtypeStruct((8, width), F32),
        ),
        in_specs=[ANY] * 4 + [vmem] * 4,
        out_specs=(ANY, ANY, vmem, vmem),
        scratch_shapes=[
            V((rows, width), F32), V((rows, width), BF), V((rows, width), BF),
            V((2, width, rows), BF), V((2, rows, TILE), BF),
            V((tiles, width, TILE), BF), V((tiles, TILE, width), BF),
            V((rows, width), F32), V((rows, width), F32), V((rows, width), BF),
            V((2, width, TILE), F32), V((2, width, TILE), BF), V((tiles, width, TILE), BF),
            V((2, width // near, TILE), F32), V((2, near - 1, width // near, TILE), BF),
            V((tiles, near - 1, width // near, TILE), BF),
            V((2, chunk * 2, TILE), F32), V((2, fm, chunk * 2, TILE), BF), V((tiles, fm, chunk * 2, TILE), BF),
            V((2, chunk, TILE), F32), V((2, chunk, TILE), BF), V((tiles, chunk, TILE), BF),
            DMA((2,)), DMA((2, tiles)), DMA((2, 4)),
            DMA((2,)), DMA((tiles,)),
            DMA((2, near - 1)), DMA((tiles, near - 1)),
            DMA((2, fm)), DMA((tiles, fm)),
            DMA((2,)), DMA((tiles,)),
        ],
        compiler_params=pltpu.CompilerParams(
            collective_id=0, has_side_effects=True, vmem_limit_bytes=TOP
        ),
    )(y, ec, w1, w2, b1.reshape(1, -1), gain.reshape(1, -1), bias.reshape(1, -1), b2.reshape(1, -1))


NT = (((1,), (1,)), ((), ()))


def matmul(left, right):
    return jnp.dot(left, right, preferred_element_type=F32)


def matmul_nt(left, right):
    return lax.dot_general(left, right, NT, preferred_element_type=F32)


class Swap:
    def __init__(self, peers, size, per_l, per_s, patches_l, patches_s):
        self.peers, self.size = peers, size
        self.per_l, self.per_s = per_l, per_s
        self.pl, self.ps = patches_l, patches_s

    def other(self, step):
        return lax.rem(self.peers.blk + step, self.size)

    def copy(self, src, dst, ss, rs, place):
        return pltpu.make_async_remote_copy(
            src_ref=src, dst_ref=dst, send_sem=ss, recv_sem=rs,
            device_id=(self.peers.img, place), device_id_type=MESH,
        )

    def rows(self, place, patches):
        return pl.ds(pl.multiple_of(place * patches, patches), patches)

    def out(self, kind, j, place, source, tx, cols, ss, rs):
        per, patches = (self.per_l, self.pl) if kind == "l" else (self.per_s, self.ps)
        unit = place * per + j
        return self.copy(
            tx.at[unit], cols.at[j, self.rows(source, patches)], ss.at[unit], rs.at[j, source], place
        )

    def back(self, kind, j, owner, place, cols, rx, ss, rs):
        per, patches = (self.per_l, self.pl) if kind == "l" else (self.per_s, self.ps)
        unit = owner * per + j
        return self.copy(
            cols.at[j, self.rows(place, patches)], rx.at[unit], ss.at[j, place], rs.at[unit], place
        )


def greet_all(peers, size, near, far):
    barrier = pltpu.get_barrier_semaphore()
    total = 0
    for j in range(1, size):
        there = lax.rem(peers.blk + j, size)
        pl.semaphore_signal(barrier, inc=1, device_id=(peers.img, there), device_id_type=MESH)
        total += 1
    for axis, count in (("near", near), ("far", far)):
        for j in range(1, count):
            there = lax.rem(peers.mine(axis) + j, count)
            pl.semaphore_signal(barrier, inc=1, device_id=peers.at(axis, there), device_id_type=MESH)
            total += 1
    pl.semaphore_wait(barrier, total)


def unit_rows(row):
    mean = jnp.mean(row, axis=-1, keepdims=True)
    centered = row - mean
    var = jnp.mean(centered * centered, axis=-1, keepdims=True)
    scale = lax.rsqrt(var + EPSILON)
    return centered * scale, scale


def token_kernel(
    near, size,
    xl, xs, wq_l, wq_s, b1_l, b1_s, b2_l, b2_s, gain_ref, bias_ref,
    y_hbm, u_l, u_s, h_l, h_s, sl_l, sl_s, w_l, w_s,
    tx_l, tx_s, w1t_l, w1t_s, m_l, m_s, rx_l, rx_s, y,
    y_sem, own_sem, wown, w_ss, w_rs, out_ss_l, out_ss_s, out_rs_l, out_rs_s, bk_ss_l, bk_ss_s, bk_rs_l, bk_rs_s,
):
    peers = Peers(near)
    me = peers.blk
    count_l, patches_l, width = xl.shape
    count_s, patches_s, _ = xs.shape
    half = width // 2
    per_l, per_s = count_l * 2 // size, count_s // size
    swap = Swap(peers, size, per_l, per_s, patches_l, patches_s)

    barrier = pltpu.get_barrier_semaphore()
    for j in range(1, size):
        pl.semaphore_signal(barrier, inc=1, device_id=(peers.img, swap.other(j)), device_id_type=MESH)
    pl.semaphore_wait(barrier, size - 1)

    def weights(src_l, src_s, quarter, n, place):
        return (
            swap.copy(src_l, w_l.at[:, swap.rows(quarter, patches_l)], w_ss.at[n, 0], w_rs.at[n, 0], place),
            swap.copy(src_s, w_s.at[:, swap.rows(quarter, patches_s)], w_ss.at[n, 1], w_rs.at[n, 1], place),
        )

    x_peer = (1 - peers.x) * 2 + peers.core
    core_peer = peers.x * 2 + 1 - peers.core
    to_x = weights(wq_l, wq_s, me, 0, x_peer)
    to_core = weights(wq_l, wq_s, me, 1, core_peer)
    relay = weights(
        w_l.at[:, swap.rows(x_peer, patches_l)], w_s.at[:, swap.rows(x_peer, patches_s)], x_peer, 2, core_peer
    )
    for copy in to_x + to_core:
        copy.start()
    own_w = (
        pltpu.make_async_copy(wq_l, w_l.at[:, swap.rows(me, patches_l)], wown.at[0]),
        pltpu.make_async_copy(wq_s, w_s.at[:, swap.rows(me, patches_s)], wown.at[1]),
    )
    for copy in own_w:
        copy.start()

    def norm(row):
        unit, _ = unit_rows(row.astype(F32))
        return (unit * gain_ref[...] + bias_ref[...]).astype(BF)

    def norm_l(n, carry):
        u = norm(xl[n])
        tx_l[2 * n] = u[:, :half]
        tx_l[2 * n + 1] = u[:, half:]
        return carry

    def norm_s(n, carry):
        tx_s[n] = norm(xs[n])
        return carry

    lax.fori_loop(0, count_l, norm_l, 0)
    for j in range(per_l):
        for k in range(1, size):
            swap.out("l", j, swap.other(k), me, tx_l, u_l, out_ss_l, out_rs_l).start()
    lax.fori_loop(0, count_s, norm_s, 0)
    for j in range(per_s):
        for k in range(1, size):
            swap.out("s", j, swap.other(k), me, tx_s, u_s, out_ss_s, out_rs_s).start()
    for j in range(per_l):
        u_l[j, swap.rows(me, patches_l)] = tx_l[me * per_l + j]
    for j in range(per_s):
        u_s[j, swap.rows(me, patches_s)] = tx_s[me * per_s + j]

    for copy in to_x:
        copy.wait_recv()
    for copy in relay:
        copy.start()
    for copy in own_w:
        copy.wait()
    for copy in to_core + relay:
        copy.wait_recv()
    w1t_l[...] = w_l[0].T
    w1t_s[...] = w_s[0].T

    def mix(kind, j, cols, w1t, w2t, b1, h, slope, m, outs, tx, rx, bss, brs):
        for k in range(1, size):
            source = swap.other(k)
            swap.out(kind, j, me, source, tx, cols, *outs).wait_recv()
        g, d = gelu_pair(matmul(w1t[...], cols[j]) + b1[...])
        low = g.astype(BF)
        h[j] = low
        slope[j] = d.astype(BF)
        m[j] = matmul(w2t, low).astype(BF)
        for k in range(1, size):
            swap.back(kind, j, me, swap.other(k), m, rx, bss, brs).start()
        patches, per = (patches_l, per_l) if kind == "l" else (patches_s, per_s)
        rx[me * per + j] = m[j, swap.rows(me, patches)]

    for j in range(per_l):
        mix("l", j, u_l, w1t_l, w_l[1], b1_l, h_l, sl_l, m_l, (out_ss_l, out_rs_l), tx_l, rx_l, bk_ss_l, bk_rs_l)
    for j in range(per_s):
        mix("s", j, u_s, w1t_s, w_s[1], b1_s, h_s, sl_s, m_s, (out_ss_s, out_rs_s), tx_s, rx_s, bk_ss_s, bk_rs_s)

    small_rows = count_s * patches_s
    rows = y.shape[0]
    used = small_rows + count_l * patches_l
    if rows > used:
        y[used:rows, :] = jnp.zeros((rows - used, width), F32)

    def arrived(kind, unit, m, rx, bss, brs):
        per = per_l if kind == "l" else per_s
        owner = unit // per

        @pl.when(owner != me)
        def _():
            swap.back(kind, unit - owner * per, owner, me, m, rx, bss, brs).wait_recv()

    def home_l(n, carry):
        arrived("l", 2 * n, m_l, rx_l, bk_ss_l, bk_rs_l)
        arrived("l", 2 * n + 1, m_l, rx_l, bk_ss_l, bk_rs_l)
        at = pl.ds(pl.multiple_of(small_rows + n * patches_l, 16), patches_l)
        y[at, :half] = xl[n, :, :half].astype(F32) + rx_l[2 * n].astype(F32) + b2_l[...]
        y[at, half:] = xl[n, :, half:].astype(F32) + rx_l[2 * n + 1].astype(F32) + b2_l[...]
        return carry

    def home_s(n, carry):
        arrived("s", n, m_s, rx_s, bk_ss_s, bk_rs_s)
        at = pl.ds(pl.multiple_of(n * patches_s, 16), patches_s)
        y[at, :] = xs[n].astype(F32) + rx_s[n].astype(F32) + b2_s[...]
        return carry

    lax.fori_loop(0, count_l, home_l, 0)
    lax.fori_loop(0, count_s, home_s, 0)
    y_out = pltpu.make_async_copy(y, y_hbm, y_sem.at[0])
    y_out.start()
    for copy in to_x + to_core + relay:
        copy.wait_send()
    for k in range(1, size):
        there = swap.other(k)
        for j in range(per_l):
            swap.out("l", j, there, me, tx_l, u_l, out_ss_l, out_rs_l).wait_send()
            swap.back("l", j, me, there, m_l, rx_l, bk_ss_l, bk_rs_l).wait_send()
        for j in range(per_s):
            swap.out("s", j, there, me, tx_s, u_s, out_ss_s, out_rs_s).wait_send()
            swap.back("s", j, me, there, m_s, rx_s, bk_ss_s, bk_rs_s).wait_send()
    y_out.wait()


def token_forward(xl, xs, wq_l, wq_s, b1_l, b1_s, b2_l, b2_s, gain, bias, rows):
    size = lax.axis_size("blk")
    near, far = img_split(lax.axis_size("img"))
    count_l, patches_l, width = xl.shape
    count_s, patches_s, _ = xs.shape
    token = wq_l.shape[2]
    half = width // 2
    per_l, per_s = count_l * 2 // size, count_s // size
    vmem = pl.BlockSpec(memory_space=pltpu.VMEM)
    V = pltpu.VMEM
    DMA = pltpu.SemaphoreType.DMA
    low = lambda *shape: jax.ShapeDtypeStruct(shape, BF)
    return pl.pallas_call(
        functools.partial(token_kernel, near, size),
        out_shape=(
            jax.ShapeDtypeStruct((rows, width), F32),
            low(per_l, size * patches_l, half), low(per_s, size * patches_s, width),
            low(per_l, token, half), low(per_s, token, width),
            low(per_l, token, half), low(per_s, token, width),
            low(2, size * patches_l, token), low(2, size * patches_s, token),
        ),
        in_specs=[vmem] * 10,
        out_specs=(ANY,) + (vmem,) * 8,
        scratch_shapes=[
            V((count_l * 2, patches_l, half), BF), V((count_s, patches_s, width), BF),
            V((token, size * patches_l), BF), V((token, size * patches_s), BF),
            V((per_l, size * patches_l, half), BF), V((per_s, size * patches_s, width), BF),
            V((count_l * 2, patches_l, half), BF), V((count_s, patches_s, width), BF),
            V((rows, width), F32),
            DMA((1,)), DMA((1,)), DMA((2,)), DMA((3, 2)), DMA((3, 2)),
            DMA((count_l * 2,)), DMA((count_s,)), DMA((per_l, size)), DMA((per_s, size)),
            DMA((per_l, size)), DMA((per_s, size)), DMA((count_l * 2,)), DMA((count_s,)),
        ],
        compiler_params=pltpu.CompilerParams(
            collective_id=2, has_side_effects=True, vmem_limit_bytes=TOP
        ),
    )(
        xl, xs, wq_l, wq_s, b1_l.reshape(-1, 1), b1_s.reshape(-1, 1), b2_l.reshape(-1, 1), b2_s.reshape(-1, 1),
        gain.reshape(1, -1), bias.reshape(1, -1),
    )


GROUPS = 6
SLAB = 512


def backward_kernel(
    near, far, size, far_inside,
    chunk_hbm, ey_hbm, xl, xs, u_l, u_s, h_l, h_s, sl_l, sl_s, w_l, w_s, small_in, gain_ref,
    full_hbm, gx_hbm, tok_out, vec_out,
    ey, tx_l, tx_s, e_l, e_s, w2_l, w2_s, ep_l, ep_s, eu_l, eu_s, rx_l, rx_s,
    grads, tok_tx, tok_rx, tokx_tx, tokx_rx, tok_sum, tokn_tx, tokn_rx, tok_half, tokf_tx, tokf_rx,
    vec, vec_rx, vecn_rx, vecf_rx,
    ey_sem, gx_sem,
    own_sem, gx_ss, gx_rs, gf_ss, gf_rs, gn_ss, gn_rs, gc_ss, gc_rs,
    out_ss_l, out_ss_s, out_rs_l, out_rs_s, bk_ss_l, bk_ss_s, bk_rs_l, bk_rs_s,
    tc_ss, tc_rs, tx_ss, tx_rs, tn_ss, tn_rs, tf_ss, tf_rs, taf_ss, taf_rs, tan_ss, tan_rs,
    v_ss, v_rs, vn_ss, vn_rs, vf_ss, vf_rs,
):
    peers = Peers(near)
    me = peers.blk
    count_l, patches_l, width = xl.shape
    count_s, patches_s, _ = xs.shape
    token = w_l.shape[2]
    half = width // 2
    per_l, per_s = count_l * 2 // size, count_s // size
    swap = Swap(peers, size, per_l, per_s, patches_l, patches_s)
    small_rows = count_s * patches_s
    x_peer = peers.at("x", 1 - peers.x)
    core_peer = peers.at("core", 1 - peers.core)

    def send(src, dst, ss, rs, device):
        return pltpu.make_async_remote_copy(
            src_ref=src, dst_ref=dst, send_sem=ss, recv_sem=rs, device_id=device, device_id_type=MESH
        )

    def others(axis, count):
        return [(j, peers.at(axis, lax.rem(peers.mine(axis) + j, count))) for j in range(1, count)]

    near_peers = others("near", near)
    far_peers = others("far", far)

    each, hidden = chunk_hbm.shape
    f = far if far_inside else 1
    f_place = peers.far if far_inside else 0
    cols = hidden // GROUPS
    base_n = peers.near * (each * 2 * f)
    base_f = base_n + f_place * (each * 2)
    base_x = base_f + peers.x * each

    def block(start, rows, k):
        return full_hbm.at[peers.core, pl.ds(pl.multiple_of(start, each), rows), pl.ds(k * cols, cols)]

    def g_own(k):
        return pltpu.make_async_copy(chunk_hbm.at[:, pl.ds(k * cols, cols)], block(base_x, each, k), own_sem.at[k])

    def g_x(k):
        return send(chunk_hbm.at[:, pl.ds(k * cols, cols)], block(base_x, each, k), gx_ss.at[k], gx_rs.at[k], x_peer)

    def g_far(k):
        span = block(base_f, each * 2, k)
        return [
            send(span, span, gf_ss.at[k, j - 1], gf_rs.at[k, j - 1], there) for j, there in far_peers
        ] if far_inside else []

    def g_near(k):
        span = block(base_n, each * 2 * f, k)
        return [send(span, span, gn_ss.at[k, j - 1], gn_rs.at[k, j - 1], there) for j, there in near_peers]

    def g_core(k):
        span = block(0, each * 2 * f * near, k)
        return send(span, span, gc_ss.at[k], gc_rs.at[k], core_peer)

    def tick_near(k):
        for copy in g_far(k):
            copy.wait_recv()
        for copy in g_near(k):
            copy.start()

    def tick_core(k):
        for copy in g_near(k):
            copy.wait_recv()
        g_core(k).start()

    ey_in = pltpu.make_async_copy(ey_hbm, ey, ey_sem.at[0])
    ey_in.start()
    greet_all(peers, size, near, far)
    for k in range(GROUPS):
        g_x(k).start()
        g_own(k).start()
    ey_in.wait()
    vec[...] = jnp.zeros_like(vec)
    vec[0:8, :] = small_in[...]
    ones = jnp.ones((8, width), BF)

    def cast_l(n, total):
        at = pl.ds(pl.multiple_of(small_rows + n * patches_l, 16), patches_l)
        et = ey[at, :].astype(BF)
        tx_l[2 * n] = et[:, :half]
        tx_l[2 * n + 1] = et[:, half:]
        return total + matmul_nt(ones, et)

    def cast_s(n, total):
        at = pl.ds(pl.multiple_of(n * patches_s, 16), patches_s)
        et = ey[at, :].astype(BF)
        tx_s[n] = et
        return total + matmul_nt(ones, et)

    total_l = lax.fori_loop(0, count_l, cast_l, jnp.zeros((8, patches_l), F32))
    for j in range(per_l):
        for k in range(1, size):
            swap.out("l", j, swap.other(k), me, tx_l, e_l, out_ss_l, out_rs_l).start()
    total_s = lax.fori_loop(0, count_s, cast_s, jnp.zeros((8, patches_s), F32))
    for j in range(per_s):
        for k in range(1, size):
            swap.out("s", j, swap.other(k), me, tx_s, e_s, out_ss_s, out_rs_s).start()
    vec[16:24, 0:patches_l] = total_l
    vec[16:24, half:half + patches_s] = total_s
    for j in range(per_l):
        e_l[j, swap.rows(me, patches_l)] = tx_l[me * per_l + j]
    for j in range(per_s):
        e_s[j, swap.rows(me, patches_s)] = tx_s[me * per_s + j]
    w2_l[...] = w_l[1].T
    w2_s[...] = w_s[1].T
    for k in range(GROUPS):
        g_own(k).wait()
        g_x(k).wait_recv()
        for copy in g_far(k):
            copy.start()
        if not far_inside:
            tick_near(k)

    def unmix(kind, j, e, w2, w1, slope, ep, eu, outs, tx, rx, bss, brs):
        for k in range(1, size):
            swap.out(kind, j, me, swap.other(k), tx, e, *outs).wait_recv()
        low = (matmul(w2[...], e[j]) * slope[j].astype(F32)).astype(BF)
        ep[j] = low
        eu[j] = matmul(w1, low).astype(BF)
        for k in range(1, size):
            swap.back(kind, j, me, swap.other(k), eu, rx, bss, brs).start()
        patches, per = (patches_l, per_l) if kind == "l" else (patches_s, per_s)
        rx[me * per + j] = eu[j, swap.rows(me, patches)]

    for j in range(per_l):
        unmix("l", j, e_l, w2_l, w_l[0], sl_l, ep_l, eu_l, (out_ss_l, out_rs_l), tx_l, rx_l, bk_ss_l, bk_rs_l)
    for j in range(per_s):
        unmix("s", j, e_s, w2_s, w_s[0], sl_s, ep_s, eu_s, (out_ss_s, out_rs_s), tx_s, rx_s, bk_ss_s, bk_rs_s)
    if far_inside:
        tick_near(0)

    ones_l = jnp.ones((8, half), BF)
    vec[8:16, 0:half] = sum(matmul_nt(ones_l, ep_l[j]) for j in range(per_l))
    ones_s = jnp.ones((8, width), BF)
    vec[8:16, half:width] = sum(matmul_nt(ones_s, ep_s[j]) for j in range(per_s))
    top = 2 * patches_l + 2 * patches_s
    if SLAB > top:
        grads[:, top:SLAB, :] = jnp.zeros((size, SLAB - top, token), F32)
    begin = 0
    for left, right, per, patches in (
        (u_l, ep_l, per_l, patches_l), (e_l, h_l, per_l, patches_l),
        (u_s, ep_s, per_s, patches_s), (e_s, h_s, per_s, patches_s),
    ):
        value = sum(matmul_nt(left[j], right[j]) for j in range(per))
        for q in range(size):
            grads[q, begin:begin + patches] = value[q * patches:(q + 1) * patches]
        begin += patches
    for p in range(2):
        tok_tx[p] = grads[p * 2 + 1 - peers.core].astype(BF)
    t_core = send(tok_tx, tok_rx, tc_ss.at[0], tc_rs.at[0], core_peer)
    t_core.start()
    if far_inside:
        tick_near(1)
    t_core.wait_recv()
    there = 1 - peers.x
    tokx_tx[...] = (grads[there * 2 + peers.core] + tok_rx[there].astype(F32)).astype(BF)
    t_x = send(tokx_tx, tokx_rx, tx_ss.at[0], tx_rs.at[0], x_peer)
    t_x.start()
    tok_sum[...] = grads[me] + tok_rx[peers.x].astype(F32)
    tick_core(0)

    def arrived(kind, unit, eu, rx, bss, brs):
        per = per_l if kind == "l" else per_s
        owner = unit // per

        @pl.when(owner != me)
        def _():
            swap.back(kind, unit - owner * per, owner, me, eu, rx, bss, brs).wait_recv()

    def norm_back(x, eu, at):
        unit, scale = unit_rows(x.astype(F32))
        d = eu * gain_ref[...]
        m1 = jnp.mean(d, axis=-1, keepdims=True)
        m2 = jnp.mean(d * unit, axis=-1, keepdims=True)
        ey[at, :] += scale * (d - m1 - unit * m2)
        vec[7:8, :] += jnp.sum(eu * unit, axis=0, keepdims=True)
        return jnp.sum(eu, axis=0, keepdims=True)

    def home_l(n, total):
        arrived("l", 2 * n, eu_l, rx_l, bk_ss_l, bk_rs_l)
        arrived("l", 2 * n + 1, eu_l, rx_l, bk_ss_l, bk_rs_l)
        at = pl.ds(pl.multiple_of(small_rows + n * patches_l, 16), patches_l)
        eu = jnp.concatenate([rx_l[2 * n], rx_l[2 * n + 1]], axis=1).astype(F32)
        return total + norm_back(xl[n], eu, at)

    def home_s(n, total):
        arrived("s", n, eu_s, rx_s, bk_ss_s, bk_rs_s)
        at = pl.ds(pl.multiple_of(n * patches_s, 16), patches_s)
        eu = rx_s[n].astype(F32)
        return total + norm_back(xs[n], eu, at)

    total = lax.fori_loop(0, count_l, home_l, jnp.zeros((1, width), F32))
    total = lax.fori_loop(0, count_s, home_s, total)
    vec[9:10, :] = total
    gx_out = pltpu.make_async_copy(ey, gx_hbm, gx_sem.at[0])
    gx_out.start()

    both = vec.at[0:16]
    v_core = send(both, vec_rx.at[0], v_ss.at[0], v_rs.at[0], core_peer)
    v_core.start()
    if far_inside:
        tick_near(2)
    tick_core(1)
    t_x.wait_recv()
    tok_sum[...] += tokx_rx[...].astype(F32)
    t_near = []
    part_n = SLAB // near
    if far_inside:
        for j, device in near_peers:
            at = pl.ds(pl.multiple_of(lax.rem(peers.near + j, near) * part_n, part_n), part_n)
            tokn_tx[j - 1] = tok_sum[at, :].astype(BF)
            copy = send(tokn_tx.at[j - 1], tokn_rx.at[j - 1], tn_ss.at[j - 1], tn_rs.at[j - 1], device)
            copy.start()
            t_near.append(copy)
    else:
        tok_out[...] = tok_sum[...].astype(BF)
    v_core.wait()
    vec[0:16, :] += vec_rx[0]
    v_x = send(both, vec_rx.at[1], v_ss.at[1], v_rs.at[1], x_peer)
    v_x.start()
    if far_inside:
        tick_near(3)
    tick_core(2)
    t_far = []
    part_f = part_n // far
    if far_inside:
        for copy in t_near:
            copy.wait_recv()
        mine = pl.ds(pl.multiple_of(peers.near * part_n, part_n), part_n)
        tok_half[...] = tok_sum[mine, :]
        for j in range(near - 1):
            tok_half[...] += tokn_rx[j].astype(F32)
        for j, device in far_peers:
            at = pl.ds(pl.multiple_of(lax.rem(peers.far + j, far) * part_f, part_f), part_f)
            tokf_tx[j - 1] = tok_half[at, :].astype(BF)
            copy = send(tokf_tx.at[j - 1], tokf_rx.at[j - 1], tf_ss.at[j - 1], tf_rs.at[j - 1], device)
            copy.start()
            t_far.append(copy)
    v_x.wait()
    vec[0:16, :] += vec_rx[1]
    v_near = [send(vec, vecn_rx.at[j - 1], vn_ss.at[j - 1], vn_rs.at[j - 1], device) for j, device in near_peers]
    for copy in v_near:
        copy.start()
    if far_inside:
        tick_near(4)
    tick_core(3)
    ta_far = []
    if far_inside:
        for copy in t_far:
            copy.wait_recv()
        value = tok_half[pl.ds(pl.multiple_of(peers.far * part_f, part_f), part_f), :]
        for j in range(far - 1):
            value = value + tokf_rx[j].astype(F32)
        span = tok_out.at[pl.ds(pl.multiple_of(peers.near * part_n + peers.far * part_f, part_f), part_f)]
        span[...] = value.astype(BF)
        for j, device in far_peers:
            copy = send(span, span, taf_ss.at[j - 1], taf_rs.at[j - 1], device)
            copy.start()
            ta_far.append(copy)
    for copy in v_near:
        copy.wait()
    for j in range(near - 1):
        vec[...] += vecn_rx[j]
    v_far = [send(vec, vecf_rx.at[j - 1], vf_ss.at[j - 1], vf_rs.at[j - 1], device) for j, device in far_peers]
    for copy in v_far:
        copy.start()
    ta_near = []
    if far_inside:
        for copy in ta_far:
            copy.wait_recv()
        span = tok_out.at[pl.ds(pl.multiple_of(peers.near * part_n, part_n), part_n)]
        for j, device in near_peers:
            copy = send(span, span, tan_ss.at[j - 1], tan_rs.at[j - 1], device)
            copy.start()
            ta_near.append(copy)
        tick_near(5)
    tick_core(4)
    for copy in v_far:
        copy.wait()
    value = vec[...]
    for j in range(far - 1):
        value = value + vecf_rx[j]
    vec_out[...] = value
    for copy in ta_near:
        copy.wait_recv()
    tick_core(5)

    for copy in [t_core, t_x] + t_near + t_far + ta_far + ta_near:
        copy.wait_send()
    for k in range(1, size):
        there = swap.other(k)
        for j in range(per_l):
            swap.out("l", j, there, me, tx_l, e_l, out_ss_l, out_rs_l).wait_send()
            swap.back("l", j, me, there, eu_l, rx_l, bk_ss_l, bk_rs_l).wait_send()
        for j in range(per_s):
            swap.out("s", j, there, me, tx_s, e_s, out_ss_s, out_rs_s).wait_send()
            swap.back("s", j, me, there, eu_s, rx_s, bk_ss_s, bk_rs_s).wait_send()
    for k in range(GROUPS):
        g_x(k).wait_send()
        for copy in g_far(k) + g_near(k):
            copy.wait_send()
        g_core(k).wait()
    gx_out.wait()


def backward(chunk, ey, xl, xs, saved, small, gain):
    size = lax.axis_size("blk")
    near, far = img_split(lax.axis_size("img"))
    rows, width = ey.shape
    far_inside = width % (near * far * 2 * 16) == 0
    u_l, u_s, h_l, h_s, sl_l, sl_s, w_l, w_s = saved
    count_l, patches_l, _ = xl.shape
    count_s, patches_s, _ = xs.shape
    token = w_l.shape[2]
    half = width // 2
    per_l, per_s = u_l.shape[0], u_s.shape[0]
    each, hidden = chunk.shape
    vmem = pl.BlockSpec(memory_space=pltpu.VMEM)
    V = pltpu.VMEM
    DMA = pltpu.SemaphoreType.DMA
    n1, f1 = near - 1, far - 1
    part_n = SLAB // near
    part_f = max(part_n // far, 16)
    return pl.pallas_call(
        functools.partial(backward_kernel, near, far, size, far_inside),
        out_shape=(
            jax.ShapeDtypeStruct((2, width, hidden), BF),
            jax.ShapeDtypeStruct((rows, width), F32),
            jax.ShapeDtypeStruct((SLAB, token), BF),
            jax.ShapeDtypeStruct((24, width), F32),
        ),
        in_specs=[ANY, ANY] + [vmem] * 12,
        out_specs=(ANY, ANY, vmem, vmem),
        scratch_shapes=[
            V((rows, width), F32),
            V((count_l * 2, patches_l, half), BF), V((count_s, patches_s, width), BF),
            V(u_l.shape, BF), V(u_s.shape, BF),
            V((token, size * patches_l), BF), V((token, size * patches_s), BF),
            V(h_l.shape, BF), V(h_s.shape, BF), V(u_l.shape, BF), V(u_s.shape, BF),
            V((count_l * 2, patches_l, half), BF), V((count_s, patches_s, width), BF),
            V((size, SLAB, token), F32), V((2, SLAB, token), BF), V((2, SLAB, token), BF),
            V((SLAB, token), BF), V((SLAB, token), BF), V((SLAB, token), F32),
            V((n1, part_n, token), BF), V((n1, part_n, token), BF), V((part_n, token), F32),
            V((f1, part_f, token), BF), V((f1, part_f, token), BF),
            V((24, width), F32), V((2, 16, width), F32), V((n1, 24, width), F32), V((f1, 24, width), F32),
            DMA((1,)), DMA((1,)),
            DMA((GROUPS,)), DMA((GROUPS,)), DMA((GROUPS,)), DMA((GROUPS, f1)), DMA((GROUPS, f1)),
            DMA((GROUPS, n1)), DMA((GROUPS, n1)), DMA((GROUPS,)), DMA((GROUPS,)),
            DMA((count_l * 2,)), DMA((count_s,)), DMA((per_l, size)), DMA((per_s, size)),
            DMA((per_l, size)), DMA((per_s, size)), DMA((count_l * 2,)), DMA((count_s,)),
            DMA((1,)), DMA((1,)), DMA((1,)), DMA((1,)), DMA((n1,)), DMA((n1,)), DMA((f1,)), DMA((f1,)),
            DMA((f1,)), DMA((f1,)), DMA((n1,)), DMA((n1,)),
            DMA((2,)), DMA((2,)), DMA((n1,)), DMA((n1,)), DMA((f1,)), DMA((f1,)),
        ],
        compiler_params=pltpu.CompilerParams(
            collective_id=1, has_side_effects=True, vmem_limit_bytes=TOP
        ),
    )(chunk, ey, xl, xs, u_l, u_s, h_l, h_s, sl_l, sl_s, w_l, w_s, small, gain.reshape(1, -1))


def widen_kernel(first, second, out_first, out_second):
    out_first[...] = first[0].astype(F32)
    out_second[...] = second[0].astype(F32).T


def widen(full):
    _, width, hidden = full.shape
    step = 384
    return pl.pallas_call(
        widen_kernel,
        grid=(hidden // step,),
        out_shape=(jax.ShapeDtypeStruct((width, hidden), F32), jax.ShapeDtypeStruct((hidden, width), F32)),
        in_specs=[
            pl.BlockSpec((1, width, step), lambda i: (0, 0, i)),
            pl.BlockSpec((1, width, step), lambda i: (1, 0, i)),
        ],
        out_specs=(pl.BlockSpec((width, step), lambda i: (0, i)), pl.BlockSpec((step, width), lambda i: (i, 0))),
        compiler_params=pltpu.CompilerParams(vmem_limit_bytes=TOP),
    )(full, full)


def local(
    x_small, x_large, live_counts, ln1_gain, ln1_bias,
    tok_w1_small, tok_b1_small, tok_w2_small, tok_b2_small,
    tok_w1_large, tok_b1_large, tok_w2_large, tok_b2_large,
    ln2_gain, ln2_bias, ch_w1, ch_b1, ch_w2, ch_b2, cot_small, cot_large,
):
    width = x_small.shape[2]
    token = tok_w1_large.shape[1]
    patches_s, patches_l = x_small.shape[1], x_large.shape[1]
    extra = -patches_s % 64
    wide_s = patches_s + extra
    small_rows = x_small.shape[0] * wide_s
    large_rows = x_large.shape[0] * patches_l
    rows = small_rows + large_rows
    spare = -rows % (3 * LANES)

    def widen_small(small):
        return jnp.pad(small, ((0, 0), (0, extra), (0, 0)))

    def part(joined):
        small = joined[:small_rows].reshape(x_small.shape[0], wide_s, width)[:, :patches_s]
        return small, joined[small_rows:rows].reshape(x_large.shape)

    mask_small = (jnp.arange(x_small.shape[0]) < live_counts[0, 0]).astype(BF)[:, None, None]
    mask_large = (jnp.arange(x_large.shape[0]) < live_counts[0, 1]).astype(BF)[:, None, None]
    xs = widen_small(x_small)
    wq_l = jnp.stack([tok_w1_large, tok_w2_large.T])
    wq_s = widen_small(jnp.stack([tok_w1_small, tok_w2_small.T]))
    y, *saved = token_forward(
        x_large, xs, wq_l, wq_s, tok_b1_large, tok_b1_small, tok_b2_large, jnp.pad(tok_b2_small, (0, extra)),
        ln1_gain, ln1_bias, rows + spare,
    )
    ec = jnp.concatenate([
        widen_small(cot_small * mask_small).reshape(-1, width),
        (cot_large * mask_large).reshape(-1, width),
        jnp.zeros((spare, width), BF),
    ])
    out, ey, chunk, small_grads = channel(y, ec, ch_w1, ch_w2, ch_b1, ln2_gain, ln2_bias, ch_b2)
    near, far = img_split(lax.axis_size("img"))
    far_inside = width % (near * far * 2 * 16) == 0
    if not far_inside:
        same = [[a * near + b for a in range(far)] for b in range(near)]
        chunk = lax.psum(chunk.astype(F32), "img", axis_index_groups=same).astype(BF)
    full, gx, tok, vec = backward(chunk, ey, x_large, xs, saved, small_grads, ln1_gain)
    tok = tok.astype(F32)
    if not far_inside:
        tok = lax.psum(tok, "img")
    grad_ch_w1, grad_ch_w2 = widen(full)
    out_small, out_large = part(out)
    gx_small, gx_large = part(gx)
    half = width // 2
    b2_l = vec[16, :patches_l]
    b2_s = vec[16, half:half + patches_s]
    at = 2 * patches_l
    return (
        out_small * mask_small, out_large * mask_large, gx_small, gx_large, vec[7], vec[9],
        tok[at:at + patches_s], vec[8, half:], tok[at + wide_s:at + wide_s + patches_s].T, b2_s,
        tok[:patches_l], vec[8, :half], tok[patches_l:at].T, b2_l,
        vec[5], vec[6], grad_ch_w1, vec[:4].reshape(-1), grad_ch_w2, vec[4],
    )


def solution(mesh):
    image = P("img", "blk", None)
    whole = P()
    rows = P("blk", None)
    columns = P(None, "blk")
    vector = P("blk")
    in_specs = (
        image, image, P("img", None), whole, whole,
        rows, whole, columns, vector, rows, whole, columns, vector,
        whole, whole, whole, whole, whole, whole, image, image,
    )
    out_specs = (
        image, image, image, image, whole, whole,
        rows, whole, columns, vector, rows, whole, columns, vector,
        whole, whole, whole, whole, whole, whole,
    )
    return jax.shard_map(local, mesh=mesh, in_specs=in_specs, out_specs=out_specs, check_vma=False)
```

```python
import functools

import jax
import jax.numpy as jnp
from jax import lax
from jax.experimental import pallas as pl
from jax.experimental.pallas import tpu as pltpu
from jax.sharding import PartitionSpec as P

EPSILON = 1e-06
LANES = 128
BF = jnp.bfloat16
F32 = jnp.float32


MESH = pl.DeviceIdType.MESH
ANY = pl.BlockSpec(memory_space=pl.ANY)
TILE = 256
TOP = 62 * 1024 * 1024


def img_split(size):
    near = 2 if size <= 8 else 8
    return near, size // near


def gelu_pair(a):
    square = a * a
    slope = 0.7978845608028654
    t = jnp.tanh(a * (slope + (slope * 0.044715) * square))
    half = 0.5 + 0.5 * t
    inner = slope + (3.0 * slope * 0.044715) * square
    return a * half, half + (0.5 * a) * (1.0 - t * t) * inner


class Peers:
    def __init__(self, near_count):
        self.img = lax.axis_index("img")
        self.blk = lax.axis_index("blk")
        self.core = lax.rem(self.blk, 2)
        self.x = self.blk // 2
        self.near_count = near_count
        self.near = lax.rem(self.img, near_count)
        self.far = self.img // near_count

    def at(self, axis, place):
        if axis == "core":
            return (self.img, self.x * 2 + place)
        if axis == "x":
            return (self.img, place * 2 + self.core)
        if axis == "near":
            return (self.far * self.near_count + place, self.blk)
        return (place * self.near_count + self.near, self.blk)

    def mine(self, axis):
        return {"core": self.core, "x": self.x, "near": self.near, "far": self.far}[axis]


def greet(peers, axes):
    barrier = pltpu.get_barrier_semaphore()
    total = 0
    for axis, count in axes:
        for j in range(1, count):
            there = lax.rem(peers.mine(axis) + j, count)
            pl.semaphore_signal(barrier, inc=1, device_id=peers.at(axis, there), device_id_type=MESH)
            total += 1
    pl.semaphore_wait(barrier, total)


def row(ref):
    return ref[...].reshape(1, -1)


def column(ref, rows):
    value = jnp.broadcast_to(ref[...].reshape(1, -1), (8, ref.shape[0])).T[:, :1]
    return value if rows == ref.shape[0] else jnp.concatenate([value, jnp.zeros((rows - ref.shape[0], 1), F32)])


def channel_kernel(
    near, far, far_inside,
    y_hbm, live, cot_l, cot_s, w1_hbm, w2_hbm, b1_ref, gain_ref, bias_ref, b2_ref,
    out_l, ey_hbm, chunk_ref, small_ref, out_s,
    y, ec, v, lt, rt, w1, w2, acc_out, acc_ev, out_low,
    keep, core_tx, core_rx,
    a_keep_n, a_near_tx, a_near_rx, a_keep_f, a_far_tx, a_far_rx, a_keep_x, a_x_tx, a_x_rx,
    b_keep_x, b_x_tx, b_x_rx, b_keep_n, b_near_tx, b_near_rx, b_keep_f, b_far_tx, b_far_rx,
    in_sem, w_sem, out_sem, core_ss, core_rs,
    a_near_ss, a_near_rs, a_far_ss, a_far_rs, a_x_ss, a_x_rs,
    b_near_ss, b_near_rs, b_far_ss, b_far_rs, b_x_ss, b_x_rs,
):
    rows, width = y.shape
    tiles = w1.shape[0]
    count_l, patches_l, _ = cot_l.shape
    count_s, patches_s, _ = cot_s.shape
    wide_s = patches_s + -patches_s % 64
    small_rows = count_s * wide_s
    peers = Peers(near)
    core = peers.core
    f_place = peers.far if far_inside else 0
    part = 128
    parts = rows // part
    gain, bias, b2 = row(gain_ref), row(bias_ref), row(b2_ref)

    def w_copies(t):
        return (
            pltpu.make_async_copy(w1_hbm.at[:, pl.ds(t * TILE, TILE)], w1.at[t], w_sem.at[0, t]),
            pltpu.make_async_copy(w2_hbm.at[pl.ds(t * TILE, TILE)], w2.at[t], w_sem.at[1, t]),
        )

    y_in = pltpu.make_async_copy(y_hbm, y, in_sem.at[0])
    y_in.start()

    def start_w(t, carry):
        for copy in w_copies(t):
            copy.start()
        return carry

    lax.fori_loop(0, tiles, start_w, 0)
    axes = [("core", 2), ("near", near)] + ([("far", far)] if far_inside else []) + [("x", 2)]
    greet(peers, axes)
    small_ref[...] = jnp.zeros_like(small_ref)
    used = small_rows + count_l * patches_l
    ec[0:small_rows, :] = jnp.zeros((small_rows, width), BF)
    if rows > used:
        ec[used:rows, :] = jnp.zeros((rows - used, width), BF)

    def live_l(n):
        return jnp.where(n < live[0, 1], 1.0, 0.0).astype(F32)

    def live_s(n):
        return jnp.where(n < live[0, 0], 1.0, 0.0).astype(F32)

    def mask_l(n, carry):
        ec[pl.ds(pl.multiple_of(small_rows + n * patches_l, 16), patches_l), :] = (
            cot_l[n].astype(F32) * live_l(n)
        ).astype(BF)
        return carry

    def mask_s(n, carry):
        ec[pl.ds(pl.multiple_of(n * wide_s, 16), patches_s), :] = (cot_s[n].astype(F32) * live_s(n)).astype(BF)
        return carry

    lax.fori_loop(0, count_l, mask_l, 0)
    lax.fori_loop(0, count_s, mask_s, 0)
    y_in.wait()

    def prepare(p, carry):
        at = pl.ds(pl.multiple_of(p * part, part), part)
        unit, _ = unit_rows(y[at, :])
        low = (unit * gain + bias).astype(BF)
        v[at, :] = low
        lt[0, :, at] = low.T
        own = ec[at, :]
        lt[1, :, at] = own.T
        small_ref[4:5, :] += jnp.sum(own.astype(F32), axis=0, keepdims=True)
        acc_out[at, :] = jnp.zeros((part, width), F32)
        acc_ev[at, :] = jnp.zeros((part, width), F32)
        return carry

    lax.fori_loop(0, parts, prepare, 0)

    def send(src, dst, ss, rs, device):
        return pltpu.make_async_remote_copy(
            src_ref=src, dst_ref=dst, send_sem=ss, recv_sem=rs, device_id=device, device_id_type=MESH
        )

    def core_copy(t):
        slot = lax.rem(t, 2)
        return send(core_tx.at[slot], core_rx.at[t], core_ss.at[slot], core_rs.at[t], peers.at("core", 1 - core))

    def spread(tx, rx, ss, rs, axis, count, i):
        slot = lax.rem(i, 2)
        copies = []
        for j in range(1, count):
            there = lax.rem(peers.mine(axis) + j, count)
            copies.append(
                send(tx.at[slot, j - 1], rx.at[i, j - 1], ss.at[slot, j - 1], rs.at[i, j - 1], peers.at(axis, there))
            )
        return copies

    f = far if far_inside else 1
    a_near = lambda i: spread(a_near_tx, a_near_rx, a_near_ss, a_near_rs, "near", near, i)
    a_far = lambda i: spread(a_far_tx, a_far_rx, a_far_ss, a_far_rs, "far", f, i)
    a_x = lambda i: spread(a_x_tx, a_x_rx, a_x_ss, a_x_rs, "x", 2, i)
    b_near = lambda i: spread(b_near_tx, b_near_rx, b_near_ss, b_near_rs, "near", near, i)
    b_far = lambda i: spread(b_far_tx, b_far_rx, b_far_ss, b_far_rs, "far", f, i)
    b_x = lambda i: spread(b_x_tx, b_x_rx, b_x_ss, b_x_rs, "x", 2, i)
    each = width // near // f // 2

    def tile_step(t):
        for copy in w_copies(t):
            copy.wait()
        columns = pl.ds(pl.multiple_of(t * TILE, TILE), TILE)
        a = matmul(v[...], w1[t]) + b1_ref[columns].reshape(1, -1)
        gh = matmul_nt(ec[...], w2[t])
        g, slope = gelu_pair(a)
        ea = (slope * gh).astype(BF)
        rt[1] = g.astype(BF)
        rt[0] = ea
        per = width // TILE
        small_ref[lax.div(t, per), pl.ds(pl.multiple_of(lax.rem(t, per) * TILE, TILE), TILE)] = jnp.sum(
            ea.astype(F32), axis=0
        )
        slot = lax.rem(t, 2)

        @pl.when(t >= 2)
        def _():
            core_copy(t - 2).wait_send()

        core_tx[slot] = matmul(lt[1 - core], rt[1 - core]).astype(BF).reshape(near, f, 2, each, TILE)
        core_copy(t).start()
        keep[slot] = matmul(lt[core], rt[core]).reshape(near, f, 2, each, TILE)
        acc_out[...] += matmul(rt[1], w2[t])
        acc_ev[...] += matmul_nt(rt[0], w1[t])

    def ey_copy(at, n):
        return pltpu.make_async_copy(acc_ev.at[at], ey_hbm.at[at], out_sem.at[n])

    def at_l(n):
        return pl.ds(pl.multiple_of(small_rows + n * patches_l, 16), patches_l)

    def at_s(n):
        return pl.ds(pl.multiple_of(n * wide_s, 16), wide_s)

    def out_copy(n):
        return pltpu.make_async_copy(out_low.at[n], out_l.at[n], out_sem.at[count_l + count_s + n])

    def finish_rows(at, live_here):
        here = y[at, :]
        result = ((here + acc_out[at, :] + b2) * live_here).astype(BF)
        unit, scale = unit_rows(here)
        ev = acc_ev[at, :]
        small_ref[5:6, :] += jnp.sum(ev * unit, axis=0, keepdims=True)
        small_ref[6:7, :] += jnp.sum(ev, axis=0, keepdims=True)
        d = ev * gain
        m1 = jnp.mean(d, axis=-1, keepdims=True)
        m2 = jnp.mean(d * unit, axis=-1, keepdims=True)
        acc_ev[at, :] = ec[at, :].astype(F32) + scale * (d - m1 - unit * m2)
        return result

    def finish(p):
        def one_l(q, carry):
            n = p + q * 4

            @pl.when(n < count_l)
            def _():
                out_low[n] = finish_rows(at_l(n), live_l(n))
                ey_copy(at_l(n), n).start()
                out_copy(n).start()

            return carry

        def one_s(q, carry):
            n = p + q * 4

            @pl.when(n < count_s)
            def _():
                out_s[n] = finish_rows(at_s(n), live_s(n))[:patches_s]
                ey_copy(at_s(n), count_l + n).start()

            return carry

        lax.fori_loop(0, pl.cdiv(count_l, 4), one_l, 0)
        lax.fori_loop(0, pl.cdiv(count_s, 4), one_s, 0)

    def free(copies, i):
        @pl.when(i >= 2)
        def _():
            for copy in copies(i - 2):
                copy.wait_send()

    def reduce(value, axis, count, place, tx, own, copies, i):
        slot = lax.rem(i, 2)
        free(copies, i)
        made = copies(i)
        for j in range(1, count + 1):
            there = lax.rem(place + j, count)
            piece = value(there)
            if j < count:
                tx[slot, j - 1] = piece.astype(BF)
                made[j - 1].start()
            else:
                own(slot, piece)

    def arrivals(copies, i):
        for copy in copies(i):
            copy.wait_recv()

    def save(ref):
        def put(slot, piece):
            ref[slot] = piece
        return put

    def plus(base, rx, i, count, index):
        value = base
        for k in range(count - 1):
            value = value + rx[(i, k) + index].astype(F32)
        return value

    def chunk_out(t, value):
        chunk_ref[:, pl.ds(pl.multiple_of(t * TILE, TILE), TILE)] = value.astype(BF)

    def even_core(t):
        i = lax.div(t, 2)
        core_copy(t).wait_recv()
        reduce(
            lambda p: keep[0, p] + core_rx[t, p].astype(F32),
            "near", near, peers.near, a_near_tx, save(a_keep_n), a_near, i,
        )

    def even_near(t):
        i = lax.div(t, 2)
        slot = lax.rem(i, 2)
        arrivals(a_near, i)
        reduce(
            lambda p: plus(a_keep_n[slot, p], a_near_rx, i, near, (p,)),
            "far", f, f_place, a_far_tx, save(a_keep_f), a_far, i,
        )

    def even_far(t):
        i = lax.div(t, 2)
        slot = lax.rem(i, 2)
        arrivals(a_far, i)
        reduce(
            lambda p: plus(a_keep_f[slot, p], a_far_rx, i, f, (p,)),
            "x", 2, peers.x, a_x_tx, save(a_keep_x), a_x, i,
        )

    def even_x(t):
        i = lax.div(t, 2)
        arrivals(a_x, i)
        chunk_out(t, a_keep_x[lax.rem(i, 2)] + a_x_rx[i, 0].astype(F32))

    def odd_core(t):
        i = lax.div(t, 2)
        core_copy(t).wait_recv()
        reduce(
            lambda p: keep[1, :, :, p] + core_rx[t, :, :, p].astype(F32),
            "x", 2, peers.x, b_x_tx, save(b_keep_x), b_x, i,
        )

    def odd_x(t):
        i = lax.div(t, 2)
        slot = lax.rem(i, 2)
        arrivals(b_x, i)
        reduce(
            lambda p: plus(b_keep_x[slot, p], b_x_rx, i, 2, (p,)),
            "near", near, peers.near, b_near_tx, save(b_keep_n), b_near, i,
        )

    def odd_near(t):
        i = lax.div(t, 2)
        slot = lax.rem(i, 2)
        arrivals(b_near, i)
        reduce(
            lambda p: plus(b_keep_n[slot, p], b_near_rx, i, near, (p,)),
            "far", f, f_place, b_far_tx, save(b_keep_f), b_far, i,
        )

    def odd_far(t):
        i = lax.div(t, 2)
        arrivals(b_far, i)
        slot = lax.rem(i, 2)
        chunk_out(t, plus(b_keep_f[slot], b_far_rx, i, f, ()))

    stages = ((even_core, even_near, even_far, even_x), (odd_core, odd_x, odd_near, odd_far))

    def pair(s2, carry):
        for parity in range(2):
            s = s2 * 2 + parity

            @pl.when(s < tiles)
            def _():
                tile_step(s)

            for lag in range(1, 5):
                t = s - lag
                stage = stages[(parity - lag) % 2][lag - 1]

                @pl.when((t >= 0) & (t < tiles))
                def _(t=t, stage=stage):
                    stage(t)

            @pl.when(s >= tiles)
            def _():
                finish(s - tiles)

        return carry

    lax.fori_loop(0, (tiles + 4) // 2, pair, 0)
    for t in (tiles - 2, tiles - 1):
        core_copy(t).wait_send()
    for copies in (a_near, a_far, a_x, b_near, b_far, b_x):
        for i in (tiles // 2 - 2, tiles // 2 - 1):
            for copy in copies(i):
                copy.wait_send()
    for n in range(count_l):
        ey_copy(at_l(n), n).wait()
        out_copy(n).wait()
    for n in range(count_s):
        ey_copy(at_s(n), count_l + n).wait()


def channel(y, live, cot_l, cot_s, w1, w2, b1, gain, bias, b2):
    rows, width = y.shape
    hidden = w1.shape[1]
    tiles = hidden // TILE
    near, far = img_split(lax.axis_size("img"))
    far_inside = width % (near * far * 2 * 16) == 0
    f = far if far_inside else 1
    chunk = width // near // f // 2
    vmem = pl.BlockSpec(memory_space=pltpu.VMEM)
    V = pltpu.VMEM
    DMA = pltpu.SemaphoreType.DMA
    fm = max(f - 1, 1)
    nm = near - 1
    pairs = tiles // 2
    count = cot_l.shape[0] + cot_s.shape[0]
    return pl.pallas_call(
        functools.partial(channel_kernel, near, far, far_inside),
        out_shape=(
            jax.ShapeDtypeStruct(cot_l.shape, BF),
            jax.ShapeDtypeStruct((rows, width), F32),
            jax.ShapeDtypeStruct((chunk, hidden), BF),
            jax.ShapeDtypeStruct((8, width), F32),
            jax.ShapeDtypeStruct(cot_s.shape, BF),
        ),
        in_specs=[ANY, pl.BlockSpec(memory_space=pltpu.SMEM), vmem, vmem, ANY, ANY] + [vmem] * 4,
        out_specs=(ANY, ANY, vmem, vmem, vmem),
        scratch_shapes=[
            V((rows, width), F32), V((rows, width), BF), V((rows, width), BF),
            V((2, width, rows), BF), V((2, rows, TILE), BF),
            V((tiles, width, TILE), BF), V((tiles, TILE, width), BF),
            V((rows, width), F32), V((rows, width), F32), V(cot_l.shape, BF),
            V((2, near, f, 2, chunk, TILE), F32), V((2, near, f, 2, chunk, TILE), BF),
            V((tiles, near, f, 2, chunk, TILE), BF),
            V((2, f, 2, chunk, TILE), F32), V((2, nm, f, 2, chunk, TILE), BF), V((pairs, nm, f, 2, chunk, TILE), BF),
            V((2, 2, chunk, TILE), F32), V((2, fm, 2, chunk, TILE), BF), V((pairs, fm, 2, chunk, TILE), BF),
            V((2, chunk, TILE), F32), V((2, 1, chunk, TILE), BF), V((pairs, 1, chunk, TILE), BF),
            V((2, near, f, chunk, TILE), F32), V((2, 1, near, f, chunk, TILE), BF),
            V((pairs, 1, near, f, chunk, TILE), BF),
            V((2, f, chunk, TILE), F32), V((2, nm, f, chunk, TILE), BF), V((pairs, nm, f, chunk, TILE), BF),
            V((2, chunk, TILE), F32), V((2, fm, chunk, TILE), BF), V((pairs, fm, chunk, TILE), BF),
            DMA((1,)), DMA((2, tiles)), DMA((2 * count,)), DMA((2,)), DMA((tiles,)),
            DMA((2, nm)), DMA((pairs, nm)), DMA((2, fm)), DMA((pairs, fm)), DMA((2, 1)), DMA((pairs, 1)),
            DMA((2, nm)), DMA((pairs, nm)), DMA((2, fm)), DMA((pairs, fm)), DMA((2, 1)), DMA((pairs, 1)),
        ],
        compiler_params=pltpu.CompilerParams(
            collective_id=0, has_side_effects=True, vmem_limit_bytes=TOP
        ),
    )(y, live, cot_l, cot_s, w1, w2, b1, gain, bias, b2)


NT = (((1,), (1,)), ((), ()))


def matmul(left, right):
    return jnp.dot(left, right, preferred_element_type=F32)


def matmul_nt(left, right):
    return lax.dot_general(left, right, NT, preferred_element_type=F32)


class Swap:
    def __init__(self, peers, size, per_l, per_s, patches_l, patches_s):
        self.peers, self.size = peers, size
        self.per_l, self.per_s = per_l, per_s
        self.pl, self.ps = patches_l, patches_s

    def other(self, step):
        return lax.rem(self.peers.blk + step, self.size)

    def copy(self, src, dst, ss, rs, place):
        return pltpu.make_async_remote_copy(
            src_ref=src, dst_ref=dst, send_sem=ss, recv_sem=rs,
            device_id=(self.peers.img, place), device_id_type=MESH,
        )

    def rows(self, place, patches):
        return pl.ds(pl.multiple_of(place * patches, patches), patches)

    def out(self, kind, j, place, source, tx, cols, ss, rs):
        per, patches = (self.per_l, self.pl) if kind == "l" else (self.per_s, self.ps)
        unit = place * per + j
        return self.copy(
            tx.at[unit], cols.at[j, self.rows(source, patches)], ss.at[unit], rs.at[j, source], place
        )

    def back(self, kind, j, owner, place, cols, rx, ss, rs):
        per, patches = (self.per_l, self.pl) if kind == "l" else (self.per_s, self.ps)
        unit = owner * per + j
        return self.copy(
            cols.at[j, self.rows(place, patches)], rx.at[unit], ss.at[j, place], rs.at[unit], place
        )


def greet_all(peers, size, near, far):
    barrier = pltpu.get_barrier_semaphore()
    total = 0
    for j in range(1, size):
        there = lax.rem(peers.blk + j, size)
        pl.semaphore_signal(barrier, inc=1, device_id=(peers.img, there), device_id_type=MESH)
        total += 1
    for axis, count in (("near", near), ("far", far)):
        for j in range(1, count):
            there = lax.rem(peers.mine(axis) + j, count)
            pl.semaphore_signal(barrier, inc=1, device_id=peers.at(axis, there), device_id_type=MESH)
            total += 1
    pl.semaphore_wait(barrier, total)


def unit_rows(row):
    mean = jnp.mean(row, axis=-1, keepdims=True)
    centered = row - mean
    var = jnp.mean(centered * centered, axis=-1, keepdims=True)
    scale = lax.rsqrt(var + EPSILON)
    return centered * scale, scale


def token_kernel(
    near, size,
    xl, xs, w1_l, w1_s, w2_l, w2_s, b1_l_ref, b1_s_ref, b2_l_ref, b2_s_ref, gain_ref, bias_ref,
    y_hbm, u_l, u_s, h_l, h_s, sl_l, sl_s, w_l, w_s,
    wq_l, wq_s, tx_l, tx_s, w1t_l, w1t_s, m_l, m_s, rx_l, rx_s, y,
    y_sem, own_sem, wown, w_ss, w_rs, out_ss_l, out_ss_s, out_rs_l, out_rs_s, bk_ss_l, bk_ss_s, bk_rs_l, bk_rs_s,
):
    peers = Peers(near)
    me = peers.blk
    count_l, patches_l, width = xl.shape
    count_s, real_s, _ = xs.shape
    patches_s = tx_s.shape[1]
    token = w1_l.shape[1]
    half = width // 2
    per_l, per_s = count_l * 2 // size, count_s // size
    swap = Swap(peers, size, per_l, per_s, patches_l, patches_s)
    wq_l[0] = w1_l[...]
    wq_l[1] = w2_l[...].astype(F32).T.astype(BF)
    wq_s[...] = jnp.zeros_like(wq_s)
    wq_s[0, :real_s] = w1_s[...]
    wq_s[1, :real_s] = w2_s[...].astype(F32).T.astype(BF)

    barrier = pltpu.get_barrier_semaphore()
    for j in range(1, size):
        pl.semaphore_signal(barrier, inc=1, device_id=(peers.img, swap.other(j)), device_id_type=MESH)
    pl.semaphore_wait(barrier, size - 1)

    def weights(src_l, src_s, quarter, n, place):
        return (
            swap.copy(src_l, w_l.at[:, swap.rows(quarter, patches_l)], w_ss.at[n, 0], w_rs.at[n, 0], place),
            swap.copy(src_s, w_s.at[:, swap.rows(quarter, patches_s)], w_ss.at[n, 1], w_rs.at[n, 1], place),
        )

    x_peer = (1 - peers.x) * 2 + peers.core
    core_peer = peers.x * 2 + 1 - peers.core
    to_x = weights(wq_l, wq_s, me, 0, x_peer)
    to_core = weights(wq_l, wq_s, me, 1, core_peer)
    relay = weights(
        w_l.at[:, swap.rows(x_peer, patches_l)], w_s.at[:, swap.rows(x_peer, patches_s)], x_peer, 2, core_peer
    )
    for copy in to_x + to_core:
        copy.start()
    own_w = (
        pltpu.make_async_copy(wq_l, w_l.at[:, swap.rows(me, patches_l)], wown.at[0]),
        pltpu.make_async_copy(wq_s, w_s.at[:, swap.rows(me, patches_s)], wown.at[1]),
    )
    for copy in own_w:
        copy.start()

    gain, bias = row(gain_ref), row(bias_ref)

    def norm(values):
        unit, _ = unit_rows(values.astype(F32))
        return (unit * gain + bias).astype(BF)

    def norm_l(n, carry):
        u = norm(xl[n])
        tx_l[2 * n] = u[:, :half]
        tx_l[2 * n + 1] = u[:, half:]
        return carry

    tx_s[...] = jnp.zeros_like(tx_s)

    def norm_s(n, carry):
        tx_s[n, :real_s] = norm(xs[n])
        return carry

    lax.fori_loop(0, count_l, norm_l, 0)
    for j in range(per_l):
        for k in range(1, size):
            swap.out("l", j, swap.other(k), me, tx_l, u_l, out_ss_l, out_rs_l).start()
    lax.fori_loop(0, count_s, norm_s, 0)
    for j in range(per_s):
        for k in range(1, size):
            swap.out("s", j, swap.other(k), me, tx_s, u_s, out_ss_s, out_rs_s).start()
    for j in range(per_l):
        u_l[j, swap.rows(me, patches_l)] = tx_l[me * per_l + j]
    for j in range(per_s):
        u_s[j, swap.rows(me, patches_s)] = tx_s[me * per_s + j]

    for copy in to_x:
        copy.wait_recv()
    for copy in relay:
        copy.start()
    for copy in own_w:
        copy.wait()
    for copy in to_core + relay:
        copy.wait_recv()
    b1_l, b1_s = column(b1_l_ref, token), column(b1_s_ref, token)
    b2_l, b2_s = column(b2_l_ref, patches_l), column(b2_s_ref, real_s)
    w1t_l[...] = w_l[0].T
    w1t_s[...] = w_s[0].T

    def mix(kind, j, cols, w1t, w2t, b1, h, slope, m, outs, tx, rx, bss, brs):
        for k in range(1, size):
            source = swap.other(k)
            swap.out(kind, j, me, source, tx, cols, *outs).wait_recv()
        g, d = gelu_pair(matmul(w1t[...], cols[j]) + b1)
        low = g.astype(BF)
        h[j] = low
        slope[j] = d.astype(BF)
        m[j] = matmul(w2t, low).astype(BF)
        for k in range(1, size):
            swap.back(kind, j, me, swap.other(k), m, rx, bss, brs).start()
        patches, per = (patches_l, per_l) if kind == "l" else (patches_s, per_s)
        rx[me * per + j] = m[j, swap.rows(me, patches)]

    for j in range(per_l):
        mix("l", j, u_l, w1t_l, w_l[1], b1_l, h_l, sl_l, m_l, (out_ss_l, out_rs_l), tx_l, rx_l, bk_ss_l, bk_rs_l)
    for j in range(per_s):
        mix("s", j, u_s, w1t_s, w_s[1], b1_s, h_s, sl_s, m_s, (out_ss_s, out_rs_s), tx_s, rx_s, bk_ss_s, bk_rs_s)

    small_rows = count_s * patches_s
    rows = y.shape[0]
    used = small_rows + count_l * patches_l
    y[0:small_rows, :] = jnp.zeros((small_rows, width), F32)
    if rows > used:
        y[used:rows, :] = jnp.zeros((rows - used, width), F32)

    def arrived(kind, unit, m, rx, bss, brs):
        per = per_l if kind == "l" else per_s
        owner = unit // per

        @pl.when(owner != me)
        def _():
            swap.back(kind, unit - owner * per, owner, me, m, rx, bss, brs).wait_recv()

    def home_l(n, carry):
        arrived("l", 2 * n, m_l, rx_l, bk_ss_l, bk_rs_l)
        arrived("l", 2 * n + 1, m_l, rx_l, bk_ss_l, bk_rs_l)
        at = pl.ds(pl.multiple_of(small_rows + n * patches_l, 16), patches_l)
        y[at, :half] = xl[n, :, :half].astype(F32) + rx_l[2 * n].astype(F32) + b2_l
        y[at, half:] = xl[n, :, half:].astype(F32) + rx_l[2 * n + 1].astype(F32) + b2_l
        return carry

    def home_s(n, carry):
        arrived("s", n, m_s, rx_s, bk_ss_s, bk_rs_s)
        at = pl.ds(pl.multiple_of(n * patches_s, 16), real_s)
        y[at, :] = xs[n].astype(F32) + rx_s[n, :real_s].astype(F32) + b2_s
        return carry

    lax.fori_loop(0, count_l, home_l, 0)
    lax.fori_loop(0, count_s, home_s, 0)
    y_out = pltpu.make_async_copy(y, y_hbm, y_sem.at[0])
    y_out.start()
    for copy in to_x + to_core + relay:
        copy.wait_send()
    for k in range(1, size):
        there = swap.other(k)
        for j in range(per_l):
            swap.out("l", j, there, me, tx_l, u_l, out_ss_l, out_rs_l).wait_send()
            swap.back("l", j, me, there, m_l, rx_l, bk_ss_l, bk_rs_l).wait_send()
        for j in range(per_s):
            swap.out("s", j, there, me, tx_s, u_s, out_ss_s, out_rs_s).wait_send()
            swap.back("s", j, me, there, m_s, rx_s, bk_ss_s, bk_rs_s).wait_send()
    y_out.wait()


def token_forward(xl, xs, w1_l, w1_s, w2_l, w2_s, b1_l, b1_s, b2_l, b2_s, gain, bias, rows):
    size = lax.axis_size("blk")
    near, far = img_split(lax.axis_size("img"))
    count_l, patches_l, width = xl.shape
    count_s, patches_s, _ = xs.shape
    patches_s += -patches_s % 64
    token = w1_l.shape[1]
    half = width // 2
    per_l, per_s = count_l * 2 // size, count_s // size
    vmem = pl.BlockSpec(memory_space=pltpu.VMEM)
    V = pltpu.VMEM
    DMA = pltpu.SemaphoreType.DMA
    low = lambda *shape: jax.ShapeDtypeStruct(shape, BF)
    return pl.pallas_call(
        functools.partial(token_kernel, near, size),
        out_shape=(
            jax.ShapeDtypeStruct((rows, width), F32),
            low(per_l, size * patches_l, half), low(per_s, size * patches_s, width),
            low(per_l, token, half), low(per_s, token, width),
            low(per_l, token, half), low(per_s, token, width),
            low(2, size * patches_l, token), low(2, size * patches_s, token),
        ),
        in_specs=[vmem] * 12,
        out_specs=(ANY,) + (vmem,) * 8,
        scratch_shapes=[
            V((2, patches_l, token), BF), V((2, patches_s, token), BF),
            V((count_l * 2, patches_l, half), BF), V((count_s, patches_s, width), BF),
            V((token, size * patches_l), BF), V((token, size * patches_s), BF),
            V((per_l, size * patches_l, half), BF), V((per_s, size * patches_s, width), BF),
            V((count_l * 2, patches_l, half), BF), V((count_s, patches_s, width), BF),
            V((rows, width), F32),
            DMA((1,)), DMA((1,)), DMA((2,)), DMA((3, 2)), DMA((3, 2)),
            DMA((count_l * 2,)), DMA((count_s,)), DMA((per_l, size)), DMA((per_s, size)),
            DMA((per_l, size)), DMA((per_s, size)), DMA((count_l * 2,)), DMA((count_s,)),
        ],
        compiler_params=pltpu.CompilerParams(
            collective_id=2, has_side_effects=True, vmem_limit_bytes=TOP
        ),
    )(xl, xs, w1_l, w1_s, w2_l, w2_s, b1_l, b1_s, b2_l, b2_s, gain, bias)


GROUPS = 12
DEPTH = 3
SLAB = 512


def backward_kernel(
    near, far, size, far_inside,
    chunk_hbm, ey_hbm, xl, xs, u_l, u_s, h_l, h_s, sl_l, sl_s, w_l, w_s, small_in, gain_ref,
    full_hbm, gx_hbm, tok_out, vec_out, gx_s,
    ey, tx_l, tx_s, e_l, e_s, w2_l, w2_s, ep_l, ep_s, eu_l, eu_s, rx_l, rx_s,
    grads, tok_tx, tok_rx, tokx_tx, tokx_rx, tok_sum, tokn_tx, tokn_rx, tok_half, tokf_tx, tokf_rx,
    vec, vec_rx, vecn_rx, vecf_rx,
    ey_sem, gx_sem,
    own_sem, gx_ss, gx_rs, gf_ss, gf_rs, gn_ss, gn_rs, gc_ss, gc_rs,
    out_ss_l, out_ss_s, out_rs_l, out_rs_s, bk_ss_l, bk_ss_s, bk_rs_l, bk_rs_s,
    tc_ss, tc_rs, tx_ss, tx_rs, tn_ss, tn_rs, tf_ss, tf_rs, taf_ss, taf_rs, tan_ss, tan_rs,
    v_ss, v_rs, vn_ss, vn_rs, vf_ss, vf_rs,
):
    peers = Peers(near)
    me = peers.blk
    count_l, patches_l, width = xl.shape
    count_s, real_s, _ = xs.shape
    patches_s = tx_s.shape[1]
    token = w_l.shape[2]
    gain = row(gain_ref)
    half = width // 2
    per_l, per_s = count_l * 2 // size, count_s // size
    swap = Swap(peers, size, per_l, per_s, patches_l, patches_s)
    small_rows = count_s * patches_s
    x_peer = peers.at("x", 1 - peers.x)
    core_peer = peers.at("core", 1 - peers.core)

    def send(src, dst, ss, rs, device):
        return pltpu.make_async_remote_copy(
            src_ref=src, dst_ref=dst, send_sem=ss, recv_sem=rs, device_id=device, device_id_type=MESH
        )

    def others(axis, count):
        return [(j, peers.at(axis, lax.rem(peers.mine(axis) + j, count))) for j in range(1, count)]

    near_peers = others("near", near)
    far_peers = others("far", far)

    each, hidden = chunk_hbm.shape
    f = far if far_inside else 1
    f_place = peers.far if far_inside else 0
    cols = hidden // GROUPS
    base_n = peers.near * (each * 2 * f)
    base_f = base_n + f_place * (each * 2)
    base_x = base_f + peers.x * each

    def block(start, rows, k):
        return full_hbm.at[peers.core, pl.ds(pl.multiple_of(start, each), rows), pl.ds(k * cols, cols)]

    def g_own(k):
        return pltpu.make_async_copy(chunk_hbm.at[:, pl.ds(k * cols, cols)], block(base_x, each, k), own_sem.at[k])

    def g_x(k):
        return send(chunk_hbm.at[:, pl.ds(k * cols, cols)], block(base_x, each, k), gx_ss.at[k], gx_rs.at[k], x_peer)

    def g_far(k):
        span = block(base_f, each * 2, k)
        return [
            send(span, span, gf_ss.at[k, j - 1], gf_rs.at[k, j - 1], there) for j, there in far_peers
        ] if far_inside else []

    def g_near(k):
        span = block(base_n, each * 2 * f, k)
        return [send(span, span, gn_ss.at[k, j - 1], gn_rs.at[k, j - 1], there) for j, there in near_peers]

    def g_core(k):
        span = block(0, each * 2 * f * near, k)
        return send(span, span, gc_ss.at[k], gc_rs.at[k], core_peer)

    def g_open(k):
        if k < GROUPS:
            g_own(k).wait()
            g_x(k).wait_recv()
            for copy in g_far(k):
                copy.start()

    def g_close(k):
        for copy in g_near(k):
            copy.wait_recv()
        g_core(k).start()

    def tick(k):
        for copy in g_far(k):
            copy.wait_recv()
        for copy in g_near(k):
            copy.start()
        g_open(k + DEPTH)
        if k >= 1:
            g_close(k - 1)

    ey_in = pltpu.make_async_copy(ey_hbm, ey, ey_sem.at[0])
    ey_in.start()
    greet_all(peers, size, near, far)
    for k in range(GROUPS):
        g_x(k).start()
        g_own(k).start()
    ey_in.wait()
    vec[...] = jnp.zeros_like(vec)
    vec[0:8, :] = small_in[...]
    ones = jnp.ones((8, width), BF)

    def cast_l(n, total):
        at = pl.ds(pl.multiple_of(small_rows + n * patches_l, 16), patches_l)
        et = ey[at, :].astype(BF)
        tx_l[2 * n] = et[:, :half]
        tx_l[2 * n + 1] = et[:, half:]
        return total + matmul_nt(ones, et)

    def cast_s(n, total):
        at = pl.ds(pl.multiple_of(n * patches_s, 16), patches_s)
        et = ey[at, :].astype(BF)
        tx_s[n] = et
        return total + matmul_nt(ones, et)

    total_l = lax.fori_loop(0, count_l, cast_l, jnp.zeros((8, patches_l), F32))
    for j in range(per_l):
        for k in range(1, size):
            swap.out("l", j, swap.other(k), me, tx_l, e_l, out_ss_l, out_rs_l).start()
    total_s = lax.fori_loop(0, count_s, cast_s, jnp.zeros((8, patches_s), F32))
    for j in range(per_s):
        for k in range(1, size):
            swap.out("s", j, swap.other(k), me, tx_s, e_s, out_ss_s, out_rs_s).start()
    vec[16:24, 0:patches_l] = total_l
    vec[16:24, half:half + patches_s] = total_s
    for j in range(per_l):
        e_l[j, swap.rows(me, patches_l)] = tx_l[me * per_l + j]
    for j in range(per_s):
        e_s[j, swap.rows(me, patches_s)] = tx_s[me * per_s + j]
    w2_l[...] = w_l[1].T
    w2_s[...] = w_s[1].T
    for k in range(DEPTH):
        g_open(k)

    def unmix(kind, j, e, w2, w1, slope, ep, eu, outs, tx, rx, bss, brs):
        for k in range(1, size):
            swap.out(kind, j, me, swap.other(k), tx, e, *outs).wait_recv()
        low = (matmul(w2[...], e[j]) * slope[j].astype(F32)).astype(BF)
        ep[j] = low
        eu[j] = matmul(w1, low).astype(BF)
        for k in range(1, size):
            swap.back(kind, j, me, swap.other(k), eu, rx, bss, brs).start()
        patches, per = (patches_l, per_l) if kind == "l" else (patches_s, per_s)
        rx[me * per + j] = eu[j, swap.rows(me, patches)]

    for j in range(per_l):
        unmix("l", j, e_l, w2_l, w_l[0], sl_l, ep_l, eu_l, (out_ss_l, out_rs_l), tx_l, rx_l, bk_ss_l, bk_rs_l)
        tick(j)
    for j in range(per_s):
        unmix("s", j, e_s, w2_s, w_s[0], sl_s, ep_s, eu_s, (out_ss_s, out_rs_s), tx_s, rx_s, bk_ss_s, bk_rs_s)
    tick(3)

    ones_l = jnp.ones((8, half), BF)
    vec[8:16, 0:half] = sum(matmul_nt(ones_l, ep_l[j]) for j in range(per_l))
    ones_s = jnp.ones((8, width), BF)
    vec[8:16, half:width] = sum(matmul_nt(ones_s, ep_s[j]) for j in range(per_s))
    top = 2 * patches_l + 2 * patches_s
    if SLAB > top:
        grads[:, top:SLAB, :] = jnp.zeros((size, SLAB - top, token), F32)
    begin = 0
    for left, right, per, patches in (
        (u_l, ep_l, per_l, patches_l), (e_l, h_l, per_l, patches_l),
        (u_s, ep_s, per_s, patches_s), (e_s, h_s, per_s, patches_s),
    ):
        value = sum(matmul_nt(left[j], right[j]) for j in range(per))
        for q in range(size):
            grads[q, begin:begin + patches] = value[q * patches:(q + 1) * patches]
        begin += patches
    for p in range(2):
        tok_tx[p] = grads[p * 2 + 1 - peers.core].astype(BF)
    t_core = send(tok_tx, tok_rx, tc_ss.at[0], tc_rs.at[0], core_peer)
    t_core.start()
    tick(4)
    t_core.wait_recv()
    there = 1 - peers.x
    tokx_tx[...] = (grads[there * 2 + peers.core] + tok_rx[there].astype(F32)).astype(BF)
    t_x = send(tokx_tx, tokx_rx, tx_ss.at[0], tx_rs.at[0], x_peer)
    t_x.start()
    tok_sum[...] = grads[me] + tok_rx[peers.x].astype(F32)
    tick(5)
    tick(6)

    def arrived(kind, unit, eu, rx, bss, brs):
        per = per_l if kind == "l" else per_s
        owner = unit // per

        @pl.when(owner != me)
        def _():
            swap.back(kind, unit - owner * per, owner, me, eu, rx, bss, brs).wait_recv()

    def norm_back(x, eu, at):
        unit, scale = unit_rows(x.astype(F32))
        d = eu * gain
        m1 = jnp.mean(d, axis=-1, keepdims=True)
        m2 = jnp.mean(d * unit, axis=-1, keepdims=True)
        vec[7:8, :] += jnp.sum(eu * unit, axis=0, keepdims=True)
        vec[9:10, :] += jnp.sum(eu, axis=0, keepdims=True)
        return ey[at, :] + scale * (d - m1 - unit * m2)

    def gx_copy(n):
        at = pl.ds(pl.multiple_of(small_rows + n * patches_l, 16), patches_l)
        return pltpu.make_async_copy(ey.at[at], gx_hbm.at[n], gx_sem.at[n])

    def home_l(n, carry):
        arrived("l", 2 * n, eu_l, rx_l, bk_ss_l, bk_rs_l)
        arrived("l", 2 * n + 1, eu_l, rx_l, bk_ss_l, bk_rs_l)
        at = pl.ds(pl.multiple_of(small_rows + n * patches_l, 16), patches_l)
        eu = jnp.concatenate([rx_l[2 * n], rx_l[2 * n + 1]], axis=1).astype(F32)
        ey[at, :] = norm_back(xl[n], eu, at)
        gx_copy(n).start()
        return carry

    def home_s(n, carry):
        arrived("s", n, eu_s, rx_s, bk_ss_s, bk_rs_s)
        at = pl.ds(pl.multiple_of(n * patches_s, 16), real_s)
        gx_s[n] = norm_back(xs[n], rx_s[n, :real_s].astype(F32), at)
        return carry

    vec[9:10, :] = jnp.zeros((1, width), F32)
    lax.fori_loop(0, count_l // 2, home_l, 0)
    tick(7)
    lax.fori_loop(count_l // 2, count_l, home_l, 0)
    tick(8)
    lax.fori_loop(0, count_s, home_s, 0)

    both = vec.at[0:16]
    v_core = send(both, vec_rx.at[0], v_ss.at[0], v_rs.at[0], core_peer)
    v_core.start()
    t_x.wait_recv()
    tok_sum[...] += tokx_rx[...].astype(F32)
    part_n = SLAB // near
    part_f = part_n // far
    t_near, t_far, ta_far, ta_near = [], [], [], []
    if far_inside:
        for j, device in near_peers:
            at = pl.ds(pl.multiple_of(lax.rem(peers.near + j, near) * part_n, part_n), part_n)
            tokn_tx[j - 1] = tok_sum[at, :].astype(BF)
            copy = send(tokn_tx.at[j - 1], tokn_rx.at[j - 1], tn_ss.at[j - 1], tn_rs.at[j - 1], device)
            copy.start()
            t_near.append(copy)
    else:
        tok_out[...] = tok_sum[...].astype(BF)
    v_core.wait()
    vec[0:16, :] += vec_rx[0]
    v_x = send(both, vec_rx.at[1], v_ss.at[1], v_rs.at[1], x_peer)
    v_x.start()
    tick(9)
    v_x.wait()
    vec[0:16, :] += vec_rx[1]
    v_near = [send(vec, vecn_rx.at[j - 1], vn_ss.at[j - 1], vn_rs.at[j - 1], device) for j, device in near_peers]
    for copy in v_near:
        copy.start()
    if far_inside:
        for copy in t_near:
            copy.wait_recv()
        mine = pl.ds(pl.multiple_of(peers.near * part_n, part_n), part_n)
        tok_half[...] = tok_sum[mine, :]
        for j in range(near - 1):
            tok_half[...] += tokn_rx[j].astype(F32)
        for j, device in far_peers:
            at = pl.ds(pl.multiple_of(lax.rem(peers.far + j, far) * part_f, part_f), part_f)
            tokf_tx[j - 1] = tok_half[at, :].astype(BF)
            copy = send(tokf_tx.at[j - 1], tokf_rx.at[j - 1], tf_ss.at[j - 1], tf_rs.at[j - 1], device)
            copy.start()
            t_far.append(copy)
    tick(10)
    for copy in v_near:
        copy.wait()
    for j in range(near - 1):
        vec[...] += vecn_rx[j]
    v_far = [send(vec, vecf_rx.at[j - 1], vf_ss.at[j - 1], vf_rs.at[j - 1], device) for j, device in far_peers]
    for copy in v_far:
        copy.start()
    if far_inside:
        for copy in t_far:
            copy.wait_recv()
        value = tok_half[pl.ds(pl.multiple_of(peers.far * part_f, part_f), part_f), :]
        for j in range(far - 1):
            value = value + tokf_rx[j].astype(F32)
        span = tok_out.at[pl.ds(pl.multiple_of(peers.near * part_n + peers.far * part_f, part_f), part_f)]
        span[...] = value.astype(BF)
        for j, device in far_peers:
            copy = send(span, span, taf_ss.at[j - 1], taf_rs.at[j - 1], device)
            copy.start()
            ta_far.append(copy)
    tick(11)
    for copy in v_far:
        copy.wait()
    value = vec[...]
    for j in range(far - 1):
        value = value + vecf_rx[j]
    vec_out[...] = value
    if far_inside:
        for copy in ta_far:
            copy.wait_recv()
        span = tok_out.at[pl.ds(pl.multiple_of(peers.near * part_n, part_n), part_n)]
        for j, device in near_peers:
            copy = send(span, span, tan_ss.at[j - 1], tan_rs.at[j - 1], device)
            copy.start()
            ta_near.append(copy)
    g_close(GROUPS - 1)
    for copy in ta_near:
        copy.wait_recv()

    for copy in [t_core, t_x] + t_near + t_far + ta_far + ta_near:
        copy.wait_send()
    for k in range(1, size):
        there = swap.other(k)
        for j in range(per_l):
            swap.out("l", j, there, me, tx_l, e_l, out_ss_l, out_rs_l).wait_send()
            swap.back("l", j, me, there, eu_l, rx_l, bk_ss_l, bk_rs_l).wait_send()
        for j in range(per_s):
            swap.out("s", j, there, me, tx_s, e_s, out_ss_s, out_rs_s).wait_send()
            swap.back("s", j, me, there, eu_s, rx_s, bk_ss_s, bk_rs_s).wait_send()
    for k in range(GROUPS):
        g_x(k).wait_send()
        for copy in g_far(k) + g_near(k):
            copy.wait_send()
        g_core(k).wait()
    for n in range(count_l):
        gx_copy(n).wait()


def backward(chunk, ey, xl, xs, saved, small, gain):
    size = lax.axis_size("blk")
    near, far = img_split(lax.axis_size("img"))
    rows, width = ey.shape
    far_inside = width % (near * far * 2 * 16) == 0
    u_l, u_s, h_l, h_s, sl_l, sl_s, w_l, w_s = saved
    count_l, patches_l, _ = xl.shape
    count_s, patches_s, _ = xs.shape
    patches_s += -patches_s % 64
    token = w_l.shape[2]
    half = width // 2
    per_l, per_s = u_l.shape[0], u_s.shape[0]
    each, hidden = chunk.shape
    vmem = pl.BlockSpec(memory_space=pltpu.VMEM)
    V = pltpu.VMEM
    DMA = pltpu.SemaphoreType.DMA
    n1, f1 = near - 1, far - 1
    part_n = SLAB // near
    part_f = max(part_n // far, 16)
    return pl.pallas_call(
        functools.partial(backward_kernel, near, far, size, far_inside),
        out_shape=(
            jax.ShapeDtypeStruct((2, width, hidden), BF),
            jax.ShapeDtypeStruct(xl.shape, F32),
            jax.ShapeDtypeStruct((SLAB, token), BF),
            jax.ShapeDtypeStruct((24, width), F32),
            jax.ShapeDtypeStruct(xs.shape, F32),
        ),
        in_specs=[ANY, ANY] + [vmem] * 12,
        out_specs=(ANY, ANY, vmem, vmem, vmem),
        scratch_shapes=[
            V((rows, width), F32),
            V((count_l * 2, patches_l, half), BF), V((count_s, patches_s, width), BF),
            V(u_l.shape, BF), V(u_s.shape, BF),
            V((token, size * patches_l), BF), V((token, size * patches_s), BF),
            V(h_l.shape, BF), V(h_s.shape, BF), V(u_l.shape, BF), V(u_s.shape, BF),
            V((count_l * 2, patches_l, half), BF), V((count_s, patches_s, width), BF),
            V((size, SLAB, token), F32), V((2, SLAB, token), BF), V((2, SLAB, token), BF),
            V((SLAB, token), BF), V((SLAB, token), BF), V((SLAB, token), F32),
            V((n1, part_n, token), BF), V((n1, part_n, token), BF), V((part_n, token), F32),
            V((f1, part_f, token), BF), V((f1, part_f, token), BF),
            V((24, width), F32), V((2, 16, width), F32), V((n1, 24, width), F32), V((f1, 24, width), F32),
            DMA((1,)), DMA((count_l,)),
            DMA((GROUPS,)), DMA((GROUPS,)), DMA((GROUPS,)), DMA((GROUPS, f1)), DMA((GROUPS, f1)),
            DMA((GROUPS, n1)), DMA((GROUPS, n1)), DMA((GROUPS,)), DMA((GROUPS,)),
            DMA((count_l * 2,)), DMA((count_s,)), DMA((per_l, size)), DMA((per_s, size)),
            DMA((per_l, size)), DMA((per_s, size)), DMA((count_l * 2,)), DMA((count_s,)),
            DMA((1,)), DMA((1,)), DMA((1,)), DMA((1,)), DMA((n1,)), DMA((n1,)), DMA((f1,)), DMA((f1,)),
            DMA((f1,)), DMA((f1,)), DMA((n1,)), DMA((n1,)),
            DMA((2,)), DMA((2,)), DMA((n1,)), DMA((n1,)), DMA((f1,)), DMA((f1,)),
        ],
        compiler_params=pltpu.CompilerParams(
            collective_id=1, has_side_effects=True, vmem_limit_bytes=TOP
        ),
    )(chunk, ey, xl, xs, u_l, u_s, h_l, h_s, sl_l, sl_s, w_l, w_s, small, gain)


def widen_kernel(
    first, second, tok, vec,
    out_first, out_second, gain1, bias1, w1_s, b1_s, w2_s, b2_s, w1_l, b1_l, w2_l, b2_l, gain2, bias2, b1, b2,
):
    out_first[...] = first[0].astype(F32)
    out_second[...] = second[0].astype(F32).T

    @pl.when(pl.program_id(0) == 0)
    def _():
        width = vec.shape[1]
        half = width // 2
        large, small = w1_l.shape[0], w1_s.shape[0]
        wide = small + -small % 64
        at = 2 * large
        w1_l[...] = tok[0:large, :].astype(F32)
        w2_l[...] = tok[large:at, :].astype(F32).T
        w1_s[...] = tok[at:at + wide, :].astype(F32)[:small]
        w2_s[...] = tok[at + wide:at + 2 * wide, :].astype(F32).T[:, :small]
        gain1[...] = vec[7, :]
        bias1[...] = vec[9, :]
        b1_l[...] = vec[8, 0:half]
        b1_s[...] = vec[8, half:width]
        b2_l[...] = vec[16, 0:large]
        b2_s[...] = vec[16, half:half + small]
        gain2[...] = vec[5, :]
        bias2[...] = vec[6, :]
        for k in range(b1.shape[0] // width):
            b1[k * width:(k + 1) * width] = vec[k, :]
        b2[...] = vec[4, :]


def widen(full, tok, vec, patches_s, patches_l):
    _, width, hidden = full.shape
    token = tok.shape[1]
    step = 384
    shapes = (
        (width,), (width,), (patches_s, token), (token,), (token, patches_s), (patches_s,),
        (patches_l, token), (token,), (token, patches_l), (patches_l,), (width,), (width,), (hidden,), (width,),
    )

    def whole(shape):
        return pl.BlockSpec(shape, lambda i: (0,) * len(shape))

    return pl.pallas_call(
        widen_kernel,
        grid=(hidden // step,),
        out_shape=(
            jax.ShapeDtypeStruct((width, hidden), F32), jax.ShapeDtypeStruct((hidden, width), F32),
        ) + tuple(jax.ShapeDtypeStruct(shape, F32) for shape in shapes),
        in_specs=[
            pl.BlockSpec((1, width, step), lambda i: (0, 0, i)),
            pl.BlockSpec((1, width, step), lambda i: (1, 0, i)),
            whole(tok.shape), whole(vec.shape),
        ],
        out_specs=(
            pl.BlockSpec((width, step), lambda i: (0, i)), pl.BlockSpec((step, width), lambda i: (i, 0)),
        ) + tuple(whole(shape) for shape in shapes),
        compiler_params=pltpu.CompilerParams(vmem_limit_bytes=TOP),
    )(full, full, tok, vec)


def local(
    x_small, x_large, live_counts, ln1_gain, ln1_bias,
    tok_w1_small, tok_b1_small, tok_w2_small, tok_b2_small,
    tok_w1_large, tok_b1_large, tok_w2_large, tok_b2_large,
    ln2_gain, ln2_bias, ch_w1, ch_b1, ch_w2, ch_b2, cot_small, cot_large,
):
    width = x_small.shape[2]
    patches_s, patches_l = x_small.shape[1], x_large.shape[1]
    rows = x_small.shape[0] * (patches_s + -patches_s % 64) + x_large.shape[0] * patches_l
    y, *saved = token_forward(
        x_large, x_small, tok_w1_large, tok_w1_small, tok_w2_large, tok_w2_small,
        tok_b1_large, tok_b1_small, tok_b2_large, tok_b2_small, ln1_gain, ln1_bias, rows + -rows % (3 * LANES),
    )
    out_large, ey, chunk, small_grads, out_small = channel(
        y, live_counts, cot_large, cot_small, ch_w1, ch_w2, ch_b1, ln2_gain, ln2_bias, ch_b2
    )
    near, far = img_split(lax.axis_size("img"))
    far_inside = width % (near * far * 2 * 16) == 0
    if not far_inside:
        same = [[a * near + b for a in range(far)] for b in range(near)]
        chunk = lax.psum(chunk.astype(F32), "img", axis_index_groups=same).astype(BF)
    full, gx_large, tok, vec, gx_small = backward(
        chunk, ey, x_large, x_small, saved, small_grads, ln1_gain
    )
    if not far_inside:
        tok = lax.psum(tok.astype(F32), "img")
    (
        grad_ch_w1, grad_ch_w2, gain1, bias1, w1_s, b1_s, w2_s, b2_s, w1_l, b1_l, w2_l, b2_l,
        gain2, bias2, grad_b1, grad_b2,
    ) = widen(full, tok, vec, patches_s, patches_l)
    return (
        out_small, out_large, gx_small, gx_large, gain1, bias1,
        w1_s, b1_s, w2_s, b2_s, w1_l, b1_l, w2_l, b2_l,
        gain2, bias2, grad_ch_w1, grad_b1, grad_ch_w2, grad_b2,
    )


def solution(mesh):
    image = P("img", "blk", None)
    whole = P()
    rows = P("blk", None)
    columns = P(None, "blk")
    vector = P("blk")
    in_specs = (
        image, image, P("img", None), whole, whole,
        rows, whole, columns, vector, rows, whole, columns, vector,
        whole, whole, whole, whole, whole, whole, image, image,
    )
    out_specs = (
        image, image, image, image, whole, whole,
        rows, whole, columns, vector, rows, whole, columns, vector,
        whole, whole, whole, whole, whole, whole,
    )
    return jax.shard_map(local, mesh=mesh, in_specs=in_specs, out_specs=out_specs, check_vma=False)
```

```python
import functools

import jax
import jax.numpy as jnp
from jax import lax
from jax.experimental import pallas as pl
from jax.experimental.pallas import tpu as pltpu
from jax.sharding import PartitionSpec as P

EPSILON = 1e-06
LANES = 128
BF = jnp.bfloat16
F32 = jnp.float32


MESH = pl.DeviceIdType.MESH
ANY = pl.BlockSpec(memory_space=pl.ANY)
TILE = 256
LAGS = (1, 3, 5, 7)
TOP = 62 * 1024 * 1024


def img_split(size):
    near = 2 if size <= 8 else 8
    return near, size // near


def gelu_pair(a):
    square = a * a
    slope = 0.7978845608028654
    t = jnp.tanh(a * (slope + (slope * 0.044715) * square))
    half = 0.5 + 0.5 * t
    inner = slope + (3.0 * slope * 0.044715) * square
    return a * half, half + (0.5 * a) * (1.0 - t * t) * inner


class Peers:
    def __init__(self, near_count):
        self.img = lax.axis_index("img")
        self.blk = lax.axis_index("blk")
        self.core = lax.rem(self.blk, 2)
        self.x = self.blk // 2
        self.near_count = near_count
        self.near = lax.rem(self.img, near_count)
        self.far = self.img // near_count

    def at(self, axis, place):
        if axis == "core":
            return (self.img, self.x * 2 + place)
        if axis == "x":
            return (self.img, place * 2 + self.core)
        if axis == "near":
            return (self.far * self.near_count + place, self.blk)
        return (place * self.near_count + self.near, self.blk)

    def mine(self, axis):
        return {"core": self.core, "x": self.x, "near": self.near, "far": self.far}[axis]


def greet(peers, axes):
    barrier = pltpu.get_barrier_semaphore()
    total = 0
    for axis, count in axes:
        for j in range(1, count):
            there = lax.rem(peers.mine(axis) + j, count)
            pl.semaphore_signal(barrier, inc=1, device_id=peers.at(axis, there), device_id_type=MESH)
            total += 1
    pl.semaphore_wait(barrier, total)


class Gather:
    def __init__(self, peers, near, far, far_inside, chunk, full, sems):
        self.peers, self.near, self.far, self.far_inside = peers, near, far, far_inside
        self.chunk, self.full = chunk, full
        self.each = each = chunk.shape[1]
        self.f = far if far_inside else 1
        self.own_sem, self.x_ss, self.x_rs, self.f_ss, self.f_rs, self.n_ss, self.n_rs, self.c_ss, self.c_rs = sems
        self.base_n = peers.near * (each * 2 * self.f)
        self.base_f = self.base_n + (peers.far if far_inside else 0) * (each * 2)
        self.base_x = self.base_f + peers.x * each

    def block(self, start, rows, k):
        return self.full.at[self.peers.core, k, pl.ds(pl.multiple_of(start, self.each), rows)]

    def send(self, src, dst, ss, rs, device):
        return pltpu.make_async_remote_copy(
            src_ref=src, dst_ref=dst, send_sem=ss, recv_sem=rs, device_id=device, device_id_type=MESH
        )

    def own(self, k):
        return pltpu.make_async_copy(self.chunk.at[k], self.block(self.base_x, self.each, k), self.own_sem.at[k])

    def to_x(self, k):
        there = self.peers.at("x", 1 - self.peers.x)
        return self.send(
            self.chunk.at[k], self.block(self.base_x, self.each, k), self.x_ss.at[k], self.x_rs.at[k], there
        )

    def spread(self, axis, count, span, ss, rs, k):
        copies = []
        for j in range(1, count):
            there = self.peers.at(axis, lax.rem(self.peers.mine(axis) + j, count))
            copies.append(self.send(span, span, ss.at[k, j - 1], rs.at[k, j - 1], there))
        return copies

    def to_far(self, k):
        return self.spread("far", self.f, self.block(self.base_f, self.each * 2, k), self.f_ss, self.f_rs, k)

    def to_near(self, k):
        return self.spread(
            "near", self.near, self.block(self.base_n, self.each * 2 * self.f, k), self.n_ss, self.n_rs, k
        )

    def to_core(self, k):
        span = self.block(0, self.each * 2 * self.f * self.near, k)
        return self.send(span, span, self.c_ss.at[k], self.c_rs.at[k], self.peers.at("core", 1 - self.peers.core))

    def first(self, k):
        self.to_x(k).start()
        self.own(k).start()

    def second(self, k, begun):
        if not begun:
            self.own(k).wait()
            self.to_x(k).wait_recv()
        for copy in self.to_far(k):
            copy.start()

    def third(self, k):
        for copy in self.to_far(k):
            copy.wait_recv()
        for copy in self.to_near(k):
            copy.start()

    def fourth(self, k):
        for copy in self.to_near(k):
            copy.wait_recv()
        self.to_core(k).start()

    def drain(self, k, begun):
        if not begun:
            self.to_x(k).wait_send()
        for copy in self.to_far(k) + self.to_near(k):
            copy.wait_send()
        self.to_core(k).wait()

    @staticmethod
    def sems(groups, near, far):
        DMA = pltpu.SemaphoreType.DMA
        n1, f1 = near - 1, max(far - 1, 1)
        return [DMA((groups,))] * 3 + [DMA((groups, f1))] * 2 + [DMA((groups, n1))] * 2 + [DMA((groups,))] * 2


def row(ref):
    return ref[...].reshape(1, -1)


def column(ref, rows):
    value = jnp.broadcast_to(ref[...].reshape(1, -1), (8, ref.shape[0])).T[:, :1]
    return value if rows == ref.shape[0] else jnp.concatenate([value, jnp.zeros((rows - ref.shape[0], 1), F32)])


def channel_kernel(
    near, far, far_inside,
    y_hbm, live, cot_l, cot_s, w1_hbm, w2_hbm, b1_ref, gain_ref, bias_ref, b2_ref,
    out_l, ey_hbm, chunk_ref, small_ref, out_s, full_hbm,
    y, ec, v, lt, rt, w1, w2, acc_out, acc_ev, out_low,
    keep, core_tx, core_rx,
    a_keep_n, a_near_tx, a_near_rx, a_keep_f, a_far_tx, a_far_rx, a_keep_x, a_x_tx, a_x_rx,
    b_keep_x, b_x_tx, b_x_rx, b_keep_n, b_near_tx, b_near_rx, b_keep_f, b_far_tx, b_far_rx,
    in_sem, w_sem, out_sem, core_ss, core_rs,
    a_near_ss, a_near_rs, a_far_ss, a_far_rs, a_x_ss, a_x_rs,
    b_near_ss, b_near_rs, b_far_ss, b_far_rs, b_x_ss, b_x_rs, *gather_sems,
):
    rows, width = y.shape
    tiles = w1.shape[0]
    count_l, patches_l, _ = cot_l.shape
    count_s, patches_s, _ = cot_s.shape
    wide_s = patches_s + -patches_s % 64
    small_rows = count_s * wide_s
    peers = Peers(near)
    core = peers.core
    f_place = peers.far if far_inside else 0
    gather = Gather(peers, near, far, far_inside, chunk_ref, full_hbm, gather_sems)
    part = 128
    parts = rows // part
    gain, bias, b2 = row(gain_ref), row(bias_ref), row(b2_ref)

    def w_copies(t):
        return (
            pltpu.make_async_copy(w1_hbm.at[:, pl.ds(t * TILE, TILE)], w1.at[t], w_sem.at[0, t]),
            pltpu.make_async_copy(w2_hbm.at[pl.ds(t * TILE, TILE)], w2.at[t], w_sem.at[1, t]),
        )

    y_in = pltpu.make_async_copy(y_hbm, y, in_sem.at[0])
    y_in.start()

    def start_w(t, carry):
        for copy in w_copies(t):
            copy.start()
        return carry

    lax.fori_loop(0, tiles, start_w, 0)
    axes = [("core", 2), ("near", near)] + ([("far", far)] if far_inside else []) + [("x", 2)]
    greet(peers, axes)
    small_ref[...] = jnp.zeros_like(small_ref)
    used = small_rows + count_l * patches_l
    ec[0:small_rows, :] = jnp.zeros((small_rows, width), BF)
    if rows > used:
        ec[used:rows, :] = jnp.zeros((rows - used, width), BF)

    def live_l(n):
        return jnp.where(n < live[0, 1], 1.0, 0.0).astype(F32)

    def live_s(n):
        return jnp.where(n < live[0, 0], 1.0, 0.0).astype(F32)

    def mask_l(n, carry):
        ec[pl.ds(pl.multiple_of(small_rows + n * patches_l, 16), patches_l), :] = (
            cot_l[n].astype(F32) * live_l(n)
        ).astype(BF)
        return carry

    def mask_s(n, carry):
        ec[pl.ds(pl.multiple_of(n * wide_s, 16), patches_s), :] = (cot_s[n].astype(F32) * live_s(n)).astype(BF)
        return carry

    lax.fori_loop(0, count_l, mask_l, 0)
    lax.fori_loop(0, count_s, mask_s, 0)
    y_in.wait()

    def prepare(p, carry):
        at = pl.ds(pl.multiple_of(p * part, part), part)
        unit, _ = unit_rows(y[at, :])
        low = (unit * gain + bias).astype(BF)
        v[at, :] = low
        lt[0, :, at] = low.T
        own = ec[at, :]
        lt[1, :, at] = own.T
        small_ref[4:5, :] += jnp.sum(own.astype(F32), axis=0, keepdims=True)
        acc_out[at, :] = jnp.zeros((part, width), F32)
        acc_ev[at, :] = jnp.zeros((part, width), F32)
        return carry

    lax.fori_loop(0, parts, prepare, 0)

    def send(src, dst, ss, rs, device):
        return pltpu.make_async_remote_copy(
            src_ref=src, dst_ref=dst, send_sem=ss, recv_sem=rs, device_id=device, device_id_type=MESH
        )

    def core_copy(t):
        slot = lax.rem(t, 2)
        return send(core_tx.at[slot], core_rx.at[t], core_ss.at[slot], core_rs.at[t], peers.at("core", 1 - core))

    def spread(tx, rx, ss, rs, axis, count, i):
        slot = lax.rem(i, 2)
        copies = []
        for j in range(1, count):
            there = lax.rem(peers.mine(axis) + j, count)
            copies.append(
                send(tx.at[slot, j - 1], rx.at[i, j - 1], ss.at[slot, j - 1], rs.at[i, j - 1], peers.at(axis, there))
            )
        return copies

    f = far if far_inside else 1
    a_near = lambda i: spread(a_near_tx, a_near_rx, a_near_ss, a_near_rs, "near", near, i)
    a_far = lambda i: spread(a_far_tx, a_far_rx, a_far_ss, a_far_rs, "far", f, i)
    a_x = lambda i: spread(a_x_tx, a_x_rx, a_x_ss, a_x_rs, "x", 2, i)
    b_near = lambda i: spread(b_near_tx, b_near_rx, b_near_ss, b_near_rs, "near", near, i)
    b_far = lambda i: spread(b_far_tx, b_far_rx, b_far_ss, b_far_rs, "far", f, i)
    b_x = lambda i: spread(b_x_tx, b_x_rx, b_x_ss, b_x_rs, "x", 2, i)
    each = width // near // f // 2

    def tile_step(t):
        for copy in w_copies(t):
            copy.wait()

        @pl.when(t >= 2)
        def _():
            core_copy(t - 2).wait_send()

        slot = lax.rem(t, 2)
        columns = pl.ds(pl.multiple_of(t * TILE, TILE), TILE)
        a = matmul(v[...], w1[t]) + b1_ref[columns].reshape(1, -1)
        gh = matmul_nt(ec[...], w2[t])
        g, slope = gelu_pair(a)
        ea = (slope * gh).astype(BF)
        rt[1] = g.astype(BF)
        rt[0] = ea
        per = width // TILE
        small_ref[lax.div(t, per), pl.ds(pl.multiple_of(lax.rem(t, per) * TILE, TILE), TILE)] = jnp.sum(
            ea.astype(F32), axis=0
        )
        core_tx[slot] = matmul(lt[1 - core], rt[1 - core]).astype(BF).reshape(near, f, 2, each, TILE)
        keep[slot] = matmul(lt[core], rt[core]).reshape(near, f, 2, each, TILE)
        acc_out[...] += matmul(rt[1], w2[t])
        acc_ev[...] += matmul_nt(rt[0], w1[t])
        core_copy(t).start()

    def ey_copy(at, n):
        return pltpu.make_async_copy(acc_ev.at[at], ey_hbm.at[at], out_sem.at[n])

    def at_l(n):
        return pl.ds(pl.multiple_of(small_rows + n * patches_l, 16), patches_l)

    def at_s(n):
        return pl.ds(pl.multiple_of(n * wide_s, 16), wide_s)

    def out_copy(n):
        return pltpu.make_async_copy(out_low.at[n], out_l.at[n], out_sem.at[count_l + count_s + n])

    def finish_rows(at, live_here):
        here = y[at, :]
        result = ((here + acc_out[at, :] + b2) * live_here).astype(BF)
        unit, scale = unit_rows(here)
        ev = acc_ev[at, :]
        small_ref[5:6, :] += jnp.sum(ev * unit, axis=0, keepdims=True)
        small_ref[6:7, :] += jnp.sum(ev, axis=0, keepdims=True)
        d = ev * gain
        m1 = jnp.mean(d, axis=-1, keepdims=True)
        m2 = jnp.mean(d * unit, axis=-1, keepdims=True)
        acc_ev[at, :] = ec[at, :].astype(F32) + scale * (d - m1 - unit * m2)
        return result

    def finish(p):
        def one_l(q, carry):
            n = p + q * 4

            @pl.when(n < count_l)
            def _():
                out_low[n] = finish_rows(at_l(n), live_l(n))
                ey_copy(at_l(n), n).start()
                out_copy(n).start()

            return carry

        def one_s(q, carry):
            n = p + q * 4

            @pl.when(n < count_s)
            def _():
                out_s[n] = finish_rows(at_s(n), live_s(n))[:patches_s]
                ey_copy(at_s(n), count_l + n).start()

            return carry

        lax.fori_loop(0, pl.cdiv(count_l, 4), one_l, 0)
        lax.fori_loop(0, pl.cdiv(count_s, 4), one_s, 0)

    def free(copies, i):
        @pl.when(i >= 2)
        def _():
            for copy in copies(i - 2):
                copy.wait_send()

    def reduce(value, axis, count, place, tx, own, copies, i):
        slot = lax.rem(i, 2)
        free(copies, i)
        made = copies(i)
        for j in range(1, count + 1):
            there = lax.rem(place + j, count)
            piece = value(there)
            if j < count:
                tx[slot, j - 1] = piece.astype(BF)
                made[j - 1].start()
            else:
                own(slot, piece)

    def arrivals(copies, i):
        for copy in copies(i):
            copy.wait_recv()

    def save(ref):
        def put(slot, piece):
            ref[slot] = piece
        return put

    def plus(base, rx, i, count, index):
        value = base
        for k in range(count - 1):
            value = value + rx[(i, k) + index].astype(F32)
        return value

    def chunk_out(t, value):
        chunk_ref[t] = value.astype(BF)
        if far_inside:
            gather.first(t)

    def even_core(t):
        i = lax.div(t, 2)
        core_copy(t).wait_recv()
        reduce(
            lambda p: keep[0, p] + core_rx[t, p].astype(F32),
            "near", near, peers.near, a_near_tx, save(a_keep_n), a_near, i,
        )

    def even_near(t):
        i = lax.div(t, 2)
        slot = lax.rem(i, 2)
        arrivals(a_near, i)
        reduce(
            lambda p: plus(a_keep_n[slot, p], a_near_rx, i, near, (p,)),
            "far", f, f_place, a_far_tx, save(a_keep_f), a_far, i,
        )

    def even_far(t):
        i = lax.div(t, 2)
        slot = lax.rem(i, 2)
        arrivals(a_far, i)
        reduce(
            lambda p: plus(a_keep_f[slot, p], a_far_rx, i, f, (p,)),
            "x", 2, peers.x, a_x_tx, save(a_keep_x), a_x, i,
        )

    def even_x(t):
        i = lax.div(t, 2)
        arrivals(a_x, i)
        chunk_out(t, a_keep_x[lax.rem(i, 2)] + a_x_rx[i, 0].astype(F32))

    def odd_core(t):
        i = lax.div(t, 2)
        core_copy(t).wait_recv()
        reduce(
            lambda p: keep[1, :, :, p] + core_rx[t, :, :, p].astype(F32),
            "x", 2, peers.x, b_x_tx, save(b_keep_x), b_x, i,
        )

    def odd_x(t):
        i = lax.div(t, 2)
        slot = lax.rem(i, 2)
        arrivals(b_x, i)
        reduce(
            lambda p: plus(b_keep_x[slot, p], b_x_rx, i, 2, (p,)),
            "near", near, peers.near, b_near_tx, save(b_keep_n), b_near, i,
        )

    def odd_near(t):
        i = lax.div(t, 2)
        slot = lax.rem(i, 2)
        arrivals(b_near, i)
        reduce(
            lambda p: plus(b_keep_n[slot, p], b_near_rx, i, near, (p,)),
            "far", f, f_place, b_far_tx, save(b_keep_f), b_far, i,
        )

    def odd_far(t):
        i = lax.div(t, 2)
        arrivals(b_far, i)
        slot = lax.rem(i, 2)
        chunk_out(t, plus(b_keep_f[slot], b_far_rx, i, f, ()))

    stages = ((even_core, even_near, even_far, even_x), (odd_core, odd_x, odd_near, odd_far))

    def pair(s2, carry):
        for parity in range(2):
            s = s2 * 2 + parity

            @pl.when(s < tiles)
            def _():
                tile_step(s)

            for place, lag in enumerate(LAGS):
                t = s - lag
                stage = stages[(parity - lag) % 2][place]

                @pl.when((t >= 0) & (t < tiles))
                def _(t=t, stage=stage):
                    stage(t)

            @pl.when((s >= tiles) & (s < tiles + 4))
            def _():
                finish(s - tiles)

        return carry

    lax.fori_loop(0, (tiles + LAGS[-1] + 1) // 2, pair, 0)
    if far_inside:
        for k in range(tiles):
            gather.own(k).wait()
            gather.to_x(k).wait()
    for t in (tiles - 2, tiles - 1):
        core_copy(t).wait_send()
    for copies in (a_near, a_far, a_x, b_near, b_far, b_x):
        for i in (tiles // 2 - 2, tiles // 2 - 1):
            for copy in copies(i):
                copy.wait_send()
    for n in range(count_l):
        ey_copy(at_l(n), n).wait()
        out_copy(n).wait()
    for n in range(count_s):
        ey_copy(at_s(n), count_l + n).wait()


def channel(y, live, cot_l, cot_s, w1, w2, b1, gain, bias, b2):
    rows, width = y.shape
    hidden = w1.shape[1]
    tiles = hidden // TILE
    near, far = img_split(lax.axis_size("img"))
    far_inside = width % (near * far * 2 * 16) == 0
    f = far if far_inside else 1
    chunk = width // near // f // 2
    vmem = pl.BlockSpec(memory_space=pltpu.VMEM)
    V = pltpu.VMEM
    DMA = pltpu.SemaphoreType.DMA
    fm = max(f - 1, 1)
    nm = near - 1
    pairs = tiles // 2
    count = cot_l.shape[0] + cot_s.shape[0]
    return pl.pallas_call(
        functools.partial(channel_kernel, near, far, far_inside),
        out_shape=(
            jax.ShapeDtypeStruct(cot_l.shape, BF),
            jax.ShapeDtypeStruct((rows, width), F32),
            jax.ShapeDtypeStruct((tiles, chunk, TILE), BF),
            jax.ShapeDtypeStruct((8, width), F32),
            jax.ShapeDtypeStruct(cot_s.shape, BF),
            jax.ShapeDtypeStruct((2, tiles, width, TILE), BF),
        ),
        in_specs=[ANY, pl.BlockSpec(memory_space=pltpu.SMEM), vmem, vmem, ANY, ANY] + [vmem] * 4,
        out_specs=(ANY, ANY, vmem, vmem, vmem, ANY),
        scratch_shapes=[
            V((rows, width), F32), V((rows, width), BF), V((rows, width), BF),
            V((2, width, rows), BF), V((2, rows, TILE), BF),
            V((tiles, width, TILE), BF), V((tiles, TILE, width), BF),
            V((rows, width), F32), V((rows, width), F32), V(cot_l.shape, BF),
            V((2, near, f, 2, chunk, TILE), F32), V((2, near, f, 2, chunk, TILE), BF),
            V((tiles, near, f, 2, chunk, TILE), BF),
            V((2, f, 2, chunk, TILE), F32), V((2, nm, f, 2, chunk, TILE), BF), V((pairs, nm, f, 2, chunk, TILE), BF),
            V((2, 2, chunk, TILE), F32), V((2, fm, 2, chunk, TILE), BF), V((pairs, fm, 2, chunk, TILE), BF),
            V((2, chunk, TILE), F32), V((2, 1, chunk, TILE), BF), V((pairs, 1, chunk, TILE), BF),
            V((2, near, f, chunk, TILE), F32), V((2, 1, near, f, chunk, TILE), BF),
            V((pairs, 1, near, f, chunk, TILE), BF),
            V((2, f, chunk, TILE), F32), V((2, nm, f, chunk, TILE), BF), V((pairs, nm, f, chunk, TILE), BF),
            V((2, chunk, TILE), F32), V((2, fm, chunk, TILE), BF), V((pairs, fm, chunk, TILE), BF),
            DMA((1,)), DMA((2, tiles)), DMA((2 * count,)), DMA((2,)), DMA((tiles,)),
            DMA((2, nm)), DMA((pairs, nm)), DMA((2, fm)), DMA((pairs, fm)), DMA((2, 1)), DMA((pairs, 1)),
            DMA((2, nm)), DMA((pairs, nm)), DMA((2, fm)), DMA((pairs, fm)), DMA((2, 1)), DMA((pairs, 1)),
        ] + Gather.sems(tiles, near, f),
        compiler_params=pltpu.CompilerParams(
            collective_id=0, has_side_effects=True, vmem_limit_bytes=TOP
        ),
    )(y, live, cot_l, cot_s, w1, w2, b1, gain, bias, b2)


NT = (((1,), (1,)), ((), ()))


def matmul(left, right):
    return jnp.dot(left, right, preferred_element_type=F32)


def matmul_nt(left, right):
    return lax.dot_general(left, right, NT, preferred_element_type=F32)


class Swap:
    def __init__(self, peers, size, per_l, per_s, patches_l, patches_s):
        self.peers, self.size = peers, size
        self.per_l, self.per_s = per_l, per_s
        self.pl, self.ps = patches_l, patches_s

    def other(self, step):
        return lax.rem(self.peers.blk + step, self.size)

    def copy(self, src, dst, ss, rs, place):
        return pltpu.make_async_remote_copy(
            src_ref=src, dst_ref=dst, send_sem=ss, recv_sem=rs,
            device_id=(self.peers.img, place), device_id_type=MESH,
        )

    def rows(self, place, patches):
        return pl.ds(pl.multiple_of(place * patches, patches), patches)

    def out(self, kind, j, place, source, tx, cols, ss, rs):
        per, patches = (self.per_l, self.pl) if kind == "l" else (self.per_s, self.ps)
        unit = place * per + j
        return self.copy(
            tx.at[unit], cols.at[j, self.rows(source, patches)], ss.at[unit], rs.at[j, source], place
        )

    def back(self, kind, j, owner, place, cols, rx, ss, rs):
        per, patches = (self.per_l, self.pl) if kind == "l" else (self.per_s, self.ps)
        unit = owner * per + j
        return self.copy(
            cols.at[j, self.rows(place, patches)], rx.at[unit], ss.at[j, place], rs.at[unit], place
        )


def greet_all(peers, size, near, far):
    barrier = pltpu.get_barrier_semaphore()
    total = 0
    for j in range(1, size):
        there = lax.rem(peers.blk + j, size)
        pl.semaphore_signal(barrier, inc=1, device_id=(peers.img, there), device_id_type=MESH)
        total += 1
    for axis, count in (("near", near), ("far", far)):
        for j in range(1, count):
            there = lax.rem(peers.mine(axis) + j, count)
            pl.semaphore_signal(barrier, inc=1, device_id=peers.at(axis, there), device_id_type=MESH)
            total += 1
    pl.semaphore_wait(barrier, total)


def unit_rows(row):
    mean = jnp.mean(row, axis=-1, keepdims=True)
    centered = row - mean
    var = jnp.mean(centered * centered, axis=-1, keepdims=True)
    scale = lax.rsqrt(var + EPSILON)
    return centered * scale, scale


def token_kernel(
    near, size,
    xl, xs, w1_l, w1_s, w2_l, w2_s, b1_l_ref, b1_s_ref, b2_l_ref, b2_s_ref, gain_ref, bias_ref,
    y_hbm, u_l, u_s, h_l, h_s, sl_l, sl_s, w_l, w_s,
    wq_l, wq_s, tx_l, tx_s, w1t_l, w1t_s, m_l, m_s, rx_l, rx_s, y,
    y_sem, own_sem, wown, w_ss, w_rs, out_ss_l, out_ss_s, out_rs_l, out_rs_s, bk_ss_l, bk_ss_s, bk_rs_l, bk_rs_s,
):
    peers = Peers(near)
    me = peers.blk
    count_l, patches_l, width = xl.shape
    count_s, real_s, _ = xs.shape
    patches_s = tx_s.shape[1]
    token = w1_l.shape[1]
    half = width // 2
    per_l, per_s = count_l * 2 // size, count_s // size
    swap = Swap(peers, size, per_l, per_s, patches_l, patches_s)
    wq_l[0] = w1_l[...]
    wq_l[1] = w2_l[...]
    wq_s[...] = jnp.zeros_like(wq_s)
    wq_s[0, :real_s] = w1_s[...]
    wq_s[1, :real_s] = w2_s[...]

    barrier = pltpu.get_barrier_semaphore()
    for j in range(1, size):
        pl.semaphore_signal(barrier, inc=1, device_id=(peers.img, swap.other(j)), device_id_type=MESH)
    pl.semaphore_wait(barrier, size - 1)

    def weights(src_l, src_s, quarter, n, place):
        return (
            swap.copy(src_l, w_l.at[:, swap.rows(quarter, patches_l)], w_ss.at[n, 0], w_rs.at[n, 0], place),
            swap.copy(src_s, w_s.at[:, swap.rows(quarter, patches_s)], w_ss.at[n, 1], w_rs.at[n, 1], place),
        )

    x_peer = (1 - peers.x) * 2 + peers.core
    core_peer = peers.x * 2 + 1 - peers.core
    to_x = weights(wq_l, wq_s, me, 0, x_peer)
    to_core = weights(wq_l, wq_s, me, 1, core_peer)
    relay = weights(
        w_l.at[:, swap.rows(x_peer, patches_l)], w_s.at[:, swap.rows(x_peer, patches_s)], x_peer, 2, core_peer
    )
    for copy in to_x + to_core:
        copy.start()
    own_w = (
        pltpu.make_async_copy(wq_l, w_l.at[:, swap.rows(me, patches_l)], wown.at[0]),
        pltpu.make_async_copy(wq_s, w_s.at[:, swap.rows(me, patches_s)], wown.at[1]),
    )
    for copy in own_w:
        copy.start()

    gain, bias = row(gain_ref), row(bias_ref)

    def norm(values):
        unit, _ = unit_rows(values.astype(F32))
        return (unit * gain + bias).astype(BF)

    def norm_l(n, carry):
        u = norm(xl[n])
        tx_l[2 * n] = u[:, :half]
        tx_l[2 * n + 1] = u[:, half:]
        return carry

    tx_s[...] = jnp.zeros_like(tx_s)

    def norm_s(n, carry):
        tx_s[n, :real_s] = norm(xs[n])
        return carry

    lax.fori_loop(0, count_l, norm_l, 0)
    for j in range(per_l):
        for k in range(1, size):
            swap.out("l", j, swap.other(k), me, tx_l, u_l, out_ss_l, out_rs_l).start()
    lax.fori_loop(0, count_s, norm_s, 0)
    for j in range(per_s):
        for k in range(1, size):
            swap.out("s", j, swap.other(k), me, tx_s, u_s, out_ss_s, out_rs_s).start()
    for j in range(per_l):
        u_l[j, swap.rows(me, patches_l)] = tx_l[me * per_l + j]
    for j in range(per_s):
        u_s[j, swap.rows(me, patches_s)] = tx_s[me * per_s + j]

    for copy in to_x:
        copy.wait_recv()
    for copy in relay:
        copy.start()
    for copy in own_w:
        copy.wait()
    for copy in to_core + relay:
        copy.wait_recv()
    b1_l, b1_s = column(b1_l_ref, token), column(b1_s_ref, token)
    b2_l, b2_s = column(b2_l_ref, patches_l), column(b2_s_ref, real_s)
    w1t_l[...] = w_l[0].T
    w1t_s[...] = w_s[0].T

    def mix(kind, j, cols, w1t, w2t, b1, h, slope, m, outs, tx, rx, bss, brs):
        for k in range(1, size):
            source = swap.other(k)
            swap.out(kind, j, me, source, tx, cols, *outs).wait_recv()
        g, d = gelu_pair(matmul(w1t[...], cols[j]) + b1)
        low = g.astype(BF)
        h[j] = low
        slope[j] = d.astype(BF)
        m[j] = matmul(w2t, low).astype(BF)
        for k in range(1, size):
            swap.back(kind, j, me, swap.other(k), m, rx, bss, brs).start()
        patches, per = (patches_l, per_l) if kind == "l" else (patches_s, per_s)
        rx[me * per + j] = m[j, swap.rows(me, patches)]

    for j in range(per_l):
        mix("l", j, u_l, w1t_l, w_l[1], b1_l, h_l, sl_l, m_l, (out_ss_l, out_rs_l), tx_l, rx_l, bk_ss_l, bk_rs_l)
    for j in range(per_s):
        mix("s", j, u_s, w1t_s, w_s[1], b1_s, h_s, sl_s, m_s, (out_ss_s, out_rs_s), tx_s, rx_s, bk_ss_s, bk_rs_s)

    small_rows = count_s * patches_s
    rows = y.shape[0]
    used = small_rows + count_l * patches_l
    y[0:small_rows, :] = jnp.zeros((small_rows, width), F32)
    if rows > used:
        y[used:rows, :] = jnp.zeros((rows - used, width), F32)

    def arrived(kind, unit, m, rx, bss, brs):
        per = per_l if kind == "l" else per_s
        owner = unit // per

        @pl.when(owner != me)
        def _():
            swap.back(kind, unit - owner * per, owner, me, m, rx, bss, brs).wait_recv()

    def home_l(n, carry):
        arrived("l", 2 * n, m_l, rx_l, bk_ss_l, bk_rs_l)
        arrived("l", 2 * n + 1, m_l, rx_l, bk_ss_l, bk_rs_l)
        at = pl.ds(pl.multiple_of(small_rows + n * patches_l, 16), patches_l)
        y[at, :half] = xl[n, :, :half].astype(F32) + rx_l[2 * n].astype(F32) + b2_l
        y[at, half:] = xl[n, :, half:].astype(F32) + rx_l[2 * n + 1].astype(F32) + b2_l
        return carry

    def home_s(n, carry):
        arrived("s", n, m_s, rx_s, bk_ss_s, bk_rs_s)
        at = pl.ds(pl.multiple_of(n * patches_s, 16), real_s)
        y[at, :] = xs[n].astype(F32) + rx_s[n, :real_s].astype(F32) + b2_s
        return carry

    lax.fori_loop(0, count_l, home_l, 0)
    lax.fori_loop(0, count_s, home_s, 0)
    y_out = pltpu.make_async_copy(y, y_hbm, y_sem.at[0])
    y_out.start()
    for copy in to_x + to_core + relay:
        copy.wait_send()
    for k in range(1, size):
        there = swap.other(k)
        for j in range(per_l):
            swap.out("l", j, there, me, tx_l, u_l, out_ss_l, out_rs_l).wait_send()
            swap.back("l", j, me, there, m_l, rx_l, bk_ss_l, bk_rs_l).wait_send()
        for j in range(per_s):
            swap.out("s", j, there, me, tx_s, u_s, out_ss_s, out_rs_s).wait_send()
            swap.back("s", j, me, there, m_s, rx_s, bk_ss_s, bk_rs_s).wait_send()
    y_out.wait()


def token_forward(xl, xs, w1_l, w1_s, w2_l, w2_s, b1_l, b1_s, b2_l, b2_s, gain, bias, rows):
    size = lax.axis_size("blk")
    near, far = img_split(lax.axis_size("img"))
    count_l, patches_l, width = xl.shape
    count_s, patches_s, _ = xs.shape
    patches_s += -patches_s % 64
    token = w1_l.shape[1]
    half = width // 2
    per_l, per_s = count_l * 2 // size, count_s // size
    vmem = pl.BlockSpec(memory_space=pltpu.VMEM)
    V = pltpu.VMEM
    DMA = pltpu.SemaphoreType.DMA
    low = lambda *shape: jax.ShapeDtypeStruct(shape, BF)
    return pl.pallas_call(
        functools.partial(token_kernel, near, size),
        out_shape=(
            jax.ShapeDtypeStruct((rows, width), F32),
            low(per_l, size * patches_l, half), low(per_s, size * patches_s, width),
            low(per_l, token, half), low(per_s, token, width),
            low(per_l, token, half), low(per_s, token, width),
            low(2, size * patches_l, token), low(2, size * patches_s, token),
        ),
        in_specs=[vmem] * 12,
        out_specs=(ANY,) + (vmem,) * 8,
        scratch_shapes=[
            V((2, patches_l, token), BF), V((2, patches_s, token), BF),
            V((count_l * 2, patches_l, half), BF), V((count_s, patches_s, width), BF),
            V((token, size * patches_l), BF), V((token, size * patches_s), BF),
            V((per_l, size * patches_l, half), BF), V((per_s, size * patches_s, width), BF),
            V((count_l * 2, patches_l, half), BF), V((count_s, patches_s, width), BF),
            V((rows, width), F32),
            DMA((1,)), DMA((1,)), DMA((2,)), DMA((3, 2)), DMA((3, 2)),
            DMA((count_l * 2,)), DMA((count_s,)), DMA((per_l, size)), DMA((per_s, size)),
            DMA((per_l, size)), DMA((per_s, size)), DMA((count_l * 2,)), DMA((count_s,)),
        ],
        compiler_params=pltpu.CompilerParams(
            collective_id=2, has_side_effects=True, vmem_limit_bytes=TOP
        ),
    )(xl, xs, w1_l, w1_s, w2_l, w2_s, b1_l, b1_s, b2_l, b2_s, gain, bias)


DEPTH = 3
SLAB = 512


def backward_kernel(
    near, far, size, far_inside,
    chunk_hbm, begun_hbm, ey_hbm,
    xl_in, xs_in, u_l_in, u_s_in, h_l_in, h_s_in, sl_l_in, sl_s_in, w_l_in, w_s_in, small_in, gain_ref,
    full_hbm, gx_hbm, tok_out, vec_out, gx_s,
    xl, xs, u_l, u_s, h_l, h_s, sl_l, sl_s, w_l, w_s, in_sem,
    ey, tx_l, tx_s, e_l, e_s, w2_l, w2_s, ep_l, ep_s, eu_l, eu_s, rx_l, rx_s,
    grads, tok_tx, tok_rx, tok_sum, tokn_tx, tokn_rx, tok_half, tokf_tx, tokf_rx, tokx_tx, tokx_rx,
    vec, vec_rx, vecn_rx, vecf_rx,
    ey_sem, gx_sem,
    out_ss_l, out_ss_s, out_rs_l, out_rs_s, bk_ss_l, bk_ss_s, bk_rs_l, bk_rs_s,
    tc_ss, tc_rs, tx_ss, tx_rs, tn_ss, tn_rs, tf_ss, tf_rs, taf_ss, taf_rs, tan_ss, tan_rs,
    v_ss, v_rs, vn_ss, vn_rs, vf_ss, vf_rs, *gather_sems,
):
    peers = Peers(near)
    me = peers.blk
    count_l, patches_l, width = xl.shape
    count_s, real_s, _ = xs.shape
    patches_s = tx_s.shape[1]
    token = w_l.shape[2]
    gain = row(gain_ref)
    half = width // 2
    per_l, per_s = count_l * 2 // size, count_s // size
    swap = Swap(peers, size, per_l, per_s, patches_l, patches_s)
    small_rows = count_s * patches_s
    x_peer = peers.at("x", 1 - peers.x)
    core_peer = peers.at("core", 1 - peers.core)

    def send(src, dst, ss, rs, device):
        return pltpu.make_async_remote_copy(
            src_ref=src, dst_ref=dst, send_sem=ss, recv_sem=rs, device_id=device, device_id_type=MESH
        )

    def others(axis, count):
        return [(j, peers.at(axis, lax.rem(peers.mine(axis) + j, count))) for j in range(1, count)]

    near_peers = others("near", near)
    far_peers = others("far", far)

    groups = chunk_hbm.shape[0]
    gather = Gather(peers, near, far, far_inside, chunk_hbm, full_hbm, gather_sems)
    waiting = list(range(groups))

    def tick():
        if waiting:
            k = waiting.pop(0)
            gather.third(k)
            if k + DEPTH < groups:
                gather.second(k + DEPTH, far_inside)
            if k > 0:
                gather.fourth(k - 1)

    ey_in = pltpu.make_async_copy(ey_hbm, ey, ey_sem.at[0])
    ey_in.start()
    inputs = [
        pltpu.make_async_copy(src, dst, in_sem.at[n])
        for n, (src, dst) in enumerate((
            (w_l_in, w_l), (w_s_in, w_s), (sl_l_in, sl_l), (sl_s_in, sl_s), (u_l_in, u_l), (u_s_in, u_s),
            (h_l_in, h_l), (h_s_in, h_s), (xl_in, xl), (xs_in, xs),
        ))
    ]
    for copy in inputs:
        copy.start()
    greet_all(peers, size, near, far)
    if not far_inside:
        for k in range(groups):
            gather.first(k)
    for k in range(DEPTH):
        gather.second(k, far_inside)
    ey_in.wait()
    vec[...] = jnp.zeros_like(vec)
    vec[0:8, :] = small_in[...]
    def cast_l(n, carry):
        at = pl.ds(pl.multiple_of(small_rows + n * patches_l, 16), patches_l)
        et = ey[at, :].astype(BF)
        tx_l[2 * n] = et[:, :half]
        tx_l[2 * n + 1] = et[:, half:]
        return carry

    def cast_s(n, carry):
        at = pl.ds(pl.multiple_of(n * patches_s, 16), patches_s)
        tx_s[n] = ey[at, :].astype(BF)
        return carry

    lax.fori_loop(0, count_l, cast_l, 0)
    for j in range(per_l):
        for k in range(1, size):
            swap.out("l", j, swap.other(k), me, tx_l, e_l, out_ss_l, out_rs_l).start()
    lax.fori_loop(0, count_s, cast_s, 0)
    for j in range(per_s):
        for k in range(1, size):
            swap.out("s", j, swap.other(k), me, tx_s, e_s, out_ss_s, out_rs_s).start()
    for j in range(per_l):
        e_l[j, swap.rows(me, patches_l)] = tx_l[me * per_l + j]
    for j in range(per_s):
        e_s[j, swap.rows(me, patches_s)] = tx_s[me * per_s + j]
    for copy in inputs:
        copy.wait()
    w2_l[...] = w_l[1].T
    w2_s[...] = w_s[1].T
    ones_l = jnp.ones((8, half), BF)
    ones_s = jnp.ones((8, width), BF)
    vec[16:24, 0:patches_l] = lax.fori_loop(
        0, 2 * count_l, lambda n, total: total + matmul_nt(ones_l, tx_l[n]), jnp.zeros((8, patches_l), F32)
    )
    vec[16:24, half:half + patches_s] = lax.fori_loop(
        0, count_s, lambda n, total: total + matmul_nt(ones_s, tx_s[n]), jnp.zeros((8, patches_s), F32)
    )

    def unmix(kind, j, e, w2, w1, slope, ep, eu, outs, tx, rx, bss, brs):
        for k in range(1, size):
            swap.out(kind, j, me, swap.other(k), tx, e, *outs).wait_recv()
        low = (matmul(w2[...], e[j]) * slope[j].astype(F32)).astype(BF)
        ep[j] = low
        eu[j] = matmul(w1, low).astype(BF)
        for k in range(1, size):
            swap.back(kind, j, me, swap.other(k), eu, rx, bss, brs).start()
        patches, per = (patches_l, per_l) if kind == "l" else (patches_s, per_s)
        rx[me * per + j] = eu[j, swap.rows(me, patches)]

    for j in range(per_l):
        tick()
        unmix("l", j, e_l, w2_l, w_l[0], sl_l, ep_l, eu_l, (out_ss_l, out_rs_l), tx_l, rx_l, bk_ss_l, bk_rs_l)
    tick()
    for j in range(per_s):
        unmix("s", j, e_s, w2_s, w_s[0], sl_s, ep_s, eu_s, (out_ss_s, out_rs_s), tx_s, rx_s, bk_ss_s, bk_rs_s)

    vec[8:16, 0:half] = sum(matmul_nt(ones_l, ep_l[j]) for j in range(per_l))
    vec[8:16, half:width] = sum(matmul_nt(ones_s, ep_s[j]) for j in range(per_s))
    top = 2 * patches_l + 2 * patches_s
    if SLAB > top:
        grads[:, top:SLAB, :] = jnp.zeros((size, SLAB - top, token), F32)
    begin = 0
    for left, right, per, patches in (
        (u_l, ep_l, per_l, patches_l), (e_l, h_l, per_l, patches_l),
        (u_s, ep_s, per_s, patches_s), (e_s, h_s, per_s, patches_s),
    ):
        value = sum(matmul_nt(left[j], right[j]) for j in range(per))
        for q in range(size):
            grads[q, begin:begin + patches] = value[q * patches:(q + 1) * patches]
        begin += patches
    for p in range(2):
        tok_tx[p] = grads[p * 2 + 1 - peers.core].astype(BF)
    t_core = send(tok_tx, tok_rx, tc_ss.at[0], tc_rs.at[0], core_peer)
    t_core.start()
    tick()
    t_core.wait_recv()
    there = 1 - peers.x
    tokx_tx[...] = (grads[there * 2 + peers.core] + tok_rx[there].astype(F32)).astype(BF)
    t_x = send(tokx_tx, tokx_rx, tx_ss.at[0], tx_rs.at[0], x_peer)
    t_x.start()
    tok_sum[...] = grads[me] + tok_rx[peers.x].astype(F32)
    tick()
    tick()

    def piece(place, size):
        return pl.ds(pl.multiple_of(place * size, size), size)

    def arrived(kind, unit, eu, rx, bss, brs):
        per = per_l if kind == "l" else per_s
        owner = unit // per

        @pl.when(owner != me)
        def _():
            swap.back(kind, unit - owner * per, owner, me, eu, rx, bss, brs).wait_recv()

    def norm_back(x, eu, at):
        unit, scale = unit_rows(x.astype(F32))
        d = eu * gain
        m1 = jnp.mean(d, axis=-1, keepdims=True)
        m2 = jnp.mean(d * unit, axis=-1, keepdims=True)
        vec[7:8, :] += jnp.sum(eu * unit, axis=0, keepdims=True)
        vec[9:10, :] += jnp.sum(eu, axis=0, keepdims=True)
        return ey[at, :] + scale * (d - m1 - unit * m2)

    def gx_copy(n):
        at = pl.ds(pl.multiple_of(small_rows + n * patches_l, 16), patches_l)
        return pltpu.make_async_copy(ey.at[at], gx_hbm.at[n], gx_sem.at[n])

    def home_l(n, carry):
        arrived("l", 2 * n, eu_l, rx_l, bk_ss_l, bk_rs_l)
        arrived("l", 2 * n + 1, eu_l, rx_l, bk_ss_l, bk_rs_l)
        at = pl.ds(pl.multiple_of(small_rows + n * patches_l, 16), patches_l)
        eu = jnp.concatenate([rx_l[2 * n], rx_l[2 * n + 1]], axis=1).astype(F32)
        ey[at, :] = norm_back(xl[n], eu, at)
        gx_copy(n).start()
        return carry

    def home_s(n, carry):
        arrived("s", n, eu_s, rx_s, bk_ss_s, bk_rs_s)
        at = pl.ds(pl.multiple_of(n * patches_s, 16), real_s)
        gx_s[n] = norm_back(xs[n], rx_s[n, :real_s].astype(F32), at)
        return carry

    vec[9:10, :] = jnp.zeros((1, width), F32)
    lax.fori_loop(0, count_l // 2, home_l, 0)
    tick()
    lax.fori_loop(count_l // 2, count_l, home_l, 0)
    lax.fori_loop(0, count_s, home_s, 0)
    both = vec.at[0:16]
    v_core = send(both, vec_rx.at[0], v_ss.at[0], v_rs.at[0], core_peer)
    v_core.start()
    tick()
    t_x.wait_recv()
    tok_sum[...] += tokx_rx[...].astype(F32)
    part_n = SLAB // near
    part_f = part_n // far
    t_near, t_far, ta_far, ta_near = [], [], [], []
    if far_inside:
        for j, device in near_peers:
            tokn_tx[j - 1] = tok_sum[piece(lax.rem(peers.near + j, near), part_n), :].astype(BF)
            copy = send(tokn_tx.at[j - 1], tokn_rx.at[j - 1], tn_ss.at[j - 1], tn_rs.at[j - 1], device)
            copy.start()
            t_near.append(copy)
    else:
        tok_out[...] = tok_sum[...].astype(BF)
    v_core.wait()
    vec[0:16, :] += vec_rx[0]
    v_x = send(both, vec_rx.at[1], v_ss.at[1], v_rs.at[1], x_peer)
    v_x.start()
    tick()
    v_x.wait()
    vec[0:16, :] += vec_rx[1]
    v_near = [send(vec, vecn_rx.at[j - 1], vn_ss.at[j - 1], vn_rs.at[j - 1], device) for j, device in near_peers]
    for copy in v_near:
        copy.start()
    if far_inside:
        for copy in t_near:
            copy.wait_recv()
        tok_half[...] = tok_sum[piece(peers.near, part_n), :]
        for j in range(near - 1):
            tok_half[...] += tokn_rx[j].astype(F32)
        for j, device in far_peers:
            tokf_tx[j - 1] = tok_half[piece(lax.rem(peers.far + j, far), part_f), :].astype(BF)
            copy = send(tokf_tx.at[j - 1], tokf_rx.at[j - 1], tf_ss.at[j - 1], tf_rs.at[j - 1], device)
            copy.start()
            t_far.append(copy)
    tick()
    for copy in v_near:
        copy.wait()
    for j in range(near - 1):
        vec[...] += vecn_rx[j]
    v_far = [send(vec, vecf_rx.at[j - 1], vf_ss.at[j - 1], vf_rs.at[j - 1], device) for j, device in far_peers]
    for copy in v_far:
        copy.start()
    if far_inside:
        for copy in t_far:
            copy.wait_recv()
        value = tok_half[piece(peers.far, part_f), :]
        for j in range(far - 1):
            value = value + tokf_rx[j].astype(F32)
        span = tok_out.at[piece(peers.near * far + peers.far, part_f)]
        span[...] = value.astype(BF)
        for j, device in far_peers:
            copy = send(span, span, taf_ss.at[j - 1], taf_rs.at[j - 1], device)
            copy.start()
            ta_far.append(copy)
    tick()
    for copy in v_far:
        copy.wait()
    value = vec[...]
    for j in range(far - 1):
        value = value + vecf_rx[j]
    vec_out[...] = value
    if far_inside:
        for copy in ta_far:
            copy.wait_recv()
        span = tok_out.at[piece(peers.near, part_n)]
        for j, device in near_peers:
            copy = send(span, span, tan_ss.at[j - 1], tan_rs.at[j - 1], device)
            copy.start()
            ta_near.append(copy)
    while waiting:
        tick()
    gather.fourth(groups - 1)
    for copy in ta_near:
        copy.wait_recv()

    for copy in [t_core, t_x] + t_near + t_far + ta_far + ta_near:
        copy.wait_send()
    for k in range(1, size):
        there = swap.other(k)
        for j in range(per_l):
            swap.out("l", j, there, me, tx_l, e_l, out_ss_l, out_rs_l).wait_send()
            swap.back("l", j, me, there, eu_l, rx_l, bk_ss_l, bk_rs_l).wait_send()
        for j in range(per_s):
            swap.out("s", j, there, me, tx_s, e_s, out_ss_s, out_rs_s).wait_send()
            swap.back("s", j, me, there, eu_s, rx_s, bk_ss_s, bk_rs_s).wait_send()
    for k in range(groups):
        gather.drain(k, far_inside)
    for n in range(count_l):
        gx_copy(n).wait()


def backward(chunk, begun, ey, xl, xs, saved, small, gain):
    size = lax.axis_size("blk")
    near, far = img_split(lax.axis_size("img"))
    rows, width = ey.shape
    far_inside = width % (near * far * 2 * 16) == 0
    u_l, u_s, h_l, h_s, sl_l, sl_s, w_l, w_s = saved
    count_l, patches_l, _ = xl.shape
    count_s, patches_s, _ = xs.shape
    patches_s += -patches_s % 64
    token = w_l.shape[2]
    half = width // 2
    per_l, per_s = u_l.shape[0], u_s.shape[0]
    groups, each, _ = chunk.shape
    vmem = pl.BlockSpec(memory_space=pltpu.VMEM)
    V = pltpu.VMEM
    DMA = pltpu.SemaphoreType.DMA
    n1, f1 = near - 1, far - 1
    part_n = SLAB // near
    part_f = max(part_n // far, 16)
    return pl.pallas_call(
        functools.partial(backward_kernel, near, far, size, far_inside),
        out_shape=(
            jax.ShapeDtypeStruct((2, groups, width, TILE), BF),
            jax.ShapeDtypeStruct(xl.shape, F32),
            jax.ShapeDtypeStruct((SLAB, token), BF),
            jax.ShapeDtypeStruct((24, width), F32),
            jax.ShapeDtypeStruct(xs.shape, F32),
        ),
        in_specs=[ANY] * 13 + [vmem] * 2,
        out_specs=(ANY, ANY, vmem, vmem, vmem),
        scratch_shapes=[
            V(xl.shape, BF), V(xs.shape, BF), V(u_l.shape, BF), V(u_s.shape, BF), V(h_l.shape, BF), V(h_s.shape, BF),
            V(sl_l.shape, BF), V(sl_s.shape, BF), V(w_l.shape, BF), V(w_s.shape, BF), DMA((10,)),
            V((rows, width), F32),
            V((count_l * 2, patches_l, half), BF), V((count_s, patches_s, width), BF),
            V(u_l.shape, BF), V(u_s.shape, BF),
            V((token, size * patches_l), BF), V((token, size * patches_s), BF),
            V(h_l.shape, BF), V(h_s.shape, BF), V(u_l.shape, BF), V(u_s.shape, BF),
            V((count_l * 2, patches_l, half), BF), V((count_s, patches_s, width), BF),
            V((size, SLAB, token), F32), V((2, SLAB, token), BF), V((2, SLAB, token), BF), V((SLAB, token), F32),
            V((n1, part_n, token), BF), V((n1, part_n, token), BF), V((part_n, token), F32),
            V((f1, part_f, token), BF), V((f1, part_f, token), BF), V((SLAB, token), BF), V((SLAB, token), BF),
            V((24, width), F32), V((2, 16, width), F32), V((n1, 24, width), F32), V((f1, 24, width), F32),
            DMA((1,)), DMA((count_l,)),
            DMA((count_l * 2,)), DMA((count_s,)), DMA((per_l, size)), DMA((per_s, size)),
            DMA((per_l, size)), DMA((per_s, size)), DMA((count_l * 2,)), DMA((count_s,)),
            DMA((1,)), DMA((1,)), DMA((1,)), DMA((1,)), DMA((n1,)), DMA((n1,)), DMA((f1,)), DMA((f1,)),
            DMA((f1,)), DMA((f1,)), DMA((n1,)), DMA((n1,)),
            DMA((2,)), DMA((2,)), DMA((n1,)), DMA((n1,)), DMA((f1,)), DMA((f1,)),
        ] + Gather.sems(groups, near, far),
        input_output_aliases={1: 0},
        compiler_params=pltpu.CompilerParams(
            collective_id=1, has_side_effects=True, vmem_limit_bytes=TOP
        ),
    )(chunk, begun, ey, xl, xs, u_l, u_s, h_l, h_s, sl_l, sl_s, w_l, w_s, small, gain)


def widen_kernel(
    first, second, tok, vec,
    out_first, out_second, gain1, bias1, w1_s, b1_s, w2_s, b2_s, w1_l, b1_l, w2_l, b2_l, gain2, bias2, b1, b2,
):
    for k in range(first.shape[1]):
        out_first[:, k * TILE:(k + 1) * TILE] = first[0, k].astype(F32)
        out_second[k * TILE:(k + 1) * TILE, :] = second[0, k].astype(F32).T

    @pl.when(pl.program_id(0) == 0)
    def _():
        width = vec.shape[1]
        half = width // 2
        large, small = w1_l.shape[0], w1_s.shape[0]
        wide = small + -small % 64
        at = 2 * large
        w1_l[...] = tok[0:large, :].astype(F32)
        w2_l[...] = tok[large:at, :].astype(F32)
        w1_s[...] = tok[at:at + wide, :].astype(F32)[:small]
        w2_s[...] = tok[at + wide:at + 2 * wide, :].astype(F32)[:small]
        gain1[...] = vec[7, :]
        bias1[...] = vec[9, :]
        b1_l[...] = vec[8, 0:half]
        b1_s[...] = vec[8, half:width]
        b2_l[...] = vec[16, 0:large]
        b2_s[...] = vec[16, half:half + small]
        gain2[...] = vec[5, :]
        bias2[...] = vec[6, :]
        for k in range(b1.shape[0] // width):
            b1[k * width:(k + 1) * width] = vec[k, :]
        b2[...] = vec[4, :]


def widen(full, tok, vec, patches_s, patches_l):
    _, groups, width, _ = full.shape
    hidden = groups * TILE
    token = tok.shape[1]
    step = 2 * TILE
    shapes = (
        (width,), (width,), (patches_s, token), (token,), (patches_s, token), (patches_s,),
        (patches_l, token), (token,), (patches_l, token), (patches_l,), (width,), (width,), (hidden,), (width,),
    )

    def whole(shape):
        return pl.BlockSpec(shape, lambda i: (0,) * len(shape))

    return pl.pallas_call(
        widen_kernel,
        grid=(hidden // step,),
        out_shape=(
            jax.ShapeDtypeStruct((width, hidden), F32), jax.ShapeDtypeStruct((hidden, width), F32),
        ) + tuple(jax.ShapeDtypeStruct(shape, F32) for shape in shapes),
        in_specs=[
            pl.BlockSpec((1, 2, width, TILE), lambda i: (0, i, 0, 0)),
            pl.BlockSpec((1, 2, width, TILE), lambda i: (1, i, 0, 0)),
            whole(tok.shape), whole(vec.shape),
        ],
        out_specs=(
            pl.BlockSpec((width, step), lambda i: (0, i)), pl.BlockSpec((step, width), lambda i: (i, 0)),
        ) + tuple(whole(shape) for shape in shapes),
        compiler_params=pltpu.CompilerParams(vmem_limit_bytes=TOP),
    )(full, full, tok, vec)


def local(
    x_small, x_large, live_counts, ln1_gain, ln1_bias,
    tok_w1_small, tok_b1_small, tok_w2_small, tok_b2_small,
    tok_w1_large, tok_b1_large, tok_w2_large, tok_b2_large,
    ln2_gain, ln2_bias, ch_w1, ch_b1, ch_w2, ch_b2, cot_small, cot_large,
):
    width = x_small.shape[2]
    patches_s, patches_l = x_small.shape[1], x_large.shape[1]
    rows = x_small.shape[0] * (patches_s + -patches_s % 64) + x_large.shape[0] * patches_l
    y, *saved = token_forward(
        x_large, x_small, tok_w1_large, tok_w1_small, tok_w2_large.T, tok_w2_small.T,
        tok_b1_large, tok_b1_small, tok_b2_large, tok_b2_small, ln1_gain, ln1_bias, rows + -rows % (3 * LANES),
    )
    out_large, ey, chunk, small_grads, out_small, begun = channel(
        y, live_counts, cot_large, cot_small, ch_w1, ch_w2, ch_b1, ln2_gain, ln2_bias, ch_b2
    )
    near, far = img_split(lax.axis_size("img"))
    far_inside = width % (near * far * 2 * 16) == 0
    if not far_inside:
        same = [[a * near + b for a in range(far)] for b in range(near)]
        chunk = lax.psum(chunk.astype(F32), "img", axis_index_groups=same).astype(BF)
    full, gx_large, tok, vec, gx_small = backward(
        chunk, begun, ey, x_large, x_small, saved, small_grads, ln1_gain
    )
    if not far_inside:
        tok = lax.psum(tok.astype(F32), "img")
    (
        grad_ch_w1, grad_ch_w2, gain1, bias1, w1_s, b1_s, w2_s, b2_s, w1_l, b1_l, w2_l, b2_l,
        gain2, bias2, grad_b1, grad_b2,
    ) = widen(full, tok, vec, patches_s, patches_l)
    return (
        out_small, out_large, gx_small, gx_large, gain1, bias1,
        w1_s, b1_s, w2_s.T, b2_s, w1_l, b1_l, w2_l.T, b2_l,
        gain2, bias2, grad_ch_w1, grad_b1, grad_ch_w2, grad_b2,
    )


def solution(mesh):
    image = P("img", "blk", None)
    whole = P()
    rows = P("blk", None)
    columns = P(None, "blk")
    vector = P("blk")
    in_specs = (
        image, image, P("img", None), whole, whole,
        rows, whole, columns, vector, rows, whole, columns, vector,
        whole, whole, whole, whole, whole, whole, image, image,
    )
    out_specs = (
        image, image, image, image, whole, whole,
        rows, whole, columns, vector, rows, whole, columns, vector,
        whole, whole, whole, whole, whole, whole,
    )
    return jax.shard_map(local, mesh=mesh, in_specs=in_specs, out_specs=out_specs, check_vma=False)
```

```python
import functools

import jax
import jax.numpy as jnp
from jax import lax
from jax.experimental import pallas as pl
from jax.experimental.pallas import tpu as pltpu
from jax.sharding import PartitionSpec as P

EPSILON = 1e-06
LANES = 128
BF = jnp.bfloat16
F32 = jnp.float32


MESH = pl.DeviceIdType.MESH
ANY = pl.BlockSpec(memory_space=pl.ANY)
TILE = 256
LAGS = (1, 3, 5, 7)
LATE = 3
TOP = 62 * 1024 * 1024


def img_split(size):
    near = 2 if size <= 8 else 8
    return near, size // near


def gelu_pair(a):
    square = a * a
    slope = 0.7978845608028654
    t = jnp.tanh(a * (slope + (slope * 0.044715) * square))
    half = 0.5 + 0.5 * t
    inner = slope + (3.0 * slope * 0.044715) * square
    return a * half, half + (0.5 * a) * (1.0 - t * t) * inner


class Peers:
    def __init__(self, near_count):
        self.img = lax.axis_index("img")
        self.blk = lax.axis_index("blk")
        self.core = lax.rem(self.blk, 2)
        self.x = self.blk // 2
        self.near_count = near_count
        self.near = lax.rem(self.img, near_count)
        self.far = self.img // near_count

    def at(self, axis, place):
        if axis == "core":
            return (self.img, self.x * 2 + place)
        if axis == "x":
            return (self.img, place * 2 + self.core)
        if axis == "near":
            return (self.far * self.near_count + place, self.blk)
        return (place * self.near_count + self.near, self.blk)

    def mine(self, axis):
        return {"core": self.core, "x": self.x, "near": self.near, "far": self.far}[axis]


def greet(peers, axes):
    barrier = pltpu.get_barrier_semaphore()
    total = 0
    for axis, count in axes:
        for j in range(1, count):
            there = lax.rem(peers.mine(axis) + j, count)
            pl.semaphore_signal(barrier, inc=1, device_id=peers.at(axis, there), device_id_type=MESH)
            total += 1
    return total


def greeted(total):
    pl.semaphore_wait(pltpu.get_barrier_semaphore(), total)


class Gather:
    def __init__(self, peers, near, far, far_inside, chunk, full, sems):
        self.peers, self.near, self.far_inside = peers, near, far_inside
        self.f = far if far_inside else 1
        self.chunk, self.full = chunk, full
        self.tiles = chunk.shape[0]
        self.late = self.tiles - LATE if far_inside else self.tiles
        self.own_sem, self.x_ss, self.x_rs, self.f_ss, self.f_rs, self.n_ss, self.n_rs, self.c_ss, self.c_rs = sems
        self.place = (peers.near, peers.far if far_inside else 0, peers.x)

    def span(self, k, axes):
        index = tuple(p if a in axes else slice(None) for p, a in zip(self.place, "nfx"))
        while index and isinstance(index[-1], slice):
            index = index[:-1]
        return self.full.at[(self.peers.core, k) + index]

    def send(self, src, dst, ss, rs, device):
        return pltpu.make_async_remote_copy(
            src_ref=src, dst_ref=dst, send_sem=ss, recv_sem=rs, device_id=device, device_id_type=MESH
        )

    def own(self, k):
        return pltpu.make_async_copy(self.chunk.at[k], self.span(k, "nfx"), self.own_sem.at[k])

    def x_first(self, k):
        there = self.peers.at("x", 1 - self.peers.x)
        return self.send(self.chunk.at[k], self.span(k, "nfx"), self.x_ss.at[k], self.x_rs.at[k], there)

    def x_last(self, k):
        there = self.peers.at("x", 1 - self.peers.x)
        return self.send(self.span(k, "x"), self.span(k, "x"), self.x_ss.at[k], self.x_rs.at[k], there)

    def spread(self, axis, count, span, ss, rs, k):
        copies = []
        for j in range(1, count):
            there = self.peers.at(axis, lax.rem(self.peers.mine(axis) + j, count))
            copies.append(self.send(span, span, ss.at[k, j - 1], rs.at[k, j - 1], there))
        return copies

    def to_far(self, k):
        return self.spread("far", self.f, self.span(k, "nf" if k < self.late else "nfx"), self.f_ss, self.f_rs, k)

    def to_near(self, k):
        return self.spread("near", self.near, self.span(k, "n" if k < self.late else "nx"), self.n_ss, self.n_rs, k)

    def to_core(self, k):
        span = self.span(k, "")
        return self.send(span, span, self.c_ss.at[k], self.c_rs.at[k], self.peers.at("core", 1 - self.peers.core))

    def first(self, k):
        self.own(k).start()

        @pl.when(k < self.late)
        def _():
            self.x_first(k).start()

    def end_first(self, k):
        self.own(k).wait()
        if k < self.late:
            self.x_first(k).wait()

    def second(self, k):
        for copy in self.to_far(k):
            copy.start()

    def third(self, k):
        for copy in self.to_far(k):
            copy.wait_recv()
        for copy in self.to_near(k):
            copy.start()

    def fourth(self, k):
        for copy in self.to_near(k):
            copy.wait_recv()
        (self.to_core(k) if k < self.late else self.x_last(k)).start()

    def fifth(self, k):
        if k >= self.late:
            self.x_last(k).wait_recv()
            self.to_core(k).start()

    def drain(self, k):
        for copy in self.to_far(k) + self.to_near(k):
            copy.wait_send()
        if k >= self.late:
            self.x_last(k).wait_send()
        self.to_core(k).wait()

    @staticmethod
    def sems(groups, near, far):
        DMA = pltpu.SemaphoreType.DMA
        n1, f1 = near - 1, max(far - 1, 1)
        return [DMA((groups,))] * 3 + [DMA((groups, f1))] * 2 + [DMA((groups, n1))] * 2 + [DMA((groups,))] * 2


def row(ref):
    return ref[...].reshape(1, -1)


def column(ref, rows):
    value = jnp.broadcast_to(ref[...].reshape(1, -1), (8, ref.shape[0])).T[:, :1]
    return value if rows == ref.shape[0] else jnp.concatenate([value, jnp.zeros((rows - ref.shape[0], 1), F32)])


def channel_kernel(
    near, far, far_inside,
    y_hbm, live, cot_l, cot_s_in, w1_hbm, w2_hbm, b1_ref, gain_ref, bias_ref, b2_ref,
    out_l, ey_hbm, chunk_ref, small_ref, out_s_t, full_hbm,
    cot_s, out_s, y, ec, v, lt, rt, w1, w2, acc_out, acc_ev, out_low,
    keep, core_tx, core_rx,
    a_keep_n, a_near_tx, a_near_rx, a_keep_f, a_far_tx, a_far_rx, a_keep_x, a_x_tx, a_x_rx,
    b_keep_x, b_x_tx, b_x_rx, b_keep_n, b_near_tx, b_near_rx, b_keep_f, b_far_tx, b_far_rx,
    in_sem, w_sem, out_sem, core_ss, core_rs,
    a_near_ss, a_near_rs, a_far_ss, a_far_rs, a_x_ss, a_x_rs,
    b_near_ss, b_near_rs, b_far_ss, b_far_rs, b_x_ss, b_x_rs, *gather_sems,
):
    rows, width = y.shape
    tiles = w1.shape[0]
    count_l, patches_l, _ = cot_l.shape
    count_s, patches_s, _ = cot_s.shape
    wide_s = patches_s + -patches_s % 64
    small_rows = count_s * wide_s
    peers = Peers(near)
    core = peers.core
    f_place = peers.far if far_inside else 0
    gather = Gather(peers, near, far, far_inside, chunk_ref, full_hbm, gather_sems)
    part = 128
    parts = rows // part
    gain, bias, b2 = row(gain_ref), row(bias_ref), row(b2_ref)

    def w_copies(t):
        return (
            pltpu.make_async_copy(w1_hbm.at[:, pl.ds(t * TILE, TILE)], w1.at[t], w_sem.at[0, t]),
            pltpu.make_async_copy(w2_hbm.at[pl.ds(t * TILE, TILE)], w2.at[t], w_sem.at[1, t]),
        )

    y_in = pltpu.make_async_copy(y_hbm, y, in_sem.at[0])
    y_in.start()

    def start_w(t, carry):
        for copy in w_copies(t):
            copy.start()
        return carry

    lax.fori_loop(0, tiles, start_w, 0)
    axes = [("core", 2), ("near", near)] + ([("far", far)] if far_inside else []) + [("x", 2)]
    greetings = greet(peers, axes)
    small_ref[...] = jnp.zeros_like(small_ref)
    used = small_rows + count_l * patches_l
    ec[0:small_rows, :] = jnp.zeros((small_rows, width), BF)
    if rows > used:
        ec[used:rows, :] = jnp.zeros((rows - used, width), BF)

    def live_l(n):
        return jnp.where(n < live[0, 1], 1.0, 0.0).astype(F32)

    def live_s(n):
        return jnp.where(n < live[0, 0], 1.0, 0.0).astype(F32)

    def mask_l(n, carry):
        ec[pl.ds(pl.multiple_of(small_rows + n * patches_l, 16), patches_l), :] = (
            cot_l[n].astype(F32) * live_l(n)
        ).astype(BF)
        return carry

    def mask_s(n, carry):
        ec[pl.ds(pl.multiple_of(n * wide_s, 16), patches_s), :] = (cot_s[n].astype(F32) * live_s(n)).astype(BF)
        return carry

    lax.fori_loop(0, count_l, mask_l, 0)
    for n in range(count_s):
        cot_s[n] = cot_s_in[:, n, :]
    lax.fori_loop(0, count_s, mask_s, 0)
    y_in.wait()

    def prepare(p, carry):
        at = pl.ds(pl.multiple_of(p * part, part), part)
        unit, _ = unit_rows(y[at, :])
        low = (unit * gain + bias).astype(BF)
        v[at, :] = low
        lt[0, :, at] = low.T
        own = ec[at, :]
        lt[1, :, at] = own.T
        small_ref[4:5, :] += jnp.sum(own.astype(F32), axis=0, keepdims=True)
        acc_out[at, :] = jnp.zeros((part, width), F32)
        acc_ev[at, :] = jnp.zeros((part, width), F32)
        return carry

    lax.fori_loop(0, parts, prepare, 0)
    greeted(greetings)

    def send(src, dst, ss, rs, device):
        return pltpu.make_async_remote_copy(
            src_ref=src, dst_ref=dst, send_sem=ss, recv_sem=rs, device_id=device, device_id_type=MESH
        )

    def core_copy(t):
        slot = lax.rem(t, 2)
        return send(core_tx.at[slot], core_rx.at[t], core_ss.at[slot], core_rs.at[t], peers.at("core", 1 - core))

    def spread(tx, rx, ss, rs, axis, count, i):
        slot = lax.rem(i, 2)
        copies = []
        for j in range(1, count):
            there = lax.rem(peers.mine(axis) + j, count)
            copies.append(
                send(tx.at[slot, j - 1], rx.at[i, j - 1], ss.at[slot, j - 1], rs.at[i, j - 1], peers.at(axis, there))
            )
        return copies

    f = far if far_inside else 1
    a_near = lambda i: spread(a_near_tx, a_near_rx, a_near_ss, a_near_rs, "near", near, i)
    a_far = lambda i: spread(a_far_tx, a_far_rx, a_far_ss, a_far_rs, "far", f, i)
    a_x = lambda i: spread(a_x_tx, a_x_rx, a_x_ss, a_x_rs, "x", 2, i)
    b_near = lambda i: spread(b_near_tx, b_near_rx, b_near_ss, b_near_rs, "near", near, i)
    b_far = lambda i: spread(b_far_tx, b_far_rx, b_far_ss, b_far_rs, "far", f, i)
    b_x = lambda i: spread(b_x_tx, b_x_rx, b_x_ss, b_x_rs, "x", 2, i)
    each = width // near // f // 2

    def tile_step(t):
        for copy in w_copies(t):
            copy.wait()

        @pl.when(t >= 2)
        def _():
            core_copy(t - 2).wait_send()

        slot = lax.rem(t, 2)
        columns = pl.ds(pl.multiple_of(t * TILE, TILE), TILE)
        a = matmul(v[...], w1[t]) + b1_ref[columns].reshape(1, -1)
        gh = matmul_nt(ec[...], w2[t])
        g, slope = gelu_pair(a)
        ea = (slope * gh).astype(BF)
        rt[1] = g.astype(BF)
        rt[0] = ea
        per = width // TILE
        small_ref[lax.div(t, per), pl.ds(pl.multiple_of(lax.rem(t, per) * TILE, TILE), TILE)] = jnp.sum(
            ea.astype(F32), axis=0
        )
        core_tx[slot] = matmul(lt[1 - core], rt[1 - core]).astype(BF).reshape(near, f, 2, each, TILE)
        keep[slot] = matmul(lt[core], rt[core]).reshape(near, f, 2, each, TILE)
        acc_out[...] += matmul(rt[1], w2[t])
        acc_ev[...] += matmul_nt(rt[0], w1[t])
        core_copy(t).start()

    def ey_copy(at, n):
        return pltpu.make_async_copy(acc_ev.at[at], ey_hbm.at[at], out_sem.at[n])

    def at_l(n):
        return pl.ds(pl.multiple_of(small_rows + n * patches_l, 16), patches_l)

    def at_s(n):
        return pl.ds(pl.multiple_of(n * wide_s, 16), wide_s)

    def out_copy(n):
        return pltpu.make_async_copy(out_low.at[n], out_l.at[n], out_sem.at[count_l + count_s + n])

    def finish_rows(at, live_here):
        here = y[at, :]
        result = ((here + acc_out[at, :] + b2) * live_here).astype(BF)
        unit, scale = unit_rows(here)
        ev = acc_ev[at, :]
        small_ref[5:6, :] += jnp.sum(ev * unit, axis=0, keepdims=True)
        small_ref[6:7, :] += jnp.sum(ev, axis=0, keepdims=True)
        d = ev * gain
        m1 = jnp.mean(d, axis=-1, keepdims=True)
        m2 = jnp.mean(d * unit, axis=-1, keepdims=True)
        acc_ev[at, :] = ec[at, :].astype(F32) + scale * (d - m1 - unit * m2)
        return result

    def finish(p):
        def one_l(q, carry):
            n = p + q * 4

            @pl.when(n < count_l)
            def _():
                out_low[n] = finish_rows(at_l(n), live_l(n))
                ey_copy(at_l(n), n).start()
                out_copy(n).start()

            return carry

        def one_s(q, carry):
            n = p + q * 4

            @pl.when(n < count_s)
            def _():
                out_s[n] = finish_rows(at_s(n), live_s(n))[:patches_s]
                ey_copy(at_s(n), count_l + n).start()

            return carry

        lax.fori_loop(0, pl.cdiv(count_l, 4), one_l, 0)
        lax.fori_loop(0, pl.cdiv(count_s, 4), one_s, 0)

    def free(copies, i):
        @pl.when(i >= 2)
        def _():
            for copy in copies(i - 2):
                copy.wait_send()

    def reduce(value, axis, count, place, tx, own, copies, i):
        slot = lax.rem(i, 2)
        free(copies, i)
        made = copies(i)
        for j in range(1, count + 1):
            there = lax.rem(place + j, count)
            piece = value(there)
            if j < count:
                tx[slot, j - 1] = piece.astype(BF)
                made[j - 1].start()
            else:
                own(slot, piece)

    def arrivals(copies, i):
        for copy in copies(i):
            copy.wait_recv()

    def save(ref):
        def put(slot, piece):
            ref[slot] = piece
        return put

    def plus(base, rx, i, count, index):
        value = base
        for k in range(count - 1):
            value = value + rx[(i, k) + index].astype(F32)
        return value

    def chunk_out(t, value):
        chunk_ref[t] = value.astype(BF)
        if far_inside:
            gather.first(t)

    def even_core(t):
        i = lax.div(t, 2)
        core_copy(t).wait_recv()
        reduce(
            lambda p: keep[0, p] + core_rx[t, p].astype(F32),
            "near", near, peers.near, a_near_tx, save(a_keep_n), a_near, i,
        )

    def even_near(t):
        i = lax.div(t, 2)
        slot = lax.rem(i, 2)
        arrivals(a_near, i)
        reduce(
            lambda p: plus(a_keep_n[slot, p], a_near_rx, i, near, (p,)),
            "far", f, f_place, a_far_tx, save(a_keep_f), a_far, i,
        )

    def even_far(t):
        i = lax.div(t, 2)
        slot = lax.rem(i, 2)
        arrivals(a_far, i)
        reduce(
            lambda p: plus(a_keep_f[slot, p], a_far_rx, i, f, (p,)),
            "x", 2, peers.x, a_x_tx, save(a_keep_x), a_x, i,
        )

    def even_x(t):
        i = lax.div(t, 2)
        arrivals(a_x, i)
        chunk_out(t, a_keep_x[lax.rem(i, 2)] + a_x_rx[i, 0].astype(F32))

    def odd_core(t):
        i = lax.div(t, 2)
        core_copy(t).wait_recv()
        reduce(
            lambda p: keep[1, :, :, p] + core_rx[t, :, :, p].astype(F32),
            "x", 2, peers.x, b_x_tx, save(b_keep_x), b_x, i,
        )

    def odd_x(t):
        i = lax.div(t, 2)
        slot = lax.rem(i, 2)
        arrivals(b_x, i)
        reduce(
            lambda p: plus(b_keep_x[slot, p], b_x_rx, i, 2, (p,)),
            "near", near, peers.near, b_near_tx, save(b_keep_n), b_near, i,
        )

    def odd_near(t):
        i = lax.div(t, 2)
        slot = lax.rem(i, 2)
        arrivals(b_near, i)
        reduce(
            lambda p: plus(b_keep_n[slot, p], b_near_rx, i, near, (p,)),
            "far", f, f_place, b_far_tx, save(b_keep_f), b_far, i,
        )

    def odd_far(t):
        i = lax.div(t, 2)
        arrivals(b_far, i)
        slot = lax.rem(i, 2)
        chunk_out(t, plus(b_keep_f[slot], b_far_rx, i, f, ()))

    stages = ((even_core, even_near, even_far, even_x), (odd_core, odd_x, odd_near, odd_far))

    def pair(s2, carry):
        for parity in range(2):
            s = s2 * 2 + parity

            @pl.when(s < tiles)
            def _():
                tile_step(s)

            for place, lag in enumerate(LAGS):
                t = s - lag
                stage = stages[(parity - lag) % 2][place]

                @pl.when((t >= 0) & (t < tiles))
                def _(t=t, stage=stage):
                    stage(t)

            @pl.when((s >= tiles) & (s < tiles + 4))
            def _():
                finish(s - tiles)

        return carry

    lax.fori_loop(0, (tiles + LAGS[-1] + 1) // 2, pair, 0)
    if far_inside:
        for k in range(tiles):
            gather.end_first(k)
    for t in (tiles - 2, tiles - 1):
        core_copy(t).wait_send()
    for copies in (a_near, a_far, a_x, b_near, b_far, b_x):
        for i in (tiles // 2 - 2, tiles // 2 - 1):
            for copy in copies(i):
                copy.wait_send()
    for n in range(count_s):
        out_s_t[:, n, :] = out_s[n]
    for n in range(count_l):
        ey_copy(at_l(n), n).wait()
        out_copy(n).wait()
    for n in range(count_s):
        ey_copy(at_s(n), count_l + n).wait()


def channel(y, live, cot_l, cot_s, w1, w2, b1, gain, bias, b2):
    rows, width = y.shape
    hidden = w1.shape[1]
    tiles = hidden // TILE
    near, far = img_split(lax.axis_size("img"))
    far_inside = width % (near * far * 2 * 16) == 0
    f = far if far_inside else 1
    chunk = width // near // f // 2
    vmem = pl.BlockSpec(memory_space=pltpu.VMEM)
    V = pltpu.VMEM
    DMA = pltpu.SemaphoreType.DMA
    fm = max(f - 1, 1)
    nm = near - 1
    pairs = tiles // 2
    real_s, count_s, _ = cot_s.shape
    count = cot_l.shape[0] + count_s
    return pl.pallas_call(
        functools.partial(channel_kernel, near, far, far_inside),
        out_shape=(
            jax.ShapeDtypeStruct(cot_l.shape, BF),
            jax.ShapeDtypeStruct((rows, width), F32),
            jax.ShapeDtypeStruct((tiles, chunk, TILE), BF),
            jax.ShapeDtypeStruct((8, width), F32),
            jax.ShapeDtypeStruct(cot_s.shape, BF),
            jax.ShapeDtypeStruct((2, tiles, near, f, 2, chunk, TILE), BF),
        ),
        in_specs=[ANY, pl.BlockSpec(memory_space=pltpu.SMEM), vmem, vmem, ANY, ANY] + [vmem] * 4,
        out_specs=(ANY, ANY, vmem, vmem, vmem, ANY),
        scratch_shapes=[
            V((count_s, real_s, width), BF), V((count_s, real_s, width), BF),
            V((rows, width), F32), V((rows, width), BF), V((rows, width), BF),
            V((2, width, rows), BF), V((2, rows, TILE), BF),
            V((tiles, width, TILE), BF), V((tiles, TILE, width), BF),
            V((rows, width), F32), V((rows, width), F32), V(cot_l.shape, BF),
            V((2, near, f, 2, chunk, TILE), F32), V((2, near, f, 2, chunk, TILE), BF),
            V((tiles, near, f, 2, chunk, TILE), BF),
            V((2, f, 2, chunk, TILE), F32), V((2, nm, f, 2, chunk, TILE), BF), V((pairs, nm, f, 2, chunk, TILE), BF),
            V((2, 2, chunk, TILE), F32), V((2, fm, 2, chunk, TILE), BF), V((pairs, fm, 2, chunk, TILE), BF),
            V((2, chunk, TILE), F32), V((2, 1, chunk, TILE), BF), V((pairs, 1, chunk, TILE), BF),
            V((2, near, f, chunk, TILE), F32), V((2, 1, near, f, chunk, TILE), BF),
            V((pairs, 1, near, f, chunk, TILE), BF),
            V((2, f, chunk, TILE), F32), V((2, nm, f, chunk, TILE), BF), V((pairs, nm, f, chunk, TILE), BF),
            V((2, chunk, TILE), F32), V((2, fm, chunk, TILE), BF), V((pairs, fm, chunk, TILE), BF),
            DMA((1,)), DMA((2, tiles)), DMA((2 * count,)), DMA((2,)), DMA((tiles,)),
            DMA((2, nm)), DMA((pairs, nm)), DMA((2, fm)), DMA((pairs, fm)), DMA((2, 1)), DMA((pairs, 1)),
            DMA((2, nm)), DMA((pairs, nm)), DMA((2, fm)), DMA((pairs, fm)), DMA((2, 1)), DMA((pairs, 1)),
        ] + Gather.sems(tiles, near, f),
        compiler_params=pltpu.CompilerParams(
            collective_id=0, has_side_effects=True, vmem_limit_bytes=TOP
        ),
    )(y, live, cot_l, cot_s, w1, w2, b1, gain, bias, b2)


NT = (((1,), (1,)), ((), ()))


def matmul(left, right):
    return jnp.dot(left, right, preferred_element_type=F32)


def matmul_nt(left, right):
    return lax.dot_general(left, right, NT, preferred_element_type=F32)


class Swap:
    def __init__(self, peers, size, per_l, per_s, patches_l, patches_s):
        self.peers, self.size = peers, size
        self.per_l, self.per_s = per_l, per_s
        self.pl, self.ps = patches_l, patches_s

    def other(self, step):
        return lax.rem(self.peers.blk + step, self.size)

    def copy(self, src, dst, ss, rs, place):
        return pltpu.make_async_remote_copy(
            src_ref=src, dst_ref=dst, send_sem=ss, recv_sem=rs,
            device_id=(self.peers.img, place), device_id_type=MESH,
        )

    def rows(self, place, patches):
        return pl.ds(pl.multiple_of(place * patches, patches), patches)

    def out(self, kind, j, place, source, tx, cols, ss, rs):
        per, patches = (self.per_l, self.pl) if kind == "l" else (self.per_s, self.ps)
        unit = place * per + j
        return self.copy(
            tx.at[unit], cols.at[j, self.rows(source, patches)], ss.at[unit], rs.at[j, source], place
        )

    def back(self, kind, j, owner, place, cols, rx, ss, rs):
        per, patches = (self.per_l, self.pl) if kind == "l" else (self.per_s, self.ps)
        unit = owner * per + j
        return self.copy(
            cols.at[j, self.rows(place, patches)], rx.at[unit], ss.at[j, place], rs.at[unit], place
        )


def greet_all(peers, size, near, far):
    barrier = pltpu.get_barrier_semaphore()
    total = 0
    for j in range(1, size):
        there = lax.rem(peers.blk + j, size)
        pl.semaphore_signal(barrier, inc=1, device_id=(peers.img, there), device_id_type=MESH)
        total += 1
    for axis, count in (("near", near), ("far", far)):
        for j in range(1, count):
            there = lax.rem(peers.mine(axis) + j, count)
            pl.semaphore_signal(barrier, inc=1, device_id=peers.at(axis, there), device_id_type=MESH)
            total += 1
    pl.semaphore_wait(barrier, total)


def unit_rows(row):
    mean = jnp.mean(row, axis=-1, keepdims=True)
    centered = row - mean
    var = jnp.mean(centered * centered, axis=-1, keepdims=True)
    scale = lax.rsqrt(var + EPSILON)
    return centered * scale, scale


def token_kernel(
    near, size,
    xl, xs_in, w1_l, w1_s, w2_l, w2_s, b1_l_ref, b1_s_ref, b2_l_ref, b2_s_ref, gain_ref, bias_ref,
    y_hbm, u_l, u_s, h_l, h_s, sl_l, sl_s, w_l, w_s,
    xs, wq_l, wq_s, tx_l, tx_s, w1t_l, w1t_s, m_l, m_s, rx_l, rx_s, y,
    y_sem, own_sem, wown, w_ss, w_rs, out_ss_l, out_ss_s, out_rs_l, out_rs_s, bk_ss_l, bk_ss_s, bk_rs_l, bk_rs_s,
):
    peers = Peers(near)
    me = peers.blk
    count_l, patches_l, width = xl.shape
    count_s, real_s, _ = xs.shape
    patches_s = tx_s.shape[1]
    token = w1_l.shape[1]
    half = width // 2
    per_l, per_s = count_l * 2 // size, count_s // size
    swap = Swap(peers, size, per_l, per_s, patches_l, patches_s)
    wq_l[0] = w1_l[...]
    wq_l[1] = w2_l[...]
    wq_s[...] = jnp.zeros_like(wq_s)
    wq_s[0, :real_s] = w1_s[...]
    wq_s[1, :real_s] = w2_s[...]

    barrier = pltpu.get_barrier_semaphore()
    for j in range(1, size):
        pl.semaphore_signal(barrier, inc=1, device_id=(peers.img, swap.other(j)), device_id_type=MESH)

    def weights(src_l, src_s, quarter, n, place):
        return (
            swap.copy(src_l, w_l.at[:, swap.rows(quarter, patches_l)], w_ss.at[n, 0], w_rs.at[n, 0], place),
            swap.copy(src_s, w_s.at[:, swap.rows(quarter, patches_s)], w_ss.at[n, 1], w_rs.at[n, 1], place),
        )

    x_peer = (1 - peers.x) * 2 + peers.core
    core_peer = peers.x * 2 + 1 - peers.core
    to_x = weights(wq_l, wq_s, me, 0, x_peer)
    to_core = weights(wq_l, wq_s, me, 1, core_peer)
    relay = weights(
        w_l.at[:, swap.rows(x_peer, patches_l)], w_s.at[:, swap.rows(x_peer, patches_s)], x_peer, 2, core_peer
    )
    own_w = (
        pltpu.make_async_copy(wq_l, w_l.at[:, swap.rows(me, patches_l)], wown.at[0]),
        pltpu.make_async_copy(wq_s, w_s.at[:, swap.rows(me, patches_s)], wown.at[1]),
    )
    for copy in own_w:
        copy.start()

    gain, bias = row(gain_ref), row(bias_ref)

    def norm(values):
        unit, _ = unit_rows(values.astype(F32))
        return (unit * gain + bias).astype(BF)

    def norm_l(n, carry):
        u = norm(xl[n])
        tx_l[2 * n] = u[:, :half]
        tx_l[2 * n + 1] = u[:, half:]
        return carry


    def norm_s(n, carry):
        tx_s[n, :real_s] = norm(xs[n])
        return carry

    lax.fori_loop(0, count_l, norm_l, 0)
    greeted(size - 1)
    for copy in to_x + to_core:
        copy.start()
    for j in range(per_l):
        for k in range(1, size):
            swap.out("l", j, swap.other(k), me, tx_l, u_l, out_ss_l, out_rs_l).start()
    tx_s[...] = jnp.zeros_like(tx_s)
    for n in range(count_s):
        xs[n] = xs_in[:, n, :]
    lax.fori_loop(0, count_s, norm_s, 0)
    for j in range(per_s):
        for k in range(1, size):
            swap.out("s", j, swap.other(k), me, tx_s, u_s, out_ss_s, out_rs_s).start()
    for j in range(per_l):
        u_l[j, swap.rows(me, patches_l)] = tx_l[me * per_l + j]
    for j in range(per_s):
        u_s[j, swap.rows(me, patches_s)] = tx_s[me * per_s + j]

    for copy in to_x:
        copy.wait_recv()
    for copy in relay:
        copy.start()
    for copy in own_w:
        copy.wait()
    for copy in to_core + relay:
        copy.wait_recv()
    b1_l, b1_s = column(b1_l_ref, token), column(b1_s_ref, token)
    b2_l, b2_s = column(b2_l_ref, patches_l), column(b2_s_ref, real_s)
    w1t_l[...] = w_l[0].T
    w1t_s[...] = w_s[0].T

    def mix(kind, j, cols, w1t, w2t, b1, h, slope, m, outs, tx, rx, bss, brs):
        for k in range(1, size):
            source = swap.other(k)
            swap.out(kind, j, me, source, tx, cols, *outs).wait_recv()
        g, d = gelu_pair(matmul(w1t[...], cols[j]) + b1)
        low = g.astype(BF)
        h[j] = low
        slope[j] = d.astype(BF)
        m[j] = matmul(w2t, low).astype(BF)
        for k in range(1, size):
            swap.back(kind, j, me, swap.other(k), m, rx, bss, brs).start()
        patches, per = (patches_l, per_l) if kind == "l" else (patches_s, per_s)
        rx[me * per + j] = m[j, swap.rows(me, patches)]

    for j in range(per_l):
        mix("l", j, u_l, w1t_l, w_l[1], b1_l, h_l, sl_l, m_l, (out_ss_l, out_rs_l), tx_l, rx_l, bk_ss_l, bk_rs_l)
    for j in range(per_s):
        mix("s", j, u_s, w1t_s, w_s[1], b1_s, h_s, sl_s, m_s, (out_ss_s, out_rs_s), tx_s, rx_s, bk_ss_s, bk_rs_s)

    small_rows = count_s * patches_s
    rows = y.shape[0]
    used = small_rows + count_l * patches_l
    y[0:small_rows, :] = jnp.zeros((small_rows, width), F32)
    if rows > used:
        y[used:rows, :] = jnp.zeros((rows - used, width), F32)

    def arrived(kind, unit, m, rx, bss, brs):
        per = per_l if kind == "l" else per_s
        owner = unit // per

        @pl.when(owner != me)
        def _():
            swap.back(kind, unit - owner * per, owner, me, m, rx, bss, brs).wait_recv()

    def home_l(n, carry):
        arrived("l", 2 * n, m_l, rx_l, bk_ss_l, bk_rs_l)
        arrived("l", 2 * n + 1, m_l, rx_l, bk_ss_l, bk_rs_l)
        at = pl.ds(pl.multiple_of(small_rows + n * patches_l, 16), patches_l)
        y[at, :half] = xl[n, :, :half].astype(F32) + rx_l[2 * n].astype(F32) + b2_l
        y[at, half:] = xl[n, :, half:].astype(F32) + rx_l[2 * n + 1].astype(F32) + b2_l
        return carry

    def home_s(n, carry):
        arrived("s", n, m_s, rx_s, bk_ss_s, bk_rs_s)
        at = pl.ds(pl.multiple_of(n * patches_s, 16), real_s)
        y[at, :] = xs[n].astype(F32) + rx_s[n, :real_s].astype(F32) + b2_s
        return carry

    lax.fori_loop(0, count_l, home_l, 0)
    lax.fori_loop(0, count_s, home_s, 0)
    y_out = pltpu.make_async_copy(y, y_hbm, y_sem.at[0])
    y_out.start()
    for copy in to_x + to_core + relay:
        copy.wait_send()
    for k in range(1, size):
        there = swap.other(k)
        for j in range(per_l):
            swap.out("l", j, there, me, tx_l, u_l, out_ss_l, out_rs_l).wait_send()
            swap.back("l", j, me, there, m_l, rx_l, bk_ss_l, bk_rs_l).wait_send()
        for j in range(per_s):
            swap.out("s", j, there, me, tx_s, u_s, out_ss_s, out_rs_s).wait_send()
            swap.back("s", j, me, there, m_s, rx_s, bk_ss_s, bk_rs_s).wait_send()
    y_out.wait()


def token_forward(xl, xs, w1_l, w1_s, w2_l, w2_s, b1_l, b1_s, b2_l, b2_s, gain, bias, rows):
    size = lax.axis_size("blk")
    near, far = img_split(lax.axis_size("img"))
    count_l, patches_l, width = xl.shape
    real_s, count_s, _ = xs.shape
    patches_s = real_s + -real_s % 64
    token = w1_l.shape[1]
    half = width // 2
    per_l, per_s = count_l * 2 // size, count_s // size
    vmem = pl.BlockSpec(memory_space=pltpu.VMEM)
    V = pltpu.VMEM
    DMA = pltpu.SemaphoreType.DMA
    low = lambda *shape: jax.ShapeDtypeStruct(shape, BF)
    return pl.pallas_call(
        functools.partial(token_kernel, near, size),
        out_shape=(
            jax.ShapeDtypeStruct((rows, width), F32),
            low(per_l, size * patches_l, half), low(per_s, size * patches_s, width),
            low(per_l, token, half), low(per_s, token, width),
            low(per_l, token, half), low(per_s, token, width),
            low(2, size * patches_l, token), low(2, size * patches_s, token),
        ),
        in_specs=[vmem] * 12,
        out_specs=(ANY,) + (vmem,) * 8,
        scratch_shapes=[
            V((count_s, real_s, width), BF), V((2, patches_l, token), BF), V((2, patches_s, token), BF),
            V((count_l * 2, patches_l, half), BF), V((count_s, patches_s, width), BF),
            V((token, size * patches_l), BF), V((token, size * patches_s), BF),
            V((per_l, size * patches_l, half), BF), V((per_s, size * patches_s, width), BF),
            V((count_l * 2, patches_l, half), BF), V((count_s, patches_s, width), BF),
            V((rows, width), F32),
            DMA((1,)), DMA((1,)), DMA((2,)), DMA((3, 2)), DMA((3, 2)),
            DMA((count_l * 2,)), DMA((count_s,)), DMA((per_l, size)), DMA((per_s, size)),
            DMA((per_l, size)), DMA((per_s, size)), DMA((count_l * 2,)), DMA((count_s,)),
        ],
        compiler_params=pltpu.CompilerParams(
            collective_id=2, has_side_effects=True, vmem_limit_bytes=TOP
        ),
    )(xl, xs, w1_l, w1_s, w2_l, w2_s, b1_l, b1_s, b2_l, b2_s, gain, bias)


DEPTH = 3
SLAB = 512


def backward_kernel(
    near, far, size, far_inside,
    chunk_hbm, begun_hbm, ey_hbm,
    xl_in, xs_in, u_l_in, u_s_in, h_l_in, h_s_in, sl_l_in, sl_s_in, w_l_in, w_s_in, small_in, gain_ref,
    full_hbm, gx_hbm, tok_out, vec_out, gx_out,
    xl, xs_in_v, u_l, u_s, h_l, h_s, sl_l, sl_s, w_l, w_s, in_sem, xs, gx_s,
    ey, tx_l, tx_s, e_l, e_s, w2_l, w2_s, ep_l, ep_s, eu_l, eu_s, rx_l, rx_s,
    grads, tok_tx, tok_rx, tok_sum, tokn_tx, tokn_rx, tok_half, tokf_tx, tokf_rx, tokx_tx, tokx_rx,
    vec, vec_rx, vecn_rx, vecf_rx,
    ey_sem, gx_sem,
    out_ss_l, out_ss_s, out_rs_l, out_rs_s, bk_ss_l, bk_ss_s, bk_rs_l, bk_rs_s,
    tc_ss, tc_rs, tx_ss, tx_rs, tn_ss, tn_rs, tf_ss, tf_rs, taf_ss, taf_rs, tan_ss, tan_rs,
    v_ss, v_rs, vn_ss, vn_rs, vf_ss, vf_rs, *gather_sems,
):
    peers = Peers(near)
    me = peers.blk
    count_l, patches_l, width = xl.shape
    count_s, real_s, _ = xs.shape
    patches_s = tx_s.shape[1]
    token = w_l.shape[2]
    gain = row(gain_ref)
    half = width // 2
    per_l, per_s = count_l * 2 // size, count_s // size
    swap = Swap(peers, size, per_l, per_s, patches_l, patches_s)
    small_rows = count_s * patches_s
    x_peer = peers.at("x", 1 - peers.x)
    core_peer = peers.at("core", 1 - peers.core)

    def send(src, dst, ss, rs, device):
        return pltpu.make_async_remote_copy(
            src_ref=src, dst_ref=dst, send_sem=ss, recv_sem=rs, device_id=device, device_id_type=MESH
        )

    def others(axis, count):
        return [(j, peers.at(axis, lax.rem(peers.mine(axis) + j, count))) for j in range(1, count)]

    near_peers = others("near", near)
    far_peers = others("far", far)

    groups = chunk_hbm.shape[0]
    gather = Gather(peers, near, far, far_inside, chunk_hbm, full_hbm, gather_sems)
    waiting = list(range(groups))

    def tick():
        if waiting:
            k = waiting.pop(0)
            gather.third(k)
            if k + DEPTH < groups:
                gather.second(k + DEPTH)
            if k > 0:
                gather.fourth(k - 1)
            if k > 1:
                gather.fifth(k - 2)

    ey_in = pltpu.make_async_copy(ey_hbm, ey, ey_sem.at[0])
    ey_in.start()
    inputs = [
        pltpu.make_async_copy(src, dst, in_sem.at[n])
        for n, (src, dst) in enumerate((
            (w_l_in, w_l), (w_s_in, w_s), (sl_l_in, sl_l), (sl_s_in, sl_s), (u_l_in, u_l), (u_s_in, u_s),
            (h_l_in, h_l), (h_s_in, h_s), (xl_in, xl), (xs_in, xs_in_v),
        ))
    ]
    for copy in inputs:
        copy.start()
    greet_all(peers, size, near, far)
    if not far_inside:
        for k in range(groups):
            gather.first(k)
        for k in range(groups):
            gather.end_first(k)
    for k in range(DEPTH):
        gather.second(k)
    ey_in.wait()
    vec[...] = jnp.zeros_like(vec)
    vec[0:8, :] = small_in[...]
    def cast_l(n, carry):
        at = pl.ds(pl.multiple_of(small_rows + n * patches_l, 16), patches_l)
        et = ey[at, :].astype(BF)
        tx_l[2 * n] = et[:, :half]
        tx_l[2 * n + 1] = et[:, half:]
        return carry

    def cast_s(n, carry):
        at = pl.ds(pl.multiple_of(n * patches_s, 16), patches_s)
        tx_s[n] = ey[at, :].astype(BF)
        return carry

    lax.fori_loop(0, count_l, cast_l, 0)
    for j in range(per_l):
        for k in range(1, size):
            swap.out("l", j, swap.other(k), me, tx_l, e_l, out_ss_l, out_rs_l).start()
    lax.fori_loop(0, count_s, cast_s, 0)
    for j in range(per_s):
        for k in range(1, size):
            swap.out("s", j, swap.other(k), me, tx_s, e_s, out_ss_s, out_rs_s).start()
    for j in range(per_l):
        e_l[j, swap.rows(me, patches_l)] = tx_l[me * per_l + j]
    for j in range(per_s):
        e_s[j, swap.rows(me, patches_s)] = tx_s[me * per_s + j]
    for copy in inputs:
        copy.wait()
    for n in range(count_s):
        xs[n] = xs_in_v[:, n, :]
    w2_l[...] = w_l[1].T
    w2_s[...] = w_s[1].T
    ones_l = jnp.ones((8, half), BF)
    ones_s = jnp.ones((8, width), BF)
    vec[16:24, 0:patches_l] = lax.fori_loop(
        0, 2 * count_l, lambda n, total: total + matmul_nt(ones_l, tx_l[n]), jnp.zeros((8, patches_l), F32)
    )
    vec[16:24, half:half + patches_s] = lax.fori_loop(
        0, count_s, lambda n, total: total + matmul_nt(ones_s, tx_s[n]), jnp.zeros((8, patches_s), F32)
    )

    def unmix(kind, j, e, w2, w1, slope, ep, eu, outs, tx, rx, bss, brs):
        for k in range(1, size):
            swap.out(kind, j, me, swap.other(k), tx, e, *outs).wait_recv()
        low = (matmul(w2[...], e[j]) * slope[j].astype(F32)).astype(BF)
        ep[j] = low
        eu[j] = matmul(w1, low).astype(BF)
        for k in range(1, size):
            swap.back(kind, j, me, swap.other(k), eu, rx, bss, brs).start()
        patches, per = (patches_l, per_l) if kind == "l" else (patches_s, per_s)
        rx[me * per + j] = eu[j, swap.rows(me, patches)]

    for j in range(per_l):
        tick()
        unmix("l", j, e_l, w2_l, w_l[0], sl_l, ep_l, eu_l, (out_ss_l, out_rs_l), tx_l, rx_l, bk_ss_l, bk_rs_l)
    tick()
    for j in range(per_s):
        unmix("s", j, e_s, w2_s, w_s[0], sl_s, ep_s, eu_s, (out_ss_s, out_rs_s), tx_s, rx_s, bk_ss_s, bk_rs_s)

    vec[8:16, 0:half] = sum(matmul_nt(ones_l, ep_l[j]) for j in range(per_l))
    vec[8:16, half:width] = sum(matmul_nt(ones_s, ep_s[j]) for j in range(per_s))
    top = 2 * patches_l + 2 * patches_s
    begin = 0
    for left, right, per, patches in (
        (u_l, ep_l, per_l, patches_l), (e_l, h_l, per_l, patches_l),
        (u_s, ep_s, per_s, patches_s), (e_s, h_s, per_s, patches_s),
    ):
        value = sum(matmul_nt(left[j], right[j]) for j in range(per))
        for q in range(size):
            grads[q, begin:begin + patches] = value[q * patches:(q + 1) * patches]
        begin += patches
    for p in range(2):
        tok_tx[p] = grads[p * 2 + 1 - peers.core, 0:top].astype(BF)
    t_core = send(tok_tx, tok_rx, tc_ss.at[0], tc_rs.at[0], core_peer)
    t_core.start()
    tick()
    t_core.wait_recv()
    there = 1 - peers.x
    tokx_tx[...] = (grads[there * 2 + peers.core, 0:top] + tok_rx[there].astype(F32)).astype(BF)
    t_x = send(tokx_tx, tokx_rx, tx_ss.at[0], tx_rs.at[0], x_peer)
    t_x.start()
    if SLAB > top:
        tok_sum[top:SLAB, :] = jnp.zeros((SLAB - top, token), F32)
    tok_sum[0:top, :] = grads[me, 0:top] + tok_rx[peers.x].astype(F32)
    tick()
    tick()

    def piece(place, size):
        return pl.ds(pl.multiple_of(place * size, size), size)

    def arrived(kind, unit, eu, rx, bss, brs):
        per = per_l if kind == "l" else per_s
        owner = unit // per

        @pl.when(owner != me)
        def _():
            swap.back(kind, unit - owner * per, owner, me, eu, rx, bss, brs).wait_recv()

    def norm_back(x, eu, at):
        unit, scale = unit_rows(x.astype(F32))
        d = eu * gain
        m1 = jnp.mean(d, axis=-1, keepdims=True)
        m2 = jnp.mean(d * unit, axis=-1, keepdims=True)
        vec[7:8, :] += jnp.sum(eu * unit, axis=0, keepdims=True)
        vec[9:10, :] += jnp.sum(eu, axis=0, keepdims=True)
        return ey[at, :] + scale * (d - m1 - unit * m2)

    def gx_copy(n):
        at = pl.ds(pl.multiple_of(small_rows + n * patches_l, 16), patches_l)
        return pltpu.make_async_copy(ey.at[at], gx_hbm.at[n], gx_sem.at[n])

    def home_l(n, carry):
        arrived("l", 2 * n, eu_l, rx_l, bk_ss_l, bk_rs_l)
        arrived("l", 2 * n + 1, eu_l, rx_l, bk_ss_l, bk_rs_l)
        at = pl.ds(pl.multiple_of(small_rows + n * patches_l, 16), patches_l)
        eu = jnp.concatenate([rx_l[2 * n], rx_l[2 * n + 1]], axis=1).astype(F32)
        ey[at, :] = norm_back(xl[n], eu, at)
        gx_copy(n).start()
        return carry

    def home_s(n, carry):
        arrived("s", n, eu_s, rx_s, bk_ss_s, bk_rs_s)
        at = pl.ds(pl.multiple_of(n * patches_s, 16), real_s)
        gx_s[n] = norm_back(xs[n], rx_s[n, :real_s].astype(F32), at)
        return carry

    vec[9:10, :] = jnp.zeros((1, width), F32)
    lax.fori_loop(0, count_l // 2, home_l, 0)
    tick()
    lax.fori_loop(count_l // 2, count_l, home_l, 0)
    lax.fori_loop(0, count_s, home_s, 0)
    for n in range(count_s):
        gx_out[:, n, :] = gx_s[n]
    both = vec.at[0:16]
    v_core = send(both, vec_rx.at[0], v_ss.at[0], v_rs.at[0], core_peer)
    v_core.start()
    tick()
    t_x.wait_recv()
    tok_sum[0:top, :] += tokx_rx[...].astype(F32)
    part_n = SLAB // near
    part_f = part_n // far
    t_near, t_far, ta_far, ta_near = [], [], [], []
    if far_inside:
        for j, device in near_peers:
            tokn_tx[j - 1] = tok_sum[piece(lax.rem(peers.near + j, near), part_n), :].astype(BF)
            copy = send(tokn_tx.at[j - 1], tokn_rx.at[j - 1], tn_ss.at[j - 1], tn_rs.at[j - 1], device)
            copy.start()
            t_near.append(copy)
    else:
        tok_out[...] = tok_sum[...].astype(BF)
    v_core.wait()
    vec[0:16, :] += vec_rx[0]
    v_x = send(both, vec_rx.at[1], v_ss.at[1], v_rs.at[1], x_peer)
    v_x.start()
    tick()
    v_x.wait()
    vec[0:16, :] += vec_rx[1]
    v_near = [send(vec, vecn_rx.at[j - 1], vn_ss.at[j - 1], vn_rs.at[j - 1], device) for j, device in near_peers]
    for copy in v_near:
        copy.start()
    if far_inside:
        for copy in t_near:
            copy.wait_recv()
        tok_half[...] = tok_sum[piece(peers.near, part_n), :]
        for j in range(near - 1):
            tok_half[...] += tokn_rx[j].astype(F32)
        for j, device in far_peers:
            tokf_tx[j - 1] = tok_half[piece(lax.rem(peers.far + j, far), part_f), :].astype(BF)
            copy = send(tokf_tx.at[j - 1], tokf_rx.at[j - 1], tf_ss.at[j - 1], tf_rs.at[j - 1], device)
            copy.start()
            t_far.append(copy)
    tick()
    for copy in v_near:
        copy.wait()
    for j in range(near - 1):
        vec[...] += vecn_rx[j]
    v_far = [send(vec, vecf_rx.at[j - 1], vf_ss.at[j - 1], vf_rs.at[j - 1], device) for j, device in far_peers]
    for copy in v_far:
        copy.start()
    if far_inside:
        for copy in t_far:
            copy.wait_recv()
        value = tok_half[piece(peers.far, part_f), :]
        for j in range(far - 1):
            value = value + tokf_rx[j].astype(F32)
        span = tok_out.at[piece(peers.near * far + peers.far, part_f)]
        span[...] = value.astype(BF)
        for j, device in far_peers:
            copy = send(span, span, taf_ss.at[j - 1], taf_rs.at[j - 1], device)
            copy.start()
            ta_far.append(copy)
    tick()
    for copy in v_far:
        copy.wait()
    value = vec[...]
    for j in range(far - 1):
        value = value + vecf_rx[j]
    vec_out[...] = value
    if far_inside:
        for copy in ta_far:
            copy.wait_recv()
        span = tok_out.at[piece(peers.near, part_n)]
        for j, device in near_peers:
            copy = send(span, span, tan_ss.at[j - 1], tan_rs.at[j - 1], device)
            copy.start()
            ta_near.append(copy)
    while waiting:
        tick()
    gather.fourth(groups - 1)
    for k in (groups - 2, groups - 1):
        gather.fifth(k)
    for copy in ta_near:
        copy.wait_recv()

    for copy in [t_core, t_x] + t_near + t_far + ta_far + ta_near:
        copy.wait_send()
    for k in range(1, size):
        there = swap.other(k)
        for j in range(per_l):
            swap.out("l", j, there, me, tx_l, e_l, out_ss_l, out_rs_l).wait_send()
            swap.back("l", j, me, there, eu_l, rx_l, bk_ss_l, bk_rs_l).wait_send()
        for j in range(per_s):
            swap.out("s", j, there, me, tx_s, e_s, out_ss_s, out_rs_s).wait_send()
            swap.back("s", j, me, there, eu_s, rx_s, bk_ss_s, bk_rs_s).wait_send()
    for k in range(groups):
        gather.drain(k)
    for n in range(count_l):
        gx_copy(n).wait()


def backward(chunk, begun, ey, xl, xs, saved, small, gain):
    size = lax.axis_size("blk")
    near, far = img_split(lax.axis_size("img"))
    rows, width = ey.shape
    far_inside = width % (near * far * 2 * 16) == 0
    u_l, u_s, h_l, h_s, sl_l, sl_s, w_l, w_s = saved
    count_l, patches_l, _ = xl.shape
    real_s, count_s, _ = xs.shape
    patches_s = real_s + -real_s % 64
    token = w_l.shape[2]
    half = width // 2
    per_l, per_s = u_l.shape[0], u_s.shape[0]
    groups, each, _ = chunk.shape
    vmem = pl.BlockSpec(memory_space=pltpu.VMEM)
    V = pltpu.VMEM
    DMA = pltpu.SemaphoreType.DMA
    n1, f1 = near - 1, far - 1
    top = 2 * patches_l + 2 * patches_s
    part_n = SLAB // near
    part_f = max(part_n // far, 16)
    return pl.pallas_call(
        functools.partial(backward_kernel, near, far, size, far_inside),
        out_shape=(
            jax.ShapeDtypeStruct(begun.shape, BF),
            jax.ShapeDtypeStruct(xl.shape, F32),
            jax.ShapeDtypeStruct((SLAB, token), BF),
            jax.ShapeDtypeStruct((24, width), F32),
            jax.ShapeDtypeStruct(xs.shape, F32),
        ),
        in_specs=[ANY] * 13 + [vmem] * 2,
        out_specs=(ANY, ANY, vmem, vmem, vmem),
        scratch_shapes=[
            V(xl.shape, BF), V(xs.shape, BF), V(u_l.shape, BF), V(u_s.shape, BF), V(h_l.shape, BF), V(h_s.shape, BF),
            V(sl_l.shape, BF), V(sl_s.shape, BF), V(w_l.shape, BF), V(w_s.shape, BF), DMA((10,)),
            V((count_s, real_s, width), BF), V((count_s, real_s, width), F32),
            V((rows, width), F32),
            V((count_l * 2, patches_l, half), BF), V((count_s, patches_s, width), BF),
            V(u_l.shape, BF), V(u_s.shape, BF),
            V((token, size * patches_l), BF), V((token, size * patches_s), BF),
            V(h_l.shape, BF), V(h_s.shape, BF), V(u_l.shape, BF), V(u_s.shape, BF),
            V((count_l * 2, patches_l, half), BF), V((count_s, patches_s, width), BF),
            V((size, top, token), F32), V((2, top, token), BF), V((2, top, token), BF), V((SLAB, token), F32),
            V((n1, part_n, token), BF), V((n1, part_n, token), BF), V((part_n, token), F32),
            V((f1, part_f, token), BF), V((f1, part_f, token), BF), V((top, token), BF), V((top, token), BF),
            V((24, width), F32), V((2, 16, width), F32), V((n1, 24, width), F32), V((f1, 24, width), F32),
            DMA((1,)), DMA((count_l,)),
            DMA((count_l * 2,)), DMA((count_s,)), DMA((per_l, size)), DMA((per_s, size)),
            DMA((per_l, size)), DMA((per_s, size)), DMA((count_l * 2,)), DMA((count_s,)),
            DMA((1,)), DMA((1,)), DMA((1,)), DMA((1,)), DMA((n1,)), DMA((n1,)), DMA((f1,)), DMA((f1,)),
            DMA((f1,)), DMA((f1,)), DMA((n1,)), DMA((n1,)),
            DMA((2,)), DMA((2,)), DMA((n1,)), DMA((n1,)), DMA((f1,)), DMA((f1,)),
        ] + Gather.sems(groups, near, far),
        input_output_aliases={1: 0},
        compiler_params=pltpu.CompilerParams(
            collective_id=1, has_side_effects=True, vmem_limit_bytes=TOP
        ),
    )(chunk, begun, ey, xl, xs, u_l, u_s, h_l, h_s, sl_l, sl_s, w_l, w_s, small, gain)


def widen_kernel(
    first, second, tok, vec, out_l_in, gx_l_in, out_s_in, gx_s_in,
    out_l, gx_l, out_s, gx_s, out_first, out_second, gain1, bias1, w1_s, b1_s, w2_s, b2_s, w1_l, b1_l, w2_l, b2_l, gain2, bias2, b1, b2,
):
    out_l[...] = out_l_in[...]
    gx_l[...] = gx_l_in[...]
    for k in range(first.shape[1]):
        out_first[:, k * TILE:(k + 1) * TILE] = first[0, k].astype(F32)
        out_second[k * TILE:(k + 1) * TILE, :] = second[0, k].astype(F32).T

    @pl.when(pl.program_id(0) == 0)
    def _():
        out_s[...] = out_s_in[...]
        gx_s[...] = gx_s_in[...]
        width = vec.shape[1]
        half = width // 2
        large, small = w1_l.shape[0], w1_s.shape[0]
        wide = small + -small % 64
        at = 2 * large
        w1_l[...] = tok[0:large, :].astype(F32)
        w2_l[...] = tok[large:at, :].astype(F32)
        w1_s[...] = tok[at:at + wide, :].astype(F32)[:small]
        w2_s[...] = tok[at + wide:at + 2 * wide, :].astype(F32)[:small]
        gain1[...] = vec[7, :]
        bias1[...] = vec[9, :]
        b1_l[...] = vec[8, 0:half]
        b1_s[...] = vec[8, half:width]
        b2_l[...] = vec[16, 0:large]
        b2_s[...] = vec[16, half:half + small]
        gain2[...] = vec[5, :]
        bias2[...] = vec[6, :]
        for k in range(b1.shape[0] // width):
            b1[k * width:(k + 1) * width] = vec[k, :]
        b2[...] = vec[4, :]


def widen(full, tok, vec, out_l, gx_l, out_s, gx_s):
    full = full.reshape(full.shape[0], full.shape[1], -1, TILE)
    _, groups, width, _ = full.shape
    count_l, patches_l, _ = out_l.shape
    patches_s = out_s.shape[0]
    hidden = groups * TILE
    token = tok.shape[1]
    step = 2 * TILE
    shapes = (
        (width,), (width,), (patches_s, token), (token,), (patches_s, token), (patches_s,),
        (patches_l, token), (token,), (patches_l, token), (patches_l,), (width,), (width,), (hidden,), (width,),
    )

    def whole(shape):
        return pl.BlockSpec(shape, lambda i: (0,) * len(shape))

    image = pl.BlockSpec((1, patches_l, width), lambda i: (jnp.minimum(i, count_l - 1), 0, 0))
    return pl.pallas_call(
        widen_kernel,
        grid=(hidden // step,),
        out_shape=tuple(jax.ShapeDtypeStruct(a.shape, a.dtype) for a in (out_l, gx_l, out_s, gx_s)) + (
            jax.ShapeDtypeStruct((width, hidden), F32), jax.ShapeDtypeStruct((hidden, width), F32),
        ) + tuple(jax.ShapeDtypeStruct(shape, F32) for shape in shapes),
        in_specs=[
            pl.BlockSpec((1, 2, width, TILE), lambda i: (0, i, 0, 0)),
            pl.BlockSpec((1, 2, width, TILE), lambda i: (1, i, 0, 0)),
            whole(tok.shape), whole(vec.shape), image, image, whole(out_s.shape), whole(gx_s.shape),
        ],
        out_specs=(
            image, image, whole(out_s.shape), whole(gx_s.shape),
            pl.BlockSpec((width, step), lambda i: (0, i)), pl.BlockSpec((step, width), lambda i: (i, 0)),
        ) + tuple(whole(shape) for shape in shapes),
        compiler_params=pltpu.CompilerParams(vmem_limit_bytes=TOP),
    )(full, full, tok, vec, out_l, gx_l, out_s, gx_s)


def local(
    x_small, x_large, live_counts, ln1_gain, ln1_bias,
    tok_w1_small, tok_b1_small, tok_w2_small, tok_b2_small,
    tok_w1_large, tok_b1_large, tok_w2_large, tok_b2_large,
    ln2_gain, ln2_bias, ch_w1, ch_b1, ch_w2, ch_b2, cot_small, cot_large,
):
    width = x_small.shape[2]
    patches_s, patches_l = x_small.shape[1], x_large.shape[1]
    rows = x_small.shape[0] * (patches_s + -patches_s % 64) + x_large.shape[0] * patches_l
    xs = x_small.transpose(1, 0, 2)
    y, *saved = token_forward(
        x_large, xs, tok_w1_large, tok_w1_small, tok_w2_large.T, tok_w2_small.T,
        tok_b1_large, tok_b1_small, tok_b2_large, tok_b2_small, ln1_gain, ln1_bias, rows + -rows % (3 * LANES),
    )
    out_large, ey, chunk, small_grads, out_small, begun = channel(
        y, live_counts, cot_large, cot_small.transpose(1, 0, 2), ch_w1, ch_w2, ch_b1, ln2_gain, ln2_bias, ch_b2
    )
    near, far = img_split(lax.axis_size("img"))
    far_inside = width % (near * far * 2 * 16) == 0
    if not far_inside:
        same = [[a * near + b for a in range(far)] for b in range(near)]
        chunk = lax.psum(chunk.astype(F32), "img", axis_index_groups=same).astype(BF)
    full, gx_large, tok, vec, gx_small = backward(
        chunk, begun, ey, x_large, xs, saved, small_grads, ln1_gain
    )
    if not far_inside:
        tok = lax.psum(tok.astype(F32), "img")
    (
        out_large, gx_large, out_small, gx_small, grad_ch_w1, grad_ch_w2, gain1, bias1, w1_s, b1_s, w2_s, b2_s, w1_l, b1_l, w2_l, b2_l,
        gain2, bias2, grad_b1, grad_b2,
    ) = widen(full, tok, vec, out_large, gx_large, out_small, gx_small)
    return (
        out_small.transpose(1, 0, 2), out_large, gx_small.transpose(1, 0, 2), gx_large, gain1, bias1,
        w1_s, b1_s, w2_s.T, b2_s, w1_l, b1_l, w2_l.T, b2_l,
        gain2, bias2, grad_ch_w1, grad_b1, grad_ch_w2, grad_b2,
    )


def solution(mesh):
    image = P("img", "blk", None)
    whole = P()
    rows = P("blk", None)
    columns = P(None, "blk")
    vector = P("blk")
    in_specs = (
        image, image, P("img", None), whole, whole,
        rows, whole, columns, vector, rows, whole, columns, vector,
        whole, whole, whole, whole, whole, whole, image, image,
    )
    out_specs = (
        image, image, image, image, whole, whole,
        rows, whole, columns, vector, rows, whole, columns, vector,
        whole, whole, whole, whole, whole, whole,
    )
    return jax.shard_map(local, mesh=mesh, in_specs=in_specs, out_specs=out_specs, check_vma=False)
```

```python
import functools

import jax
import jax.numpy as jnp
from jax import lax
from jax.experimental import pallas as pl
from jax.experimental.pallas import tpu as pltpu
from jax.sharding import PartitionSpec as P

EPSILON = 1e-06
LANES = 128
BF = jnp.bfloat16
F32 = jnp.float32


MESH = pl.DeviceIdType.MESH
ANY = pl.BlockSpec(memory_space=pl.ANY)
TILE = 256
LAGS = (1, 3, 5, 7)
LATE = 3
TOP = 62 * 1024 * 1024


def img_split(size):
    near = 2 if size <= 8 else 8
    return near, size // near


def gelu_pair(a):
    square = a * a
    slope = 0.7978845608028654
    t = jnp.tanh(a * (slope + (slope * 0.044715) * square))
    half = 0.5 + 0.5 * t
    inner = slope + (3.0 * slope * 0.044715) * square
    return a * half, half + (0.5 * a) * (1.0 - t * t) * inner


class Peers:
    def __init__(self, near_count):
        self.img = lax.axis_index("img")
        self.blk = lax.axis_index("blk")
        self.core = lax.rem(self.blk, 2)
        self.x = self.blk // 2
        self.near_count = near_count
        self.near = lax.rem(self.img, near_count)
        self.far = self.img // near_count

    def at(self, axis, place):
        if axis == "core":
            return (self.img, self.x * 2 + place)
        if axis == "x":
            return (self.img, place * 2 + self.core)
        if axis == "near":
            return (self.far * self.near_count + place, self.blk)
        return (place * self.near_count + self.near, self.blk)

    def mine(self, axis):
        return {"core": self.core, "x": self.x, "near": self.near, "far": self.far}[axis]


def greet(peers, axes):
    barrier = pltpu.get_barrier_semaphore()
    total = 0
    for axis, count in axes:
        for j in range(1, count):
            there = lax.rem(peers.mine(axis) + j, count)
            pl.semaphore_signal(barrier, inc=1, device_id=peers.at(axis, there), device_id_type=MESH)
            total += 1
    return total


def greeted(total):
    pl.semaphore_wait(pltpu.get_barrier_semaphore(), total)


class Gather:
    def __init__(self, peers, near, far, far_inside, chunk, full, sems):
        self.peers, self.near, self.far_inside = peers, near, far_inside
        self.f = far if far_inside else 1
        self.chunk, self.full = chunk, full
        self.tiles = chunk.shape[0]
        self.late = self.tiles - LATE if far_inside else self.tiles
        self.own_sem, self.x_ss, self.x_rs, self.f_ss, self.f_rs, self.n_ss, self.n_rs, self.c_ss, self.c_rs = sems
        self.place = (peers.near, peers.far if far_inside else 0, peers.x)

    def span(self, k, axes):
        index = tuple(p if a in axes else slice(None) for p, a in zip(self.place, "nfx"))
        while index and isinstance(index[-1], slice):
            index = index[:-1]
        return self.full.at[(self.peers.core, k) + index]

    def send(self, src, dst, ss, rs, device):
        return pltpu.make_async_remote_copy(
            src_ref=src, dst_ref=dst, send_sem=ss, recv_sem=rs, device_id=device, device_id_type=MESH
        )

    def own(self, k):
        return pltpu.make_async_copy(self.chunk.at[k], self.span(k, "nfx"), self.own_sem.at[k])

    def x_first(self, k):
        there = self.peers.at("x", 1 - self.peers.x)
        return self.send(self.chunk.at[k], self.span(k, "nfx"), self.x_ss.at[k], self.x_rs.at[k], there)

    def x_last(self, k):
        there = self.peers.at("x", 1 - self.peers.x)
        return self.send(self.span(k, "x"), self.span(k, "x"), self.x_ss.at[k], self.x_rs.at[k], there)

    def spread(self, axis, count, span, ss, rs, k):
        copies = []
        for j in range(1, count):
            there = self.peers.at(axis, lax.rem(self.peers.mine(axis) + j, count))
            copies.append(self.send(span, span, ss.at[k, j - 1], rs.at[k, j - 1], there))
        return copies

    def to_far(self, k):
        return self.spread("far", self.f, self.span(k, "nf" if k < self.late else "nfx"), self.f_ss, self.f_rs, k)

    def to_near(self, k):
        return self.spread("near", self.near, self.span(k, "n" if k < self.late else "nx"), self.n_ss, self.n_rs, k)

    def to_core(self, k):
        span = self.span(k, "")
        return self.send(span, span, self.c_ss.at[k], self.c_rs.at[k], self.peers.at("core", 1 - self.peers.core))

    def first(self, k):
        self.own(k).start()

        @pl.when(k < self.late)
        def _():
            self.x_first(k).start()

    def end_first(self, k):
        self.own(k).wait()
        if k < self.late:
            self.x_first(k).wait()

    def second(self, k):
        for copy in self.to_far(k):
            copy.start()

    def third(self, k):
        for copy in self.to_far(k):
            copy.wait_recv()
        for copy in self.to_near(k):
            copy.start()

    def fourth(self, k):
        for copy in self.to_near(k):
            copy.wait_recv()
        (self.to_core(k) if k < self.late else self.x_last(k)).start()

    def fifth(self, k):
        if k >= self.late:
            self.x_last(k).wait_recv()
            self.to_core(k).start()

    def drain(self, k):
        for copy in self.to_far(k) + self.to_near(k):
            copy.wait_send()
        if k >= self.late:
            self.x_last(k).wait_send()
        self.to_core(k).wait()

    @staticmethod
    def sems(groups, near, far):
        DMA = pltpu.SemaphoreType.DMA
        n1, f1 = near - 1, max(far - 1, 1)
        return [DMA((groups,))] * 3 + [DMA((groups, f1))] * 2 + [DMA((groups, n1))] * 2 + [DMA((groups,))] * 2


def row(ref):
    return ref[...].reshape(1, -1)


def column(ref, rows):
    value = jnp.broadcast_to(ref[...].reshape(1, -1), (8, ref.shape[0])).T[:, :1]
    return value if rows == ref.shape[0] else jnp.concatenate([value, jnp.zeros((rows - ref.shape[0], 1), F32)])


def channel_kernel(
    near, far, far_inside,
    y_hbm, live, cot_l, cot_s_in, w1_hbm, w2_hbm, b1_ref, gain_ref, bias_ref, b2_ref,
    out_l, ey_hbm, chunk_ref, small_ref, out_s_t, full_hbm,
    cot_s, out_s, y, ec, v, lt, rt, w1, w2, acc_out, acc_ev, out_low,
    keep, core_tx, core_rx,
    a_keep_n, a_near_tx, a_near_rx, a_keep_f, a_far_tx, a_far_rx, a_keep_x, a_x_tx, a_x_rx,
    b_keep_x, b_x_tx, b_x_rx, b_keep_n, b_near_tx, b_near_rx, b_keep_f, b_far_tx, b_far_rx,
    in_sem, w_sem, out_sem, core_ss, core_rs,
    a_near_ss, a_near_rs, a_far_ss, a_far_rs, a_x_ss, a_x_rs,
    b_near_ss, b_near_rs, b_far_ss, b_far_rs, b_x_ss, b_x_rs, *gather_sems,
):
    rows, width = y.shape
    tiles = w1.shape[0]
    count_l, patches_l, _ = cot_l.shape
    count_s, patches_s, _ = cot_s.shape
    wide_s = patches_s + -patches_s % 64
    small_rows = count_s * wide_s
    peers = Peers(near)
    core = peers.core
    f_place = peers.far if far_inside else 0
    gather = Gather(peers, near, far, far_inside, chunk_ref, full_hbm, gather_sems)
    part = 128
    parts = rows // part
    gain, bias, b2 = row(gain_ref), row(bias_ref), row(b2_ref)

    def w_copies(t):
        return (
            pltpu.make_async_copy(w1_hbm.at[:, pl.ds(t * TILE, TILE)], w1.at[t], w_sem.at[0, t]),
            pltpu.make_async_copy(w2_hbm.at[pl.ds(t * TILE, TILE)], w2.at[t], w_sem.at[1, t]),
        )

    y_in = pltpu.make_async_copy(y_hbm, y, in_sem.at[0])
    y_in.start()

    def start_w(t, carry):
        for copy in w_copies(t):
            copy.start()
        return carry

    lax.fori_loop(0, tiles, start_w, 0)
    axes = [("core", 2), ("near", near)] + ([("far", far)] if far_inside else []) + [("x", 2)]
    greetings = greet(peers, axes)
    small_ref[...] = jnp.zeros_like(small_ref)
    used = small_rows + count_l * patches_l
    ec[0:small_rows, :] = jnp.zeros((small_rows, width), BF)
    if rows > used:
        ec[used:rows, :] = jnp.zeros((rows - used, width), BF)

    def live_l(n):
        return jnp.where(n < live[0, 1], 1.0, 0.0).astype(F32)

    def live_s(n):
        return jnp.where(n < live[0, 0], 1.0, 0.0).astype(F32)

    def mask_l(n, carry):
        ec[pl.ds(pl.multiple_of(small_rows + n * patches_l, 16), patches_l), :] = (
            cot_l[n].astype(F32) * live_l(n)
        ).astype(BF)
        return carry

    def mask_s(n, carry):
        ec[pl.ds(pl.multiple_of(n * wide_s, 16), patches_s), :] = (cot_s[n].astype(F32) * live_s(n)).astype(BF)
        return carry

    lax.fori_loop(0, count_l, mask_l, 0)
    for n in range(count_s):
        cot_s[n] = cot_s_in[:, n, :]
    lax.fori_loop(0, count_s, mask_s, 0)
    y_in.wait()

    def prepare(p, carry):
        at = pl.ds(pl.multiple_of(p * part, part), part)
        unit, _ = unit_rows(y[at, :])
        low = (unit * gain + bias).astype(BF)
        v[at, :] = low
        lt[0, :, at] = low.T
        own = ec[at, :]
        lt[1, :, at] = own.T
        small_ref[4:5, :] += jnp.sum(own.astype(F32), axis=0, keepdims=True)
        acc_out[at, :] = jnp.zeros((part, width), F32)
        acc_ev[at, :] = jnp.zeros((part, width), F32)
        return carry

    lax.fori_loop(0, parts, prepare, 0)
    greeted(greetings)

    def send(src, dst, ss, rs, device):
        return pltpu.make_async_remote_copy(
            src_ref=src, dst_ref=dst, send_sem=ss, recv_sem=rs, device_id=device, device_id_type=MESH
        )

    def core_copy(t):
        slot = lax.rem(t, 2)
        return send(core_tx.at[slot], core_rx.at[t], core_ss.at[slot], core_rs.at[t], peers.at("core", 1 - core))

    def spread(tx, rx, ss, rs, axis, count, i):
        slot = lax.rem(i, 2)
        copies = []
        for j in range(1, count):
            there = lax.rem(peers.mine(axis) + j, count)
            copies.append(
                send(tx.at[slot, j - 1], rx.at[i, j - 1], ss.at[slot, j - 1], rs.at[i, j - 1], peers.at(axis, there))
            )
        return copies

    f = far if far_inside else 1
    a_near = lambda i: spread(a_near_tx, a_near_rx, a_near_ss, a_near_rs, "near", near, i)
    a_far = lambda i: spread(a_far_tx, a_far_rx, a_far_ss, a_far_rs, "far", f, i)
    a_x = lambda i: spread(a_x_tx, a_x_rx, a_x_ss, a_x_rs, "x", 2, i)
    b_near = lambda i: spread(b_near_tx, b_near_rx, b_near_ss, b_near_rs, "near", near, i)
    b_far = lambda i: spread(b_far_tx, b_far_rx, b_far_ss, b_far_rs, "far", f, i)
    b_x = lambda i: spread(b_x_tx, b_x_rx, b_x_ss, b_x_rs, "x", 2, i)
    each = width // near // f // 2

    def tile_step(t):
        for copy in w_copies(t):
            copy.wait()

        @pl.when(t >= 2)
        def _():
            core_copy(t - 2).wait_send()

        slot = lax.rem(t, 2)
        columns = pl.ds(pl.multiple_of(t * TILE, TILE), TILE)
        a = matmul(v[...], w1[t]) + b1_ref[columns].reshape(1, -1)
        gh = matmul_nt(ec[...], w2[t])
        g, slope = gelu_pair(a)
        ea = (slope * gh).astype(BF)
        rt[1] = g.astype(BF)
        rt[0] = ea
        per = width // TILE
        small_ref[lax.div(t, per), pl.ds(pl.multiple_of(lax.rem(t, per) * TILE, TILE), TILE)] = jnp.sum(
            ea.astype(F32), axis=0
        )
        core_tx[slot] = matmul(lt[1 - core], rt[1 - core]).astype(BF).reshape(near, f, 2, each, TILE)
        keep[slot] = matmul(lt[core], rt[core]).reshape(near, f, 2, each, TILE)
        acc_out[...] += matmul(rt[1], w2[t])
        acc_ev[...] += matmul_nt(rt[0], w1[t])
        core_copy(t).start()

    def ey_copy(at, n):
        return pltpu.make_async_copy(acc_ev.at[at], ey_hbm.at[at], out_sem.at[n])

    def at_l(n):
        return pl.ds(pl.multiple_of(small_rows + n * patches_l, 16), patches_l)

    def at_s(n):
        return pl.ds(pl.multiple_of(n * wide_s, 16), wide_s)

    def out_copy(n):
        return pltpu.make_async_copy(out_low.at[n], out_l.at[n], out_sem.at[count_l + count_s + n])

    def finish_rows(at, live_here):
        here = y[at, :]
        result = ((here + acc_out[at, :] + b2) * live_here).astype(BF)
        unit, scale = unit_rows(here)
        ev = acc_ev[at, :]
        small_ref[5:6, :] += jnp.sum(ev * unit, axis=0, keepdims=True)
        small_ref[6:7, :] += jnp.sum(ev, axis=0, keepdims=True)
        d = ev * gain
        m1 = jnp.mean(d, axis=-1, keepdims=True)
        m2 = jnp.mean(d * unit, axis=-1, keepdims=True)
        acc_ev[at, :] = ec[at, :].astype(F32) + scale * (d - m1 - unit * m2)
        return result

    def finish(p):
        def one_l(q, carry):
            n = p + q * 4

            @pl.when(n < count_l)
            def _():
                out_low[n] = finish_rows(at_l(n), live_l(n))
                ey_copy(at_l(n), n).start()
                out_copy(n).start()

            return carry

        def one_s(q, carry):
            n = p + q * 4

            @pl.when(n < count_s)
            def _():
                out_s[n] = finish_rows(at_s(n), live_s(n))[:patches_s]
                ey_copy(at_s(n), count_l + n).start()

            return carry

        lax.fori_loop(0, pl.cdiv(count_l, 4), one_l, 0)
        lax.fori_loop(0, pl.cdiv(count_s, 4), one_s, 0)

    def free(copies, i):
        @pl.when(i >= 2)
        def _():
            for copy in copies(i - 2):
                copy.wait_send()

    def reduce(value, axis, count, place, tx, own, copies, i):
        slot = lax.rem(i, 2)
        free(copies, i)
        made = copies(i)
        for j in range(1, count + 1):
            there = lax.rem(place + j, count)
            piece = value(there)
            if j < count:
                tx[slot, j - 1] = piece.astype(BF)
                made[j - 1].start()
            else:
                own(slot, piece)

    def arrivals(copies, i):
        for copy in copies(i):
            copy.wait_recv()

    def save(ref):
        def put(slot, piece):
            ref[slot] = piece
        return put

    def plus(base, rx, i, count, index):
        value = base
        for k in range(count - 1):
            value = value + rx[(i, k) + index].astype(F32)
        return value

    def chunk_out(t, value):
        chunk_ref[t] = value.astype(BF)
        if far_inside:
            gather.first(t)

    def even_core(t):
        i = lax.div(t, 2)
        core_copy(t).wait_recv()
        reduce(
            lambda p: keep[0, p] + core_rx[t, p].astype(F32),
            "near", near, peers.near, a_near_tx, save(a_keep_n), a_near, i,
        )

    def even_near(t):
        i = lax.div(t, 2)
        slot = lax.rem(i, 2)
        arrivals(a_near, i)
        reduce(
            lambda p: plus(a_keep_n[slot, p], a_near_rx, i, near, (p,)),
            "far", f, f_place, a_far_tx, save(a_keep_f), a_far, i,
        )

    def even_far(t):
        i = lax.div(t, 2)
        slot = lax.rem(i, 2)
        arrivals(a_far, i)
        reduce(
            lambda p: plus(a_keep_f[slot, p], a_far_rx, i, f, (p,)),
            "x", 2, peers.x, a_x_tx, save(a_keep_x), a_x, i,
        )

    def even_x(t):
        i = lax.div(t, 2)
        arrivals(a_x, i)
        chunk_out(t, a_keep_x[lax.rem(i, 2)] + a_x_rx[i, 0].astype(F32))

    def odd_core(t):
        i = lax.div(t, 2)
        core_copy(t).wait_recv()
        reduce(
            lambda p: keep[1, :, :, p] + core_rx[t, :, :, p].astype(F32),
            "x", 2, peers.x, b_x_tx, save(b_keep_x), b_x, i,
        )

    def odd_x(t):
        i = lax.div(t, 2)
        slot = lax.rem(i, 2)
        arrivals(b_x, i)
        reduce(
            lambda p: plus(b_keep_x[slot, p], b_x_rx, i, 2, (p,)),
            "near", near, peers.near, b_near_tx, save(b_keep_n), b_near, i,
        )

    def odd_near(t):
        i = lax.div(t, 2)
        slot = lax.rem(i, 2)
        arrivals(b_near, i)
        reduce(
            lambda p: plus(b_keep_n[slot, p], b_near_rx, i, near, (p,)),
            "far", f, f_place, b_far_tx, save(b_keep_f), b_far, i,
        )

    def odd_far(t):
        i = lax.div(t, 2)
        arrivals(b_far, i)
        slot = lax.rem(i, 2)
        chunk_out(t, plus(b_keep_f[slot], b_far_rx, i, f, ()))

    stages = ((even_core, even_near, even_far, even_x), (odd_core, odd_x, odd_near, odd_far))

    def pair(s2, carry):
        for parity in range(2):
            s = s2 * 2 + parity

            @pl.when(s < tiles)
            def _():
                tile_step(s)

            for place, lag in enumerate(LAGS):
                t = s - lag
                stage = stages[(parity - lag) % 2][place]

                @pl.when((t >= 0) & (t < tiles))
                def _(t=t, stage=stage):
                    stage(t)

            @pl.when((s >= tiles) & (s < tiles + 4))
            def _():
                finish(s - tiles)

        return carry

    lax.fori_loop(0, (tiles + LAGS[-1] + 1) // 2, pair, 0)
    if far_inside:
        for k in range(tiles):
            gather.end_first(k)
    for t in (tiles - 2, tiles - 1):
        core_copy(t).wait_send()
    for copies in (a_near, a_far, a_x, b_near, b_far, b_x):
        for i in (tiles // 2 - 2, tiles // 2 - 1):
            for copy in copies(i):
                copy.wait_send()
    for n in range(count_s):
        out_s_t[:, n, :] = out_s[n]
    for n in range(count_l):
        ey_copy(at_l(n), n).wait()
        out_copy(n).wait()
    for n in range(count_s):
        ey_copy(at_s(n), count_l + n).wait()


def channel(y, live, cot_l, cot_s, w1, w2, b1, gain, bias, b2):
    rows, width = y.shape
    hidden = w1.shape[1]
    tiles = hidden // TILE
    near, far = img_split(lax.axis_size("img"))
    far_inside = width % (near * far * 2 * 16) == 0
    f = far if far_inside else 1
    chunk = width // near // f // 2
    vmem = pl.BlockSpec(memory_space=pltpu.VMEM)
    V = pltpu.VMEM
    DMA = pltpu.SemaphoreType.DMA
    fm = max(f - 1, 1)
    nm = near - 1
    pairs = tiles // 2
    real_s, count_s, _ = cot_s.shape
    count = cot_l.shape[0] + count_s
    return pl.pallas_call(
        functools.partial(channel_kernel, near, far, far_inside),
        out_shape=(
            jax.ShapeDtypeStruct(cot_l.shape, BF),
            jax.ShapeDtypeStruct((rows, width), F32),
            jax.ShapeDtypeStruct((tiles, chunk, TILE), BF),
            jax.ShapeDtypeStruct((8, width), F32),
            jax.ShapeDtypeStruct(cot_s.shape, BF),
            jax.ShapeDtypeStruct((2, tiles, near, f, 2, chunk, TILE), BF),
        ),
        in_specs=[ANY, pl.BlockSpec(memory_space=pltpu.SMEM), vmem, vmem, ANY, ANY] + [vmem] * 4,
        out_specs=(ANY, ANY, vmem, vmem, vmem, ANY),
        scratch_shapes=[
            V((count_s, real_s, width), BF), V((count_s, real_s, width), BF),
            V((rows, width), F32), V((rows, width), BF), V((rows, width), BF),
            V((2, width, rows), BF), V((2, rows, TILE), BF),
            V((tiles, width, TILE), BF), V((tiles, TILE, width), BF),
            V((rows, width), F32), V((rows, width), F32), V(cot_l.shape, BF),
            V((2, near, f, 2, chunk, TILE), F32), V((2, near, f, 2, chunk, TILE), BF),
            V((tiles, near, f, 2, chunk, TILE), BF),
            V((2, f, 2, chunk, TILE), F32), V((2, nm, f, 2, chunk, TILE), BF), V((pairs, nm, f, 2, chunk, TILE), BF),
            V((2, 2, chunk, TILE), F32), V((2, fm, 2, chunk, TILE), BF), V((pairs, fm, 2, chunk, TILE), BF),
            V((2, chunk, TILE), F32), V((2, 1, chunk, TILE), BF), V((pairs, 1, chunk, TILE), BF),
            V((2, near, f, chunk, TILE), F32), V((2, 1, near, f, chunk, TILE), BF),
            V((pairs, 1, near, f, chunk, TILE), BF),
            V((2, f, chunk, TILE), F32), V((2, nm, f, chunk, TILE), BF), V((pairs, nm, f, chunk, TILE), BF),
            V((2, chunk, TILE), F32), V((2, fm, chunk, TILE), BF), V((pairs, fm, chunk, TILE), BF),
            DMA((1,)), DMA((2, tiles)), DMA((2 * count,)), DMA((2,)), DMA((tiles,)),
            DMA((2, nm)), DMA((pairs, nm)), DMA((2, fm)), DMA((pairs, fm)), DMA((2, 1)), DMA((pairs, 1)),
            DMA((2, nm)), DMA((pairs, nm)), DMA((2, fm)), DMA((pairs, fm)), DMA((2, 1)), DMA((pairs, 1)),
        ] + Gather.sems(tiles, near, f),
        compiler_params=pltpu.CompilerParams(
            collective_id=0, has_side_effects=True, vmem_limit_bytes=TOP
        ),
    )(y, live, cot_l, cot_s, w1, w2, b1, gain, bias, b2)


NT = (((1,), (1,)), ((), ()))


def matmul(left, right):
    return jnp.dot(left, right, preferred_element_type=F32)


def matmul_nt(left, right):
    return lax.dot_general(left, right, NT, preferred_element_type=F32)


class Swap:
    def __init__(self, peers, size, per_l, per_s, patches_l, patches_s):
        self.peers, self.size = peers, size
        self.per_l, self.per_s = per_l, per_s
        self.pl, self.ps = patches_l, patches_s

    def other(self, step):
        return lax.rem(self.peers.blk + step, self.size)

    def copy(self, src, dst, ss, rs, place):
        return pltpu.make_async_remote_copy(
            src_ref=src, dst_ref=dst, send_sem=ss, recv_sem=rs,
            device_id=(self.peers.img, place), device_id_type=MESH,
        )

    def rows(self, place, patches):
        return pl.ds(pl.multiple_of(place * patches, patches), patches)

    def out(self, kind, j, place, source, tx, cols, ss, rs):
        per, patches = (self.per_l, self.pl) if kind == "l" else (self.per_s, self.ps)
        unit = place * per + j
        return self.copy(
            tx.at[unit], cols.at[j, self.rows(source, patches)], ss.at[unit], rs.at[j, source], place
        )

    def back(self, kind, j, owner, place, cols, rx, ss, rs):
        per, patches = (self.per_l, self.pl) if kind == "l" else (self.per_s, self.ps)
        unit = owner * per + j
        return self.copy(
            cols.at[j, self.rows(place, patches)], rx.at[unit], ss.at[j, place], rs.at[unit], place
        )


def greet_all(peers, size, near, far):
    barrier = pltpu.get_barrier_semaphore()
    total = 0
    for j in range(1, size):
        there = lax.rem(peers.blk + j, size)
        pl.semaphore_signal(barrier, inc=1, device_id=(peers.img, there), device_id_type=MESH)
        total += 1
    for axis, count in (("near", near), ("far", far)):
        for j in range(1, count):
            there = lax.rem(peers.mine(axis) + j, count)
            pl.semaphore_signal(barrier, inc=1, device_id=peers.at(axis, there), device_id_type=MESH)
            total += 1
    return total


def unit_rows(row):
    mean = jnp.mean(row, axis=-1, keepdims=True)
    centered = row - mean
    var = jnp.mean(centered * centered, axis=-1, keepdims=True)
    scale = lax.rsqrt(var + EPSILON)
    return centered * scale, scale


def weights_shared(near, far, patches_l, patches_s):
    if near != 2 or far < 2 or patches_l % (16 * (far - 1)):
        return False
    return patches_l // (far - 1) <= patches_s


def token_kernel(
    near, far, size,
    xl, xs_in, w1_l, w1_s, w2_l, w2_s, b1_l_ref, b1_s_ref, b2_l_ref, b2_s_ref, gain_ref, bias_ref,
    y_hbm, u_l, u_s, h_l, h_s, sl_l, sl_s, w_l, w_s,
    xs, wq, mine_w, theirs_w, tx_l, tx_s, w1t_l, w1t_s, m_l, m_s, rx_l, rx_s, y,
    y_sem, own_sem, wown, w_ss, w_rs, out_ss_l, out_ss_s, out_rs_l, out_rs_s, bk_ss_l, bk_ss_s, bk_rs_l, bk_rs_s,
    sx_sem, sf_ss, sf_rs, sn_ss, sn_rs, sc_sem,
):
    peers = Peers(near)
    me = peers.blk
    count_l, patches_l, width = xl.shape
    count_s, real_s, _ = xs.shape
    patches_s = tx_s.shape[1]
    token = w1_l.shape[1]
    half = width // 2
    per_l, per_s = count_l * 2 // size, count_s // size
    swap = Swap(peers, size, per_l, per_s, patches_l, patches_s)
    shared = weights_shared(near, far, patches_l, patches_s)
    total = patches_l + patches_s
    for k, (large, small) in enumerate(((w1_l, w1_s), (w2_l, w2_s))):
        wq[k, :patches_l] = large[...]
        wq[k, patches_l:] = jnp.zeros((patches_s, token), BF)
        wq[k, patches_l:patches_l + real_s] = small[...]
    wq_l = wq.at[:, pl.ds(0, patches_l)]
    wq_s = wq.at[:, pl.ds(patches_l, patches_s)]

    greetings = greet_all(peers, size, near if shared else 1, far if shared else 1)

    def weights(src_l, src_s, quarter, n, place):
        return (
            swap.copy(src_l, w_l.at[:, swap.rows(quarter, patches_l)], w_ss.at[n, 0], w_rs.at[n, 0], place),
            swap.copy(src_s, w_s.at[:, swap.rows(quarter, patches_s)], w_ss.at[n, 1], w_rs.at[n, 1], place),
        )

    x_peer = (1 - peers.x) * 2 + peers.core
    core_peer = peers.x * 2 + 1 - peers.core
    diagonal = (1 - peers.x) * 2 + 1 - peers.core
    if shared:
        stride = patches_l // (far - 1)

        def share(src, dst, ss, rs, device):
            return pltpu.make_async_remote_copy(
                src_ref=src, dst_ref=dst, send_sem=ss, recv_sem=rs, device_id=device, device_id_type=MESH
            )

        n, f = peers.near, peers.far
        first = pl.ds(pl.multiple_of(f * stride, 16), patches_s)
        over_x = share(wq.at[n, first], mine_w.at[n, f], sx_sem.at[0], sx_sem.at[1], (peers.img, x_peer))
        over_far = [
            share(
                mine_w.at[n, f], mine_w.at[n, f], sf_ss.at[j - 1], sf_rs.at[j - 1],
                peers.at("far", lax.rem(f + j, far)),
            )
            for j in range(1, far)
        ]
        over_near = share(mine_w.at[n], mine_w.at[n], sn_ss.at[0], sn_rs.at[0], peers.at("near", 1 - n))
        over_core = share(mine_w, theirs_w, sc_sem.at[0], sc_sem.at[1], (peers.img, core_peer))
    to_x = (over_x,) if shared else weights(wq_l, wq_s, me, 0, x_peer)
    to_core = weights(wq_l, wq_s, me, 1, core_peer)
    relay = () if shared else weights(
        w_l.at[:, swap.rows(x_peer, patches_l)], w_s.at[:, swap.rows(x_peer, patches_s)], x_peer, 2, core_peer
    )
    own_w = (
        pltpu.make_async_copy(wq_l, w_l.at[:, swap.rows(me, patches_l)], wown.at[0]),
        pltpu.make_async_copy(wq_s, w_s.at[:, swap.rows(me, patches_s)], wown.at[1]),
    )
    for copy in own_w:
        copy.start()

    gain, bias = row(gain_ref), row(bias_ref)

    def norm(values):
        unit, _ = unit_rows(values.astype(F32))
        return (unit * gain + bias).astype(BF)

    def norm_l(n, carry):
        u = norm(xl[n])
        tx_l[2 * n] = u[:, :half]
        tx_l[2 * n + 1] = u[:, half:]
        return carry


    def norm_s(n, carry):
        tx_s[n, :real_s] = norm(xs[n])
        return carry

    lax.fori_loop(0, count_l, norm_l, 0)
    greeted(greetings)
    for copy in to_x + to_core:
        copy.start()
    for j in range(per_l):
        for k in range(1, size):
            swap.out("l", j, swap.other(k), me, tx_l, u_l, out_ss_l, out_rs_l).start()
    tx_s[...] = jnp.zeros_like(tx_s)
    for n in range(count_s):
        xs[n] = xs_in[:, n, :]
    lax.fori_loop(0, count_s, norm_s, 0)
    for j in range(per_s):
        for k in range(1, size):
            swap.out("s", j, swap.other(k), me, tx_s, u_s, out_ss_s, out_rs_s).start()
    for j in range(per_l):
        u_l[j, swap.rows(me, patches_l)] = tx_l[me * per_l + j]
    for j in range(per_s):
        u_s[j, swap.rows(me, patches_s)] = tx_s[me * per_s + j]

    for copy in to_x:
        copy.wait_recv()
    for copy in relay:
        copy.start()
    for copy in own_w:
        copy.wait()
    if shared:
        for copy in over_far:
            copy.start()
        for copy in over_far:
            copy.wait_recv()
        over_near.start()
        over_near.wait_recv()
        over_core.start()
        over_core.wait_recv()
        for k in range(2):
            for pieces, quarter in ((mine_w, x_peer), (theirs_w, diagonal)):
                for p in range(far - 1):
                    at = pl.ds(pl.multiple_of(quarter * patches_l + p * stride, 16), stride)
                    w_l[k, at] = pieces[k, p, :stride]
                w_s[k, swap.rows(quarter, patches_s)] = pieces[k, far - 1]
    for copy in to_core + relay:
        copy.wait_recv()
    b1_l, b1_s = column(b1_l_ref, token), column(b1_s_ref, token)
    b2_l, b2_s = column(b2_l_ref, patches_l), column(b2_s_ref, real_s)
    w1t_l[...] = w_l[0].T
    w1t_s[...] = w_s[0].T

    def mix(kind, j, cols, w1t, w2t, b1, h, slope, m, outs, tx, rx, bss, brs):
        for k in range(1, size):
            source = swap.other(k)
            swap.out(kind, j, me, source, tx, cols, *outs).wait_recv()
        g, d = gelu_pair(matmul(w1t[...], cols[j]) + b1)
        low = g.astype(BF)
        h[j] = low
        slope[j] = d.astype(BF)
        m[j] = matmul(w2t, low).astype(BF)
        for k in range(1, size):
            swap.back(kind, j, me, swap.other(k), m, rx, bss, brs).start()
        patches, per = (patches_l, per_l) if kind == "l" else (patches_s, per_s)
        rx[me * per + j] = m[j, swap.rows(me, patches)]

    for j in range(per_l):
        mix("l", j, u_l, w1t_l, w_l[1], b1_l, h_l, sl_l, m_l, (out_ss_l, out_rs_l), tx_l, rx_l, bk_ss_l, bk_rs_l)
    for j in range(per_s):
        mix("s", j, u_s, w1t_s, w_s[1], b1_s, h_s, sl_s, m_s, (out_ss_s, out_rs_s), tx_s, rx_s, bk_ss_s, bk_rs_s)

    small_rows = count_s * patches_s
    rows = y.shape[0]
    used = small_rows + count_l * patches_l
    y[0:small_rows, :] = jnp.zeros((small_rows, width), F32)
    if rows > used:
        y[used:rows, :] = jnp.zeros((rows - used, width), F32)

    def arrived(kind, unit, m, rx, bss, brs):
        per = per_l if kind == "l" else per_s
        owner = unit // per

        @pl.when(owner != me)
        def _():
            swap.back(kind, unit - owner * per, owner, me, m, rx, bss, brs).wait_recv()

    def home_l(n, carry):
        arrived("l", 2 * n, m_l, rx_l, bk_ss_l, bk_rs_l)
        arrived("l", 2 * n + 1, m_l, rx_l, bk_ss_l, bk_rs_l)
        at = pl.ds(pl.multiple_of(small_rows + n * patches_l, 16), patches_l)
        y[at, :half] = xl[n, :, :half].astype(F32) + rx_l[2 * n].astype(F32) + b2_l
        y[at, half:] = xl[n, :, half:].astype(F32) + rx_l[2 * n + 1].astype(F32) + b2_l
        return carry

    def home_s(n, carry):
        arrived("s", n, m_s, rx_s, bk_ss_s, bk_rs_s)
        at = pl.ds(pl.multiple_of(n * patches_s, 16), real_s)
        y[at, :] = xs[n].astype(F32) + rx_s[n, :real_s].astype(F32) + b2_s
        return carry

    lax.fori_loop(0, count_l, home_l, 0)
    lax.fori_loop(0, count_s, home_s, 0)
    y_out = pltpu.make_async_copy(y, y_hbm, y_sem.at[0])
    y_out.start()
    for copy in to_x + to_core + relay:
        copy.wait_send()
    if shared:
        for copy in over_far + [over_near, over_core]:
            copy.wait_send()
    for k in range(1, size):
        there = swap.other(k)
        for j in range(per_l):
            swap.out("l", j, there, me, tx_l, u_l, out_ss_l, out_rs_l).wait_send()
            swap.back("l", j, me, there, m_l, rx_l, bk_ss_l, bk_rs_l).wait_send()
        for j in range(per_s):
            swap.out("s", j, there, me, tx_s, u_s, out_ss_s, out_rs_s).wait_send()
            swap.back("s", j, me, there, m_s, rx_s, bk_ss_s, bk_rs_s).wait_send()
    y_out.wait()


def token_forward(xl, xs, w1_l, w1_s, w2_l, w2_s, b1_l, b1_s, b2_l, b2_s, gain, bias, rows):
    size = lax.axis_size("blk")
    near, far = img_split(lax.axis_size("img"))
    count_l, patches_l, width = xl.shape
    real_s, count_s, _ = xs.shape
    patches_s = real_s + -real_s % 64
    token = w1_l.shape[1]
    half = width // 2
    per_l, per_s = count_l * 2 // size, count_s // size
    vmem = pl.BlockSpec(memory_space=pltpu.VMEM)
    V = pltpu.VMEM
    DMA = pltpu.SemaphoreType.DMA
    low = lambda *shape: jax.ShapeDtypeStruct(shape, BF)
    return pl.pallas_call(
        functools.partial(token_kernel, near, far, size),
        out_shape=(
            jax.ShapeDtypeStruct((rows, width), F32),
            low(per_l, size * patches_l, half), low(per_s, size * patches_s, width),
            low(per_l, token, half), low(per_s, token, width),
            low(per_l, token, half), low(per_s, token, width),
            low(2, size * patches_l, token), low(2, size * patches_s, token),
        ),
        in_specs=[vmem] * 12,
        out_specs=(ANY,) + (vmem,) * 8,
        scratch_shapes=[
            V((count_s, real_s, width), BF), V((2, patches_l + patches_s, token), BF),
            V((2, far, patches_s, token), BF), V((2, far, patches_s, token), BF),
            V((count_l * 2, patches_l, half), BF), V((count_s, patches_s, width), BF),
            V((token, size * patches_l), BF), V((token, size * patches_s), BF),
            V((per_l, size * patches_l, half), BF), V((per_s, size * patches_s, width), BF),
            V((count_l * 2, patches_l, half), BF), V((count_s, patches_s, width), BF),
            V((rows, width), F32),
            DMA((1,)), DMA((1,)), DMA((2,)), DMA((3, 2)), DMA((3, 2)),
            DMA((count_l * 2,)), DMA((count_s,)), DMA((per_l, size)), DMA((per_s, size)),
            DMA((per_l, size)), DMA((per_s, size)), DMA((count_l * 2,)), DMA((count_s,)),
            DMA((2,)), DMA((far - 1,)), DMA((far - 1,)), DMA((1,)), DMA((1,)), DMA((2,)),
        ],
        compiler_params=pltpu.CompilerParams(
            collective_id=2, has_side_effects=True, vmem_limit_bytes=TOP
        ),
    )(xl, xs, w1_l, w1_s, w2_l, w2_s, b1_l, b1_s, b2_l, b2_s, gain, bias)


DEPTH = 3
SLAB = 512


def backward_kernel(
    near, far, size, far_inside,
    chunk_hbm, begun_hbm, ey_hbm,
    xl_in, xs_in, u_l_in, u_s_in, h_l_in, h_s_in, sl_l_in, sl_s_in, w_l_in, w_s_in, small_in, gain_ref,
    full_hbm, gx_hbm, tok_out, vec_out, gx_out,
    xl, xs_in_v, u_l, u_s, h_l, h_s, sl_l, sl_s, w_l, w_s, in_sem, xs, gx_s,
    ey, tx_l, tx_s, e_l, e_s, w2_l, w2_s, ep_l, ep_s, eu_l, eu_s, rx_l, rx_s,
    grads, tok_tx, tok_rx, tok_sum, tokn_tx, tokn_rx, tok_half, tokf_tx, tokf_rx, tokx_tx, tokx_rx,
    vec, vec_rx, vecn_rx, vecf_rx,
    ey_sem, gx_sem,
    out_ss_l, out_ss_s, out_rs_l, out_rs_s, bk_ss_l, bk_ss_s, bk_rs_l, bk_rs_s,
    tc_ss, tc_rs, tx_ss, tx_rs, tn_ss, tn_rs, tf_ss, tf_rs, taf_ss, taf_rs, tan_ss, tan_rs,
    v_ss, v_rs, vn_ss, vn_rs, vf_ss, vf_rs, *gather_sems,
):
    peers = Peers(near)
    me = peers.blk
    count_l, patches_l, width = xl.shape
    count_s, real_s, _ = xs.shape
    patches_s = tx_s.shape[1]
    token = w_l.shape[2]
    gain = row(gain_ref)
    half = width // 2
    per_l, per_s = count_l * 2 // size, count_s // size
    swap = Swap(peers, size, per_l, per_s, patches_l, patches_s)
    small_rows = count_s * patches_s
    x_peer = peers.at("x", 1 - peers.x)
    core_peer = peers.at("core", 1 - peers.core)

    def send(src, dst, ss, rs, device):
        return pltpu.make_async_remote_copy(
            src_ref=src, dst_ref=dst, send_sem=ss, recv_sem=rs, device_id=device, device_id_type=MESH
        )

    def others(axis, count):
        return [(j, peers.at(axis, lax.rem(peers.mine(axis) + j, count))) for j in range(1, count)]

    near_peers = others("near", near)
    far_peers = others("far", far)

    groups = chunk_hbm.shape[0]
    gather = Gather(peers, near, far, far_inside, chunk_hbm, full_hbm, gather_sems)
    waiting = list(range(groups))

    def tick():
        if waiting:
            k = waiting.pop(0)
            gather.third(k)
            if k + DEPTH < groups:
                gather.second(k + DEPTH)
            if k > 0:
                gather.fourth(k - 1)
            if k > 1:
                gather.fifth(k - 2)

    ey_in = pltpu.make_async_copy(ey_hbm, ey, ey_sem.at[0])
    ey_in.start()
    inputs = [
        pltpu.make_async_copy(src, dst, in_sem.at[n])
        for n, (src, dst) in enumerate((
            (w_l_in, w_l), (w_s_in, w_s), (sl_l_in, sl_l), (sl_s_in, sl_s), (u_l_in, u_l), (u_s_in, u_s),
            (h_l_in, h_l), (h_s_in, h_s), (xl_in, xl), (xs_in, xs_in_v),
        ))
    ]
    for copy in inputs:
        copy.start()
    greeted(greet_all(peers, size, near, far))
    if not far_inside:
        for k in range(groups):
            gather.first(k)
        for k in range(groups):
            gather.end_first(k)
    for k in range(DEPTH):
        gather.second(k)
    ey_in.wait()
    vec[...] = jnp.zeros_like(vec)
    vec[0:8, :] = small_in[...]
    def cast_l(n, carry):
        at = pl.ds(pl.multiple_of(small_rows + n * patches_l, 16), patches_l)
        et = ey[at, :].astype(BF)
        tx_l[2 * n] = et[:, :half]
        tx_l[2 * n + 1] = et[:, half:]
        return carry

    def cast_s(n, carry):
        at = pl.ds(pl.multiple_of(n * patches_s, 16), patches_s)
        tx_s[n] = ey[at, :].astype(BF)
        return carry

    lax.fori_loop(0, count_l, cast_l, 0)
    for j in range(per_l):
        for k in range(1, size):
            swap.out("l", j, swap.other(k), me, tx_l, e_l, out_ss_l, out_rs_l).start()
    lax.fori_loop(0, count_s, cast_s, 0)
    for j in range(per_s):
        for k in range(1, size):
            swap.out("s", j, swap.other(k), me, tx_s, e_s, out_ss_s, out_rs_s).start()
    for j in range(per_l):
        e_l[j, swap.rows(me, patches_l)] = tx_l[me * per_l + j]
    for j in range(per_s):
        e_s[j, swap.rows(me, patches_s)] = tx_s[me * per_s + j]
    for copy in inputs:
        copy.wait()
    for n in range(count_s):
        xs[n] = xs_in_v[:, n, :]
    w2_l[...] = w_l[1].T
    w2_s[...] = w_s[1].T
    ones_l = jnp.ones((8, half), BF)
    ones_s = jnp.ones((8, width), BF)
    vec[16:24, 0:patches_l] = lax.fori_loop(
        0, 2 * count_l, lambda n, total: total + matmul_nt(ones_l, tx_l[n]), jnp.zeros((8, patches_l), F32)
    )
    vec[16:24, half:half + patches_s] = lax.fori_loop(
        0, count_s, lambda n, total: total + matmul_nt(ones_s, tx_s[n]), jnp.zeros((8, patches_s), F32)
    )

    def unmix(kind, j, e, w2, w1, slope, ep, eu, outs, tx, rx, bss, brs):
        for k in range(1, size):
            swap.out(kind, j, me, swap.other(k), tx, e, *outs).wait_recv()
        low = (matmul(w2[...], e[j]) * slope[j].astype(F32)).astype(BF)
        ep[j] = low
        eu[j] = matmul(w1, low).astype(BF)
        for k in range(1, size):
            swap.back(kind, j, me, swap.other(k), eu, rx, bss, brs).start()
        patches, per = (patches_l, per_l) if kind == "l" else (patches_s, per_s)
        rx[me * per + j] = eu[j, swap.rows(me, patches)]

    for j in range(per_l):
        tick()
        unmix("l", j, e_l, w2_l, w_l[0], sl_l, ep_l, eu_l, (out_ss_l, out_rs_l), tx_l, rx_l, bk_ss_l, bk_rs_l)
    tick()
    for j in range(per_s):
        unmix("s", j, e_s, w2_s, w_s[0], sl_s, ep_s, eu_s, (out_ss_s, out_rs_s), tx_s, rx_s, bk_ss_s, bk_rs_s)

    vec[8:16, 0:half] = sum(matmul_nt(ones_l, ep_l[j]) for j in range(per_l))
    vec[8:16, half:width] = sum(matmul_nt(ones_s, ep_s[j]) for j in range(per_s))
    top = 2 * patches_l + 2 * patches_s
    begin = 0
    for left, right, per, patches in (
        (u_l, ep_l, per_l, patches_l), (e_l, h_l, per_l, patches_l),
        (u_s, ep_s, per_s, patches_s), (e_s, h_s, per_s, patches_s),
    ):
        value = sum(matmul_nt(left[j], right[j]) for j in range(per))
        for q in range(size):
            grads[q, begin:begin + patches] = value[q * patches:(q + 1) * patches]
        begin += patches
    for p in range(2):
        tok_tx[p] = grads[p * 2 + 1 - peers.core, 0:top].astype(BF)
    t_core = send(tok_tx, tok_rx, tc_ss.at[0], tc_rs.at[0], core_peer)
    t_core.start()
    tick()
    t_core.wait_recv()
    there = 1 - peers.x
    tokx_tx[...] = (grads[there * 2 + peers.core, 0:top] + tok_rx[there].astype(F32)).astype(BF)
    t_x = send(tokx_tx, tokx_rx, tx_ss.at[0], tx_rs.at[0], x_peer)
    t_x.start()
    if SLAB > top:
        tok_sum[top:SLAB, :] = jnp.zeros((SLAB - top, token), F32)
    tok_sum[0:top, :] = grads[me, 0:top] + tok_rx[peers.x].astype(F32)
    tick()
    tick()

    def piece(place, size):
        return pl.ds(pl.multiple_of(place * size, size), size)

    def arrived(kind, unit, eu, rx, bss, brs):
        per = per_l if kind == "l" else per_s
        owner = unit // per

        @pl.when(owner != me)
        def _():
            swap.back(kind, unit - owner * per, owner, me, eu, rx, bss, brs).wait_recv()

    def norm_back(x, eu, at):
        unit, scale = unit_rows(x.astype(F32))
        d = eu * gain
        m1 = jnp.mean(d, axis=-1, keepdims=True)
        m2 = jnp.mean(d * unit, axis=-1, keepdims=True)
        vec[7:8, :] += jnp.sum(eu * unit, axis=0, keepdims=True)
        vec[9:10, :] += jnp.sum(eu, axis=0, keepdims=True)
        return ey[at, :] + scale * (d - m1 - unit * m2)

    def gx_copy(n):
        at = pl.ds(pl.multiple_of(small_rows + n * patches_l, 16), patches_l)
        return pltpu.make_async_copy(ey.at[at], gx_hbm.at[n], gx_sem.at[n])

    def home_l(n, carry):
        arrived("l", 2 * n, eu_l, rx_l, bk_ss_l, bk_rs_l)
        arrived("l", 2 * n + 1, eu_l, rx_l, bk_ss_l, bk_rs_l)
        at = pl.ds(pl.multiple_of(small_rows + n * patches_l, 16), patches_l)
        eu = jnp.concatenate([rx_l[2 * n], rx_l[2 * n + 1]], axis=1).astype(F32)
        ey[at, :] = norm_back(xl[n], eu, at)
        gx_copy(n).start()
        return carry

    def home_s(n, carry):
        arrived("s", n, eu_s, rx_s, bk_ss_s, bk_rs_s)
        at = pl.ds(pl.multiple_of(n * patches_s, 16), real_s)
        gx_s[n] = norm_back(xs[n], rx_s[n, :real_s].astype(F32), at)
        return carry

    vec[9:10, :] = jnp.zeros((1, width), F32)
    lax.fori_loop(0, count_l // 2, home_l, 0)
    tick()
    lax.fori_loop(count_l // 2, count_l, home_l, 0)
    lax.fori_loop(0, count_s, home_s, 0)
    for n in range(count_s):
        gx_out[:, n, :] = gx_s[n]
    both = vec.at[0:16]
    v_core = send(both, vec_rx.at[0], v_ss.at[0], v_rs.at[0], core_peer)
    v_core.start()
    tick()
    t_x.wait_recv()
    tok_sum[0:top, :] += tokx_rx[...].astype(F32)
    part_n = SLAB // near
    part_f = part_n // far
    t_near, t_far, ta_far, ta_near = [], [], [], []
    if far_inside:
        for j, device in near_peers:
            tokn_tx[j - 1] = tok_sum[piece(lax.rem(peers.near + j, near), part_n), :].astype(BF)
            copy = send(tokn_tx.at[j - 1], tokn_rx.at[j - 1], tn_ss.at[j - 1], tn_rs.at[j - 1], device)
            copy.start()
            t_near.append(copy)
    else:
        tok_out[...] = tok_sum[...].astype(BF)
    v_core.wait()
    vec[0:16, :] += vec_rx[0]
    v_x = send(both, vec_rx.at[1], v_ss.at[1], v_rs.at[1], x_peer)
    v_x.start()
    tick()
    v_x.wait()
    vec[0:16, :] += vec_rx[1]
    v_near = [send(vec, vecn_rx.at[j - 1], vn_ss.at[j - 1], vn_rs.at[j - 1], device) for j, device in near_peers]
    for copy in v_near:
        copy.start()
    if far_inside:
        for copy in t_near:
            copy.wait_recv()
        tok_half[...] = tok_sum[piece(peers.near, part_n), :]
        for j in range(near - 1):
            tok_half[...] += tokn_rx[j].astype(F32)
        for j, device in far_peers:
            tokf_tx[j - 1] = tok_half[piece(lax.rem(peers.far + j, far), part_f), :].astype(BF)
            copy = send(tokf_tx.at[j - 1], tokf_rx.at[j - 1], tf_ss.at[j - 1], tf_rs.at[j - 1], device)
            copy.start()
            t_far.append(copy)
    tick()
    for copy in v_near:
        copy.wait()
    for j in range(near - 1):
        vec[...] += vecn_rx[j]
    v_far = [send(vec, vecf_rx.at[j - 1], vf_ss.at[j - 1], vf_rs.at[j - 1], device) for j, device in far_peers]
    for copy in v_far:
        copy.start()
    if far_inside:
        for copy in t_far:
            copy.wait_recv()
        value = tok_half[piece(peers.far, part_f), :]
        for j in range(far - 1):
            value = value + tokf_rx[j].astype(F32)
        span = tok_out.at[piece(peers.near * far + peers.far, part_f)]
        span[...] = value.astype(BF)
        for j, device in far_peers:
            copy = send(span, span, taf_ss.at[j - 1], taf_rs.at[j - 1], device)
            copy.start()
            ta_far.append(copy)
    tick()
    for copy in v_far:
        copy.wait()
    value = vec[...]
    for j in range(far - 1):
        value = value + vecf_rx[j]
    vec_out[...] = value
    if far_inside:
        for copy in ta_far:
            copy.wait_recv()
        span = tok_out.at[piece(peers.near, part_n)]
        for j, device in near_peers:
            copy = send(span, span, tan_ss.at[j - 1], tan_rs.at[j - 1], device)
            copy.start()
            ta_near.append(copy)
    while waiting:
        tick()
    gather.fourth(groups - 1)
    for k in (groups - 2, groups - 1):
        gather.fifth(k)
    for copy in ta_near:
        copy.wait_recv()

    for copy in [t_core, t_x] + t_near + t_far + ta_far + ta_near:
        copy.wait_send()
    for k in range(1, size):
        there = swap.other(k)
        for j in range(per_l):
            swap.out("l", j, there, me, tx_l, e_l, out_ss_l, out_rs_l).wait_send()
            swap.back("l", j, me, there, eu_l, rx_l, bk_ss_l, bk_rs_l).wait_send()
        for j in range(per_s):
            swap.out("s", j, there, me, tx_s, e_s, out_ss_s, out_rs_s).wait_send()
            swap.back("s", j, me, there, eu_s, rx_s, bk_ss_s, bk_rs_s).wait_send()
    for k in range(groups):
        gather.drain(k)
    for n in range(count_l):
        gx_copy(n).wait()


def backward(chunk, begun, ey, xl, xs, saved, small, gain):
    size = lax.axis_size("blk")
    near, far = img_split(lax.axis_size("img"))
    rows, width = ey.shape
    far_inside = width % (near * far * 2 * 16) == 0
    u_l, u_s, h_l, h_s, sl_l, sl_s, w_l, w_s = saved
    count_l, patches_l, _ = xl.shape
    real_s, count_s, _ = xs.shape
    patches_s = real_s + -real_s % 64
    token = w_l.shape[2]
    half = width // 2
    per_l, per_s = u_l.shape[0], u_s.shape[0]
    groups, each, _ = chunk.shape
    vmem = pl.BlockSpec(memory_space=pltpu.VMEM)
    V = pltpu.VMEM
    DMA = pltpu.SemaphoreType.DMA
    n1, f1 = near - 1, far - 1
    top = 2 * patches_l + 2 * patches_s
    part_n = SLAB // near
    part_f = max(part_n // far, 16)
    return pl.pallas_call(
        functools.partial(backward_kernel, near, far, size, far_inside),
        out_shape=(
            jax.ShapeDtypeStruct(begun.shape, BF),
            jax.ShapeDtypeStruct(xl.shape, F32),
            jax.ShapeDtypeStruct((SLAB, token), BF),
            jax.ShapeDtypeStruct((24, width), F32),
            jax.ShapeDtypeStruct(xs.shape, F32),
        ),
        in_specs=[ANY] * 13 + [vmem] * 2,
        out_specs=(ANY, ANY, vmem, vmem, vmem),
        scratch_shapes=[
            V(xl.shape, BF), V(xs.shape, BF), V(u_l.shape, BF), V(u_s.shape, BF), V(h_l.shape, BF), V(h_s.shape, BF),
            V(sl_l.shape, BF), V(sl_s.shape, BF), V(w_l.shape, BF), V(w_s.shape, BF), DMA((10,)),
            V((count_s, real_s, width), BF), V((count_s, real_s, width), F32),
            V((rows, width), F32),
            V((count_l * 2, patches_l, half), BF), V((count_s, patches_s, width), BF),
            V(u_l.shape, BF), V(u_s.shape, BF),
            V((token, size * patches_l), BF), V((token, size * patches_s), BF),
            V(h_l.shape, BF), V(h_s.shape, BF), V(u_l.shape, BF), V(u_s.shape, BF),
            V((count_l * 2, patches_l, half), BF), V((count_s, patches_s, width), BF),
            V((size, top, token), F32), V((2, top, token), BF), V((2, top, token), BF), V((SLAB, token), F32),
            V((n1, part_n, token), BF), V((n1, part_n, token), BF), V((part_n, token), F32),
            V((f1, part_f, token), BF), V((f1, part_f, token), BF), V((top, token), BF), V((top, token), BF),
            V((24, width), F32), V((2, 16, width), F32), V((n1, 24, width), F32), V((f1, 24, width), F32),
            DMA((1,)), DMA((count_l,)),
            DMA((count_l * 2,)), DMA((count_s,)), DMA((per_l, size)), DMA((per_s, size)),
            DMA((per_l, size)), DMA((per_s, size)), DMA((count_l * 2,)), DMA((count_s,)),
            DMA((1,)), DMA((1,)), DMA((1,)), DMA((1,)), DMA((n1,)), DMA((n1,)), DMA((f1,)), DMA((f1,)),
            DMA((f1,)), DMA((f1,)), DMA((n1,)), DMA((n1,)),
            DMA((2,)), DMA((2,)), DMA((n1,)), DMA((n1,)), DMA((f1,)), DMA((f1,)),
        ] + Gather.sems(groups, near, far),
        input_output_aliases={1: 0},
        compiler_params=pltpu.CompilerParams(
            collective_id=1, has_side_effects=True, vmem_limit_bytes=TOP
        ),
    )(chunk, begun, ey, xl, xs, u_l, u_s, h_l, h_s, sl_l, sl_s, w_l, w_s, small, gain)


def widen_kernel(
    first, second, tok, vec, out_l_in, gx_l_in, out_s_in, gx_s_in,
    out_l, gx_l, out_s, gx_s, out_first, out_second, gain1, bias1, w1_s, b1_s, w2_s, b2_s, w1_l, b1_l, w2_l, b2_l, gain2, bias2, b1, b2,
):
    out_l[...] = out_l_in[...]
    gx_l[...] = gx_l_in[...]
    for k in range(first.shape[1]):
        out_first[:, k * TILE:(k + 1) * TILE] = first[0, k].astype(F32)
        out_second[k * TILE:(k + 1) * TILE, :] = second[0, k].astype(F32).T

    @pl.when(pl.program_id(0) == 0)
    def _():
        out_s[...] = out_s_in[...]
        gx_s[...] = gx_s_in[...]
        width = vec.shape[1]
        half = width // 2
        large, small = w1_l.shape[0], w1_s.shape[0]
        wide = small + -small % 64
        at = 2 * large
        w1_l[...] = tok[0:large, :].astype(F32)
        w2_l[...] = tok[large:at, :].astype(F32)
        w1_s[...] = tok[at:at + wide, :].astype(F32)[:small]
        w2_s[...] = tok[at + wide:at + 2 * wide, :].astype(F32)[:small]
        gain1[...] = vec[7, :]
        bias1[...] = vec[9, :]
        b1_l[...] = vec[8, 0:half]
        b1_s[...] = vec[8, half:width]
        b2_l[...] = vec[16, 0:large]
        b2_s[...] = vec[16, half:half + small]
        gain2[...] = vec[5, :]
        bias2[...] = vec[6, :]
        for k in range(b1.shape[0] // width):
            b1[k * width:(k + 1) * width] = vec[k, :]
        b2[...] = vec[4, :]


def widen(full, tok, vec, out_l, gx_l, out_s, gx_s):
    full = full.reshape(full.shape[0], full.shape[1], -1, TILE)
    _, groups, width, _ = full.shape
    count_l, patches_l, _ = out_l.shape
    patches_s = out_s.shape[0]
    hidden = groups * TILE
    token = tok.shape[1]
    step = 2 * TILE
    shapes = (
        (width,), (width,), (patches_s, token), (token,), (patches_s, token), (patches_s,),
        (patches_l, token), (token,), (patches_l, token), (patches_l,), (width,), (width,), (hidden,), (width,),
    )

    def whole(shape):
        return pl.BlockSpec(shape, lambda i: (0,) * len(shape))

    image = pl.BlockSpec((1, patches_l, width), lambda i: (jnp.minimum(i, count_l - 1), 0, 0))
    return pl.pallas_call(
        widen_kernel,
        grid=(hidden // step,),
        out_shape=tuple(jax.ShapeDtypeStruct(a.shape, a.dtype) for a in (out_l, gx_l, out_s, gx_s)) + (
            jax.ShapeDtypeStruct((width, hidden), F32), jax.ShapeDtypeStruct((hidden, width), F32),
        ) + tuple(jax.ShapeDtypeStruct(shape, F32) for shape in shapes),
        in_specs=[
            pl.BlockSpec((1, 2, width, TILE), lambda i: (0, i, 0, 0)),
            pl.BlockSpec((1, 2, width, TILE), lambda i: (1, i, 0, 0)),
            whole(tok.shape), whole(vec.shape), image, image, whole(out_s.shape), whole(gx_s.shape),
        ],
        out_specs=(
            image, image, whole(out_s.shape), whole(gx_s.shape),
            pl.BlockSpec((width, step), lambda i: (0, i)), pl.BlockSpec((step, width), lambda i: (i, 0)),
        ) + tuple(whole(shape) for shape in shapes),
        compiler_params=pltpu.CompilerParams(vmem_limit_bytes=TOP),
    )(full, full, tok, vec, out_l, gx_l, out_s, gx_s)


def local(
    x_small, x_large, live_counts, ln1_gain, ln1_bias,
    tok_w1_small, tok_b1_small, tok_w2_small, tok_b2_small,
    tok_w1_large, tok_b1_large, tok_w2_large, tok_b2_large,
    ln2_gain, ln2_bias, ch_w1, ch_b1, ch_w2, ch_b2, cot_small, cot_large,
):
    width = x_small.shape[2]
    patches_s, patches_l = x_small.shape[1], x_large.shape[1]
    rows = x_small.shape[0] * (patches_s + -patches_s % 64) + x_large.shape[0] * patches_l
    xs = x_small.transpose(1, 0, 2)
    y, *saved = token_forward(
        x_large, xs, tok_w1_large, tok_w1_small, tok_w2_large.T, tok_w2_small.T,
        tok_b1_large, tok_b1_small, tok_b2_large, tok_b2_small, ln1_gain, ln1_bias, rows + -rows % (3 * LANES),
    )
    out_large, ey, chunk, small_grads, out_small, begun = channel(
        y, live_counts, cot_large, cot_small.transpose(1, 0, 2), ch_w1, ch_w2, ch_b1, ln2_gain, ln2_bias, ch_b2
    )
    near, far = img_split(lax.axis_size("img"))
    far_inside = width % (near * far * 2 * 16) == 0
    if not far_inside:
        same = [[a * near + b for a in range(far)] for b in range(near)]
        chunk = lax.psum(chunk.astype(F32), "img", axis_index_groups=same).astype(BF)
    full, gx_large, tok, vec, gx_small = backward(
        chunk, begun, ey, x_large, xs, saved, small_grads, ln1_gain
    )
    if not far_inside:
        tok = lax.psum(tok.astype(F32), "img")
    (
        out_large, gx_large, out_small, gx_small, grad_ch_w1, grad_ch_w2, gain1, bias1, w1_s, b1_s, w2_s, b2_s, w1_l, b1_l, w2_l, b2_l,
        gain2, bias2, grad_b1, grad_b2,
    ) = widen(full, tok, vec, out_large, gx_large, out_small, gx_small)
    return (
        out_small.transpose(1, 0, 2), out_large, gx_small.transpose(1, 0, 2), gx_large, gain1, bias1,
        w1_s, b1_s, w2_s.T, b2_s, w1_l, b1_l, w2_l.T, b2_l,
        gain2, bias2, grad_ch_w1, grad_b1, grad_ch_w2, grad_b2,
    )


def solution(mesh):
    image = P("img", "blk", None)
    whole = P()
    rows = P("blk", None)
    columns = P(None, "blk")
    vector = P("blk")
    in_specs = (
        image, image, P("img", None), whole, whole,
        rows, whole, columns, vector, rows, whole, columns, vector,
        whole, whole, whole, whole, whole, whole, image, image,
    )
    out_specs = (
        image, image, image, image, whole, whole,
        rows, whole, columns, vector, rows, whole, columns, vector,
        whole, whole, whole, whole, whole, whole,
    )
    return jax.shard_map(local, mesh=mesh, in_specs=in_specs, out_specs=out_specs, check_vma=False)
```

```python
import functools

import jax
import jax.numpy as jnp
from jax import lax
from jax.experimental import pallas as pl
from jax.experimental.pallas import tpu as pltpu
from jax.sharding import PartitionSpec as P

EPSILON = 1e-06
LANES = 128
BF = jnp.bfloat16
F32 = jnp.float32


MESH = pl.DeviceIdType.MESH
ANY = pl.BlockSpec(memory_space=pl.ANY)
TILE = 256
LAGS = (1, 3, 5, 7)
LATE = 4
TOP = 62 * 1024 * 1024


def img_split(size):
    near = 2 if size <= 8 else 8
    return near, size // near


def gelu_pair(a):
    square = a * a
    slope = 0.7978845608028654
    t = jnp.tanh(a * (slope + (slope * 0.044715) * square))
    half = 0.5 + 0.5 * t
    inner = slope + (3.0 * slope * 0.044715) * square
    return a * half, half + (0.5 * a) * (1.0 - t * t) * inner


class Peers:
    def __init__(self, near_count):
        self.img = lax.axis_index("img")
        self.blk = lax.axis_index("blk")
        self.core = lax.rem(self.blk, 2)
        self.x = self.blk // 2
        self.near_count = near_count
        self.near = lax.rem(self.img, near_count)
        self.far = self.img // near_count

    def at(self, axis, place):
        if axis == "core":
            return (self.img, self.x * 2 + place)
        if axis == "x":
            return (self.img, place * 2 + self.core)
        if axis == "near":
            return (self.far * self.near_count + place, self.blk)
        return (place * self.near_count + self.near, self.blk)

    def mine(self, axis):
        return {"core": self.core, "x": self.x, "near": self.near, "far": self.far}[axis]


def greet(peers, axes):
    barrier = pltpu.get_barrier_semaphore()
    total = 0
    for axis, count in axes:
        for j in range(1, count):
            there = lax.rem(peers.mine(axis) + j, count)
            pl.semaphore_signal(barrier, inc=1, device_id=peers.at(axis, there), device_id_type=MESH)
            total += 1
    return total


def greeted(total):
    pl.semaphore_wait(pltpu.get_barrier_semaphore(), total)


class Gather:
    def __init__(self, peers, near, far, far_inside, chunk, full, sems):
        self.peers, self.near, self.far_inside = peers, near, far_inside
        self.f = far if far_inside else 1
        self.chunk, self.full = chunk, full
        self.tiles = chunk.shape[0]
        self.late = self.tiles - LATE if far_inside else self.tiles
        self.own_sem, self.x_ss, self.x_rs, self.f_ss, self.f_rs, self.n_ss, self.n_rs, self.c_ss, self.c_rs = sems
        self.place = (peers.near, peers.far if far_inside else 0, peers.x)

    def span(self, k, axes):
        index = tuple(p if a in axes else slice(None) for p, a in zip(self.place, "nfx"))
        while index and isinstance(index[-1], slice):
            index = index[:-1]
        return self.full.at[(self.peers.core, k) + index]

    def send(self, src, dst, ss, rs, device):
        return pltpu.make_async_remote_copy(
            src_ref=src, dst_ref=dst, send_sem=ss, recv_sem=rs, device_id=device, device_id_type=MESH
        )

    def own(self, k):
        return pltpu.make_async_copy(self.chunk.at[k], self.span(k, "nfx"), self.own_sem.at[k])

    def x_first(self, k):
        there = self.peers.at("x", 1 - self.peers.x)
        return self.send(self.chunk.at[k], self.span(k, "nfx"), self.x_ss.at[k], self.x_rs.at[k], there)

    def x_last(self, k):
        there = self.peers.at("x", 1 - self.peers.x)
        return self.send(self.span(k, "x"), self.span(k, "x"), self.x_ss.at[k], self.x_rs.at[k], there)

    def spread(self, axis, count, span, ss, rs, k):
        copies = []
        for j in range(1, count):
            there = self.peers.at(axis, lax.rem(self.peers.mine(axis) + j, count))
            copies.append(self.send(span, span, ss.at[k, j - 1], rs.at[k, j - 1], there))
        return copies

    def to_far(self, k):
        return self.spread("far", self.f, self.span(k, "nf" if k < self.late else "nfx"), self.f_ss, self.f_rs, k)

    def to_near(self, k):
        return self.spread("near", self.near, self.span(k, "n" if k < self.late else "nx"), self.n_ss, self.n_rs, k)

    def to_core(self, k):
        span = self.span(k, "")
        return self.send(span, span, self.c_ss.at[k], self.c_rs.at[k], self.peers.at("core", 1 - self.peers.core))

    def first(self, k):
        self.own(k).start()

        @pl.when(k < self.late)
        def _():
            self.x_first(k).start()

    def end_first(self, k):
        self.own(k).wait()
        if k < self.late:
            self.x_first(k).wait()

    def second(self, k):
        for copy in self.to_far(k):
            copy.start()

    def third(self, k):
        for copy in self.to_far(k):
            copy.wait_recv()
        for copy in self.to_near(k):
            copy.start()

    def fourth(self, k):
        for copy in self.to_near(k):
            copy.wait_recv()
        (self.to_core(k) if k < self.late else self.x_last(k)).start()

    def fifth(self, k):
        if k >= self.late:
            self.x_last(k).wait_recv()
            self.to_core(k).start()

    def drain(self, k):
        for copy in self.to_far(k) + self.to_near(k):
            copy.wait_send()
        if k >= self.late:
            self.x_last(k).wait_send()
        self.to_core(k).wait()

    @staticmethod
    def sems(groups, near, far):
        DMA = pltpu.SemaphoreType.DMA
        n1, f1 = near - 1, max(far - 1, 1)
        return [DMA((groups,))] * 3 + [DMA((groups, f1))] * 2 + [DMA((groups, n1))] * 2 + [DMA((groups,))] * 2


def row(ref):
    return ref[...].reshape(1, -1)


def column(ref, rows):
    value = jnp.broadcast_to(ref[...].reshape(1, -1), (8, ref.shape[0])).T[:, :1]
    return value if rows == ref.shape[0] else jnp.concatenate([value, jnp.zeros((rows - ref.shape[0], 1), F32)])


def channel_kernel(
    near, far, far_inside,
    y_hbm, live, cot_l, cot_s_in, w1_hbm, w2_hbm, b1_ref, gain_ref, bias_ref, b2_ref,
    out_l, ey_hbm, chunk_ref, small_ref, out_s_t, full_hbm,
    cot_s, out_s, y, ec, v, lt, rt, w1, w2, acc_out, acc_ev, out_low,
    keep, core_tx, core_rx,
    a_keep_n, a_near_tx, a_near_rx, a_keep_f, a_far_tx, a_far_rx, a_keep_x, a_x_tx, a_x_rx,
    b_keep_x, b_x_tx, b_x_rx, b_keep_n, b_near_tx, b_near_rx, b_keep_f, b_far_tx, b_far_rx,
    in_sem, w_sem, out_sem, core_ss, core_rs,
    a_near_ss, a_near_rs, a_far_ss, a_far_rs, a_x_ss, a_x_rs,
    b_near_ss, b_near_rs, b_far_ss, b_far_rs, b_x_ss, b_x_rs, *gather_sems,
):
    rows, width = y.shape
    tiles = w1.shape[0]
    count_l, patches_l, _ = cot_l.shape
    count_s, patches_s, _ = cot_s.shape
    wide_s = patches_s + -patches_s % 64
    small_rows = count_s * wide_s
    peers = Peers(near)
    core = peers.core
    f_place = peers.far if far_inside else 0
    gather = Gather(peers, near, far, far_inside, chunk_ref, full_hbm, gather_sems)
    part = 128
    parts = rows // part
    gain, bias, b2 = row(gain_ref), row(bias_ref), row(b2_ref)

    def w_copies(t):
        return (
            pltpu.make_async_copy(w1_hbm.at[:, pl.ds(t * TILE, TILE)], w1.at[t], w_sem.at[0, t]),
            pltpu.make_async_copy(w2_hbm.at[pl.ds(t * TILE, TILE)], w2.at[t], w_sem.at[1, t]),
        )

    y_in = pltpu.make_async_copy(y_hbm, y, in_sem.at[0])
    y_in.start()

    def start_w(t, carry):
        for copy in w_copies(t):
            copy.start()
        return carry

    lax.fori_loop(0, tiles, start_w, 0)
    axes = [("core", 2), ("near", near)] + ([("far", far)] if far_inside else []) + [("x", 2)]
    greetings = greet(peers, axes)
    small_ref[...] = jnp.zeros_like(small_ref)
    used = small_rows + count_l * patches_l
    ec[0:small_rows, :] = jnp.zeros((small_rows, width), BF)
    if rows > used:
        ec[used:rows, :] = jnp.zeros((rows - used, width), BF)

    def live_l(n):
        return jnp.where(n < live[0, 1], 1.0, 0.0).astype(F32)

    def live_s(n):
        return jnp.where(n < live[0, 0], 1.0, 0.0).astype(F32)

    def mask_l(n, carry):
        ec[pl.ds(pl.multiple_of(small_rows + n * patches_l, 16), patches_l), :] = (
            cot_l[n].astype(F32) * live_l(n)
        ).astype(BF)
        return carry

    def mask_s(n, carry):
        ec[pl.ds(pl.multiple_of(n * wide_s, 16), patches_s), :] = (cot_s[n].astype(F32) * live_s(n)).astype(BF)
        return carry

    lax.fori_loop(0, count_l, mask_l, 0)
    for n in range(count_s):
        cot_s[n] = cot_s_in[:, n, :]
    lax.fori_loop(0, count_s, mask_s, 0)
    y_in.wait()

    def prepare(p, carry):
        at = pl.ds(pl.multiple_of(p * part, part), part)
        unit, _ = unit_rows(y[at, :])
        low = (unit * gain + bias).astype(BF)
        v[at, :] = low
        lt[0, :, at] = low.T
        own = ec[at, :]
        lt[1, :, at] = own.T
        small_ref[4:5, :] += jnp.sum(own.astype(F32), axis=0, keepdims=True)
        acc_out[at, :] = jnp.zeros((part, width), F32)
        acc_ev[at, :] = jnp.zeros((part, width), F32)
        return carry

    lax.fori_loop(0, parts, prepare, 0)
    greeted(greetings)

    def send(src, dst, ss, rs, device):
        return pltpu.make_async_remote_copy(
            src_ref=src, dst_ref=dst, send_sem=ss, recv_sem=rs, device_id=device, device_id_type=MESH
        )

    def core_copy(t):
        slot = lax.rem(t, 2)
        return send(core_tx.at[slot], core_rx.at[t], core_ss.at[slot], core_rs.at[t], peers.at("core", 1 - core))

    def spread(tx, rx, ss, rs, axis, count, i):
        slot = lax.rem(i, 2)
        copies = []
        for j in range(1, count):
            there = lax.rem(peers.mine(axis) + j, count)
            copies.append(
                send(tx.at[slot, j - 1], rx.at[i, j - 1], ss.at[slot, j - 1], rs.at[i, j - 1], peers.at(axis, there))
            )
        return copies

    f = far if far_inside else 1
    a_near = lambda i: spread(a_near_tx, a_near_rx, a_near_ss, a_near_rs, "near", near, i)
    a_far = lambda i: spread(a_far_tx, a_far_rx, a_far_ss, a_far_rs, "far", f, i)
    a_x = lambda i: spread(a_x_tx, a_x_rx, a_x_ss, a_x_rs, "x", 2, i)
    b_near = lambda i: spread(b_near_tx, b_near_rx, b_near_ss, b_near_rs, "near", near, i)
    b_far = lambda i: spread(b_far_tx, b_far_rx, b_far_ss, b_far_rs, "far", f, i)
    b_x = lambda i: spread(b_x_tx, b_x_rx, b_x_ss, b_x_rs, "x", 2, i)
    each = width // near // f // 2

    def tile_step(t):
        for copy in w_copies(t):
            copy.wait()

        @pl.when(t >= 2)
        def _():
            core_copy(t - 2).wait_send()

        slot = lax.rem(t, 2)
        columns = pl.ds(pl.multiple_of(t * TILE, TILE), TILE)
        a = matmul(v[...], w1[t]) + b1_ref[columns].reshape(1, -1)
        gh = matmul_nt(ec[...], w2[t])
        g, slope = gelu_pair(a)
        ea = (slope * gh).astype(BF)
        rt[1] = g.astype(BF)
        rt[0] = ea
        per = width // TILE
        small_ref[lax.div(t, per), pl.ds(pl.multiple_of(lax.rem(t, per) * TILE, TILE), TILE)] = jnp.sum(
            ea.astype(F32), axis=0
        )
        core_tx[slot] = matmul(lt[1 - core], rt[1 - core]).astype(BF).reshape(near, f, 2, each, TILE)
        keep[slot] = matmul(lt[core], rt[core]).reshape(near, f, 2, each, TILE)
        acc_out[...] += matmul(rt[1], w2[t])
        acc_ev[...] += matmul_nt(rt[0], w1[t])
        core_copy(t).start()

    def ey_copy(at, n):
        return pltpu.make_async_copy(acc_ev.at[at], ey_hbm.at[at], out_sem.at[n])

    def at_l(n):
        return pl.ds(pl.multiple_of(small_rows + n * patches_l, 16), patches_l)

    def at_s(n):
        return pl.ds(pl.multiple_of(n * wide_s, 16), wide_s)

    def out_copy(n):
        return pltpu.make_async_copy(out_low.at[n], out_l.at[n], out_sem.at[count_l + count_s + n])

    def finish_rows(at, live_here):
        here = y[at, :]
        result = ((here + acc_out[at, :] + b2) * live_here).astype(BF)
        unit, scale = unit_rows(here)
        ev = acc_ev[at, :]
        small_ref[5:6, :] += jnp.sum(ev * unit, axis=0, keepdims=True)
        small_ref[6:7, :] += jnp.sum(ev, axis=0, keepdims=True)
        d = ev * gain
        m1 = jnp.mean(d, axis=-1, keepdims=True)
        m2 = jnp.mean(d * unit, axis=-1, keepdims=True)
        acc_ev[at, :] = ec[at, :].astype(F32) + scale * (d - m1 - unit * m2)
        return result

    def finish(p):
        def one_l(q, carry):
            n = p + q * 4

            @pl.when(n < count_l)
            def _():
                out_low[n] = finish_rows(at_l(n), live_l(n))
                ey_copy(at_l(n), n).start()
                out_copy(n).start()

            return carry

        def one_s(q, carry):
            n = p + q * 4

            @pl.when(n < count_s)
            def _():
                out_s[n] = finish_rows(at_s(n), live_s(n))[:patches_s]
                ey_copy(at_s(n), count_l + n).start()

            return carry

        lax.fori_loop(0, pl.cdiv(count_l, 4), one_l, 0)
        lax.fori_loop(0, pl.cdiv(count_s, 4), one_s, 0)

    def free(copies, i):
        @pl.when(i >= 2)
        def _():
            for copy in copies(i - 2):
                copy.wait_send()

    def reduce(value, axis, count, place, tx, own, copies, i):
        slot = lax.rem(i, 2)
        free(copies, i)
        made = copies(i)
        for j in range(1, count + 1):
            there = lax.rem(place + j, count)
            piece = value(there)
            if j < count:
                tx[slot, j - 1] = piece.astype(BF)
                made[j - 1].start()
            else:
                own(slot, piece)

    def arrivals(copies, i):
        for copy in copies(i):
            copy.wait_recv()

    def save(ref):
        def put(slot, piece):
            ref[slot] = piece
        return put

    def plus(base, rx, i, count, index):
        value = base
        for k in range(count - 1):
            value = value + rx[(i, k) + index].astype(F32)
        return value

    def chunk_out(t, value):
        chunk_ref[t] = value.astype(BF)
        if far_inside:
            gather.first(t)

    def even_core(t):
        i = lax.div(t, 2)
        core_copy(t).wait_recv()
        reduce(
            lambda p: keep[0, p] + core_rx[t, p].astype(F32),
            "near", near, peers.near, a_near_tx, save(a_keep_n), a_near, i,
        )

    def even_near(t):
        i = lax.div(t, 2)
        slot = lax.rem(i, 2)
        arrivals(a_near, i)
        reduce(
            lambda p: plus(a_keep_n[slot, p], a_near_rx, i, near, (p,)),
            "far", f, f_place, a_far_tx, save(a_keep_f), a_far, i,
        )

    def even_far(t):
        i = lax.div(t, 2)
        slot = lax.rem(i, 2)
        arrivals(a_far, i)
        reduce(
            lambda p: plus(a_keep_f[slot, p], a_far_rx, i, f, (p,)),
            "x", 2, peers.x, a_x_tx, save(a_keep_x), a_x, i,
        )

    def even_x(t):
        i = lax.div(t, 2)
        arrivals(a_x, i)
        chunk_out(t, a_keep_x[lax.rem(i, 2)] + a_x_rx[i, 0].astype(F32))

    def odd_core(t):
        i = lax.div(t, 2)
        core_copy(t).wait_recv()
        reduce(
            lambda p: keep[1, :, :, p] + core_rx[t, :, :, p].astype(F32),
            "x", 2, peers.x, b_x_tx, save(b_keep_x), b_x, i,
        )

    def odd_x(t):
        i = lax.div(t, 2)
        slot = lax.rem(i, 2)
        arrivals(b_x, i)
        reduce(
            lambda p: plus(b_keep_x[slot, p], b_x_rx, i, 2, (p,)),
            "near", near, peers.near, b_near_tx, save(b_keep_n), b_near, i,
        )

    def odd_near(t):
        i = lax.div(t, 2)
        slot = lax.rem(i, 2)
        arrivals(b_near, i)
        reduce(
            lambda p: plus(b_keep_n[slot, p], b_near_rx, i, near, (p,)),
            "far", f, f_place, b_far_tx, save(b_keep_f), b_far, i,
        )

    def odd_far(t):
        i = lax.div(t, 2)
        arrivals(b_far, i)
        slot = lax.rem(i, 2)
        chunk_out(t, plus(b_keep_f[slot], b_far_rx, i, f, ()))

    stages = ((even_core, even_near, even_far, even_x), (odd_core, odd_x, odd_near, odd_far))

    def pair(s2, carry):
        for parity in range(2):
            s = s2 * 2 + parity

            @pl.when(s < tiles)
            def _():
                tile_step(s)

            for place, lag in enumerate(LAGS):
                t = s - lag
                stage = stages[(parity - lag) % 2][place]

                @pl.when((t >= 0) & (t < tiles))
                def _(t=t, stage=stage):
                    stage(t)

            @pl.when((s >= tiles) & (s < tiles + 4))
            def _():
                finish(s - tiles)

        return carry

    lax.fori_loop(0, (tiles + LAGS[-1] + 1) // 2, pair, 0)
    if far_inside:
        for k in range(tiles):
            gather.end_first(k)
    for t in (tiles - 2, tiles - 1):
        core_copy(t).wait_send()
    for copies in (a_near, a_far, a_x, b_near, b_far, b_x):
        for i in (tiles // 2 - 2, tiles // 2 - 1):
            for copy in copies(i):
                copy.wait_send()
    for n in range(count_s):
        out_s_t[:, n, :] = out_s[n]
    for n in range(count_l):
        ey_copy(at_l(n), n).wait()
        out_copy(n).wait()
    for n in range(count_s):
        ey_copy(at_s(n), count_l + n).wait()


def channel(y, live, cot_l, cot_s, w1, w2, b1, gain, bias, b2):
    rows, width = y.shape
    hidden = w1.shape[1]
    tiles = hidden // TILE
    near, far = img_split(lax.axis_size("img"))
    far_inside = width % (near * far * 2 * 16) == 0
    f = far if far_inside else 1
    chunk = width // near // f // 2
    vmem = pl.BlockSpec(memory_space=pltpu.VMEM)
    V = pltpu.VMEM
    DMA = pltpu.SemaphoreType.DMA
    fm = max(f - 1, 1)
    nm = near - 1
    pairs = tiles // 2
    real_s, count_s, _ = cot_s.shape
    count = cot_l.shape[0] + count_s
    return pl.pallas_call(
        functools.partial(channel_kernel, near, far, far_inside),
        out_shape=(
            jax.ShapeDtypeStruct(cot_l.shape, BF),
            jax.ShapeDtypeStruct((rows, width), F32),
            jax.ShapeDtypeStruct((tiles, chunk, TILE), BF),
            jax.ShapeDtypeStruct((8, width), F32),
            jax.ShapeDtypeStruct(cot_s.shape, BF),
            jax.ShapeDtypeStruct((2, tiles, near, f, 2, chunk, TILE), BF),
        ),
        in_specs=[ANY, pl.BlockSpec(memory_space=pltpu.SMEM), vmem, vmem, ANY, ANY] + [vmem] * 4,
        out_specs=(ANY, ANY, vmem, vmem, vmem, ANY),
        scratch_shapes=[
            V((count_s, real_s, width), BF), V((count_s, real_s, width), BF),
            V((rows, width), F32), V((rows, width), BF), V((rows, width), BF),
            V((2, width, rows), BF), V((2, rows, TILE), BF),
            V((tiles, width, TILE), BF), V((tiles, TILE, width), BF),
            V((rows, width), F32), V((rows, width), F32), V(cot_l.shape, BF),
            V((2, near, f, 2, chunk, TILE), F32), V((2, near, f, 2, chunk, TILE), BF),
            V((tiles, near, f, 2, chunk, TILE), BF),
            V((2, f, 2, chunk, TILE), F32), V((2, nm, f, 2, chunk, TILE), BF), V((pairs, nm, f, 2, chunk, TILE), BF),
            V((2, 2, chunk, TILE), F32), V((2, fm, 2, chunk, TILE), BF), V((pairs, fm, 2, chunk, TILE), BF),
            V((2, chunk, TILE), F32), V((2, 1, chunk, TILE), BF), V((pairs, 1, chunk, TILE), BF),
            V((2, near, f, chunk, TILE), F32), V((2, 1, near, f, chunk, TILE), BF),
            V((pairs, 1, near, f, chunk, TILE), BF),
            V((2, f, chunk, TILE), F32), V((2, nm, f, chunk, TILE), BF), V((pairs, nm, f, chunk, TILE), BF),
            V((2, chunk, TILE), F32), V((2, fm, chunk, TILE), BF), V((pairs, fm, chunk, TILE), BF),
            DMA((1,)), DMA((2, tiles)), DMA((2 * count,)), DMA((2,)), DMA((tiles,)),
            DMA((2, nm)), DMA((pairs, nm)), DMA((2, fm)), DMA((pairs, fm)), DMA((2, 1)), DMA((pairs, 1)),
            DMA((2, nm)), DMA((pairs, nm)), DMA((2, fm)), DMA((pairs, fm)), DMA((2, 1)), DMA((pairs, 1)),
        ] + Gather.sems(tiles, near, f),
        compiler_params=pltpu.CompilerParams(
            collective_id=0, has_side_effects=True, vmem_limit_bytes=TOP
        ),
    )(y, live, cot_l, cot_s, w1, w2, b1, gain, bias, b2)


NT = (((1,), (1,)), ((), ()))


def matmul(left, right):
    return jnp.dot(left, right, preferred_element_type=F32)


def matmul_nt(left, right):
    return lax.dot_general(left, right, NT, preferred_element_type=F32)


class Swap:
    def __init__(self, peers, size, per_l, per_s, patches_l, patches_s):
        self.peers, self.size = peers, size
        self.per_l, self.per_s = per_l, per_s
        self.pl, self.ps = patches_l, patches_s

    def other(self, step):
        return lax.rem(self.peers.blk + step, self.size)

    def copy(self, src, dst, ss, rs, place):
        return pltpu.make_async_remote_copy(
            src_ref=src, dst_ref=dst, send_sem=ss, recv_sem=rs,
            device_id=(self.peers.img, place), device_id_type=MESH,
        )

    def rows(self, place, patches):
        return pl.ds(pl.multiple_of(place * patches, patches), patches)

    def out(self, kind, j, place, source, tx, cols, ss, rs):
        per, patches = (self.per_l, self.pl) if kind == "l" else (self.per_s, self.ps)
        unit = place * per + j
        return self.copy(
            tx.at[unit], cols.at[j, self.rows(source, patches)], ss.at[unit], rs.at[j, source], place
        )

    def back(self, kind, j, owner, place, cols, rx, ss, rs):
        per, patches = (self.per_l, self.pl) if kind == "l" else (self.per_s, self.ps)
        unit = owner * per + j
        return self.copy(
            cols.at[j, self.rows(place, patches)], rx.at[unit], ss.at[j, place], rs.at[unit], place
        )


def greet_all(peers, size, near, far):
    barrier = pltpu.get_barrier_semaphore()
    total = 0
    for j in range(1, size):
        there = lax.rem(peers.blk + j, size)
        pl.semaphore_signal(barrier, inc=1, device_id=(peers.img, there), device_id_type=MESH)
        total += 1
    for axis, count in (("near", near), ("far", far)):
        for j in range(1, count):
            there = lax.rem(peers.mine(axis) + j, count)
            pl.semaphore_signal(barrier, inc=1, device_id=peers.at(axis, there), device_id_type=MESH)
            total += 1
    return total


def unit_rows(row):
    mean = jnp.mean(row, axis=-1, keepdims=True)
    centered = row - mean
    var = jnp.mean(centered * centered, axis=-1, keepdims=True)
    scale = lax.rsqrt(var + EPSILON)
    return centered * scale, scale


def weights_shared(near, far, patches_l, patches_s):
    if near != 2 or far < 2 or patches_l % (16 * (far - 1)):
        return False
    return patches_l // (far - 1) <= patches_s


def token_kernel(
    near, far, size,
    xl, xs_in, w1_l, w1_s, w2_l, w2_s, b1_l_ref, b1_s_ref, b2_l_ref, b2_s_ref, gain_ref, bias_ref,
    y_hbm, u_l, u_s, h_l, h_s, sl_l, sl_s, w_l, w_s,
    xs, wq, mine_w, theirs_w, tx_l, tx_s, w1t_l, w1t_s, m_l, m_s, rx_l, rx_s, y,
    y_sem, own_sem, wown, w_ss, w_rs, out_ss_l, out_ss_s, out_rs_l, out_rs_s, bk_ss_l, bk_ss_s, bk_rs_l, bk_rs_s,
    sx_sem, sf_ss, sf_rs, sn_ss, sn_rs, sc_sem,
):
    peers = Peers(near)
    me = peers.blk
    count_l, patches_l, width = xl.shape
    count_s, real_s, _ = xs.shape
    patches_s = tx_s.shape[1]
    token = w1_l.shape[1]
    half = width // 2
    per_l, per_s = count_l * 2 // size, count_s // size
    swap = Swap(peers, size, per_l, per_s, patches_l, patches_s)
    shared = weights_shared(near, far, patches_l, patches_s)
    total = patches_l + patches_s
    for k, (large, small) in enumerate(((w1_l, w1_s), (w2_l, w2_s))):
        wq[k, :patches_l] = large[...]
        wq[k, patches_l:] = jnp.zeros((patches_s, token), BF)
        wq[k, patches_l:patches_l + real_s] = small[...]
    wq_l = wq.at[:, pl.ds(0, patches_l)]
    wq_s = wq.at[:, pl.ds(patches_l, patches_s)]

    greetings = greet_all(peers, size, near if shared else 1, far if shared else 1)

    def weights(src_l, src_s, quarter, n, place):
        return (
            swap.copy(src_l, w_l.at[:, swap.rows(quarter, patches_l)], w_ss.at[n, 0], w_rs.at[n, 0], place),
            swap.copy(src_s, w_s.at[:, swap.rows(quarter, patches_s)], w_ss.at[n, 1], w_rs.at[n, 1], place),
        )

    x_peer = (1 - peers.x) * 2 + peers.core
    core_peer = peers.x * 2 + 1 - peers.core
    diagonal = (1 - peers.x) * 2 + 1 - peers.core
    if shared:
        stride = patches_l // (far - 1)

        def share(src, dst, ss, rs, device):
            return pltpu.make_async_remote_copy(
                src_ref=src, dst_ref=dst, send_sem=ss, recv_sem=rs, device_id=device, device_id_type=MESH
            )

        n, f = peers.near, peers.far
        first = pl.ds(pl.multiple_of(f * stride, 16), patches_s)
        over_x = share(wq.at[n, first], mine_w.at[n, f], sx_sem.at[0], sx_sem.at[1], (peers.img, x_peer))
        over_far = [
            share(
                mine_w.at[n, f], mine_w.at[n, f], sf_ss.at[j - 1], sf_rs.at[j - 1],
                peers.at("far", lax.rem(f + j, far)),
            )
            for j in range(1, far)
        ]
        over_near = share(mine_w.at[n], mine_w.at[n], sn_ss.at[0], sn_rs.at[0], peers.at("near", 1 - n))
        over_core = share(mine_w, theirs_w, sc_sem.at[0], sc_sem.at[1], (peers.img, core_peer))
    to_x = (over_x,) if shared else weights(wq_l, wq_s, me, 0, x_peer)
    to_core = weights(wq_l, wq_s, me, 1, core_peer)
    relay = () if shared else weights(
        w_l.at[:, swap.rows(x_peer, patches_l)], w_s.at[:, swap.rows(x_peer, patches_s)], x_peer, 2, core_peer
    )
    own_w = (
        pltpu.make_async_copy(wq_l, w_l.at[:, swap.rows(me, patches_l)], wown.at[0]),
        pltpu.make_async_copy(wq_s, w_s.at[:, swap.rows(me, patches_s)], wown.at[1]),
    )
    for copy in own_w:
        copy.start()

    gain, bias = row(gain_ref), row(bias_ref)

    def norm(values):
        unit, _ = unit_rows(values.astype(F32))
        return (unit * gain + bias).astype(BF)

    def norm_l(n, carry):
        u = norm(xl[n])
        tx_l[2 * n] = u[:, :half]
        tx_l[2 * n + 1] = u[:, half:]
        return carry


    def norm_s(n, carry):
        tx_s[n, :real_s] = norm(xs[n])
        return carry

    lax.fori_loop(0, count_l, norm_l, 0)
    greeted(greetings)
    for copy in to_x + to_core:
        copy.start()
    for j in range(per_l):
        for k in range(1, size):
            swap.out("l", j, swap.other(k), me, tx_l, u_l, out_ss_l, out_rs_l).start()
    tx_s[...] = jnp.zeros_like(tx_s)
    for n in range(count_s):
        xs[n] = xs_in[:, n, :]
    lax.fori_loop(0, count_s, norm_s, 0)
    for j in range(per_s):
        for k in range(1, size):
            swap.out("s", j, swap.other(k), me, tx_s, u_s, out_ss_s, out_rs_s).start()
    for j in range(per_l):
        u_l[j, swap.rows(me, patches_l)] = tx_l[me * per_l + j]
    for j in range(per_s):
        u_s[j, swap.rows(me, patches_s)] = tx_s[me * per_s + j]

    for copy in to_x:
        copy.wait_recv()
    for copy in relay:
        copy.start()
    for copy in own_w:
        copy.wait()
    if shared:
        for copy in over_far:
            copy.start()
        for copy in over_far:
            copy.wait_recv()
        over_near.start()
        over_near.wait_recv()
        over_core.start()
        over_core.wait_recv()
        for k in range(2):
            for pieces, quarter in ((mine_w, x_peer), (theirs_w, diagonal)):
                for p in range(far - 1):
                    at = pl.ds(pl.multiple_of(quarter * patches_l + p * stride, 16), stride)
                    w_l[k, at] = pieces[k, p, :stride]
                w_s[k, swap.rows(quarter, patches_s)] = pieces[k, far - 1]
    for copy in to_core + relay:
        copy.wait_recv()
    b1_l, b1_s = column(b1_l_ref, token), column(b1_s_ref, token)
    b2_l, b2_s = column(b2_l_ref, patches_l), column(b2_s_ref, real_s)
    w1t_l[...] = w_l[0].T
    w1t_s[...] = w_s[0].T

    def mix(kind, j, cols, w1t, w2t, b1, h, slope, m, outs, tx, rx, bss, brs):
        for k in range(1, size):
            source = swap.other(k)
            swap.out(kind, j, me, source, tx, cols, *outs).wait_recv()
        g, d = gelu_pair(matmul(w1t[...], cols[j]) + b1)
        low = g.astype(BF)
        h[j] = low
        slope[j] = d.astype(BF)
        m[j] = matmul(w2t, low).astype(BF)
        for k in range(1, size):
            swap.back(kind, j, me, swap.other(k), m, rx, bss, brs).start()
        patches, per = (patches_l, per_l) if kind == "l" else (patches_s, per_s)
        rx[me * per + j] = m[j, swap.rows(me, patches)]

    for j in range(per_l):
        mix("l", j, u_l, w1t_l, w_l[1], b1_l, h_l, sl_l, m_l, (out_ss_l, out_rs_l), tx_l, rx_l, bk_ss_l, bk_rs_l)
    for j in range(per_s):
        mix("s", j, u_s, w1t_s, w_s[1], b1_s, h_s, sl_s, m_s, (out_ss_s, out_rs_s), tx_s, rx_s, bk_ss_s, bk_rs_s)

    small_rows = count_s * patches_s
    rows = y.shape[0]
    used = small_rows + count_l * patches_l
    y[0:small_rows, :] = jnp.zeros((small_rows, width), F32)
    if rows > used:
        y[used:rows, :] = jnp.zeros((rows - used, width), F32)
        spare = pltpu.make_async_copy(
            y.at[pl.ds(used, rows - used)], y_hbm.at[pl.ds(used, rows - used)], y_sem.at[count_l + count_s]
        )
        spare.start()

    def arrived(kind, unit, m, rx, bss, brs):
        per = per_l if kind == "l" else per_s
        owner = unit // per

        @pl.when(owner != me)
        def _():
            swap.back(kind, unit - owner * per, owner, me, m, rx, bss, brs).wait_recv()

    def y_copy(start, size, n):
        at = pl.ds(pl.multiple_of(start, 16), size)
        return pltpu.make_async_copy(y.at[at], y_hbm.at[at], y_sem.at[n])

    def y_l(n):
        return y_copy(small_rows + n * patches_l, patches_l, n)

    def y_s(n):
        return y_copy(n * patches_s, patches_s, count_l + n)

    def home_l(n, carry):
        arrived("l", 2 * n, m_l, rx_l, bk_ss_l, bk_rs_l)
        arrived("l", 2 * n + 1, m_l, rx_l, bk_ss_l, bk_rs_l)
        at = pl.ds(pl.multiple_of(small_rows + n * patches_l, 16), patches_l)
        y[at, :half] = xl[n, :, :half].astype(F32) + rx_l[2 * n].astype(F32) + b2_l
        y[at, half:] = xl[n, :, half:].astype(F32) + rx_l[2 * n + 1].astype(F32) + b2_l
        y_l(n).start()
        return carry

    def home_s(n, carry):
        arrived("s", n, m_s, rx_s, bk_ss_s, bk_rs_s)
        at = pl.ds(pl.multiple_of(n * patches_s, 16), real_s)
        y[at, :] = xs[n].astype(F32) + rx_s[n, :real_s].astype(F32) + b2_s
        y_s(n).start()
        return carry

    lax.fori_loop(0, count_l, home_l, 0)
    lax.fori_loop(0, count_s, home_s, 0)
    for copy in to_x + to_core + relay:
        copy.wait_send()
    if shared:
        for copy in over_far + [over_near, over_core]:
            copy.wait_send()
    for k in range(1, size):
        there = swap.other(k)
        for j in range(per_l):
            swap.out("l", j, there, me, tx_l, u_l, out_ss_l, out_rs_l).wait_send()
            swap.back("l", j, me, there, m_l, rx_l, bk_ss_l, bk_rs_l).wait_send()
        for j in range(per_s):
            swap.out("s", j, there, me, tx_s, u_s, out_ss_s, out_rs_s).wait_send()
            swap.back("s", j, me, there, m_s, rx_s, bk_ss_s, bk_rs_s).wait_send()
    for n in range(count_l):
        y_l(n).wait()
    for n in range(count_s):
        y_s(n).wait()
    if rows > used:
        spare.wait()


def token_forward(xl, xs, w1_l, w1_s, w2_l, w2_s, b1_l, b1_s, b2_l, b2_s, gain, bias, rows):
    size = lax.axis_size("blk")
    near, far = img_split(lax.axis_size("img"))
    count_l, patches_l, width = xl.shape
    real_s, count_s, _ = xs.shape
    patches_s = real_s + -real_s % 64
    token = w1_l.shape[1]
    half = width // 2
    per_l, per_s = count_l * 2 // size, count_s // size
    vmem = pl.BlockSpec(memory_space=pltpu.VMEM)
    V = pltpu.VMEM
    DMA = pltpu.SemaphoreType.DMA
    low = lambda *shape: jax.ShapeDtypeStruct(shape, BF)
    return pl.pallas_call(
        functools.partial(token_kernel, near, far, size),
        out_shape=(
            jax.ShapeDtypeStruct((rows, width), F32),
            low(per_l, size * patches_l, half), low(per_s, size * patches_s, width),
            low(per_l, token, half), low(per_s, token, width),
            low(per_l, token, half), low(per_s, token, width),
            low(2, size * patches_l, token), low(2, size * patches_s, token),
        ),
        in_specs=[vmem] * 12,
        out_specs=(ANY,) + (vmem,) * 8,
        scratch_shapes=[
            V((count_s, real_s, width), BF), V((2, patches_l + patches_s, token), BF),
            V((2, far, patches_s, token), BF), V((2, far, patches_s, token), BF),
            V((count_l * 2, patches_l, half), BF), V((count_s, patches_s, width), BF),
            V((token, size * patches_l), BF), V((token, size * patches_s), BF),
            V((per_l, size * patches_l, half), BF), V((per_s, size * patches_s, width), BF),
            V((count_l * 2, patches_l, half), BF), V((count_s, patches_s, width), BF),
            V((rows, width), F32),
            DMA((count_l + count_s + 1,)), DMA((1,)), DMA((2,)), DMA((3, 2)), DMA((3, 2)),
            DMA((count_l * 2,)), DMA((count_s,)), DMA((per_l, size)), DMA((per_s, size)),
            DMA((per_l, size)), DMA((per_s, size)), DMA((count_l * 2,)), DMA((count_s,)),
            DMA((2,)), DMA((far - 1,)), DMA((far - 1,)), DMA((1,)), DMA((1,)), DMA((2,)),
        ],
        compiler_params=pltpu.CompilerParams(
            collective_id=2, has_side_effects=True, vmem_limit_bytes=TOP
        ),
    )(xl, xs, w1_l, w1_s, w2_l, w2_s, b1_l, b1_s, b2_l, b2_s, gain, bias)


DEPTH = 2
SLAB = 512


def backward_kernel(
    near, far, size, far_inside,
    chunk_hbm, begun_hbm, ey_hbm,
    xl_in, xs_in, u_l_in, u_s_in, h_l_in, h_s_in, sl_l_in, sl_s_in, w_l_in, w_s_in, small_in, gain_ref,
    full_hbm, gx_hbm, tok_out, vec_out, gx_out,
    xl, xs_in_v, u_l, u_s, h_l, h_s, sl_l, sl_s, w_l, w_s, in_sem, xs, gx_s,
    ey, tx_l, tx_s, e_l, e_s, w2_l, w2_s, ep_l, ep_s, eu_l, eu_s, rx_l, rx_s,
    grads, tok_tx, tok_rx, tok_sum, tokn_tx, tokn_rx, tok_half, tokf_tx, tokf_rx, tokx_tx, tokx_rx,
    vec, vec_rx, vecn_rx, vecf_rx,
    ey_sem, gx_sem,
    out_ss_l, out_ss_s, out_rs_l, out_rs_s, bk_ss_l, bk_ss_s, bk_rs_l, bk_rs_s,
    tc_ss, tc_rs, tx_ss, tx_rs, tn_ss, tn_rs, tf_ss, tf_rs, taf_ss, taf_rs, tan_ss, tan_rs,
    v_ss, v_rs, vn_ss, vn_rs, vf_ss, vf_rs, *gather_sems,
):
    peers = Peers(near)
    me = peers.blk
    count_l, patches_l, width = xl.shape
    count_s, real_s, _ = xs.shape
    patches_s = tx_s.shape[1]
    token = w_l.shape[2]
    gain = row(gain_ref)
    half = width // 2
    per_l, per_s = count_l * 2 // size, count_s // size
    swap = Swap(peers, size, per_l, per_s, patches_l, patches_s)
    small_rows = count_s * patches_s
    x_peer = peers.at("x", 1 - peers.x)
    core_peer = peers.at("core", 1 - peers.core)

    def send(src, dst, ss, rs, device):
        return pltpu.make_async_remote_copy(
            src_ref=src, dst_ref=dst, send_sem=ss, recv_sem=rs, device_id=device, device_id_type=MESH
        )

    def others(axis, count):
        return [(j, peers.at(axis, lax.rem(peers.mine(axis) + j, count))) for j in range(1, count)]

    near_peers = others("near", near)
    far_peers = others("far", far)

    groups = chunk_hbm.shape[0]
    gather = Gather(peers, near, far, far_inside, chunk_hbm, full_hbm, gather_sems)
    waiting = list(range(groups))

    def tick():
        if waiting:
            k = waiting.pop(0)
            gather.third(k)
            if k + DEPTH < groups:
                gather.second(k + DEPTH)
            if k > 0:
                gather.fourth(k - 1)
            if k > 1:
                gather.fifth(k - 2)

    ey_in = pltpu.make_async_copy(ey_hbm, ey, ey_sem.at[0])
    ey_in.start()
    inputs = [
        pltpu.make_async_copy(src, dst, in_sem.at[n])
        for n, (src, dst) in enumerate((
            (w_l_in, w_l), (w_s_in, w_s), (sl_l_in, sl_l), (sl_s_in, sl_s), (u_l_in, u_l), (u_s_in, u_s),
            (h_l_in, h_l), (h_s_in, h_s), (xl_in, xl), (xs_in, xs_in_v),
        ))
    ]
    for copy in inputs:
        copy.start()
    greeted(greet_all(peers, size, near, far))
    if not far_inside:
        for k in range(groups):
            gather.first(k)
        for k in range(groups):
            gather.end_first(k)
    for k in range(DEPTH):
        gather.second(k)
    ey_in.wait()
    vec[...] = jnp.zeros_like(vec)
    vec[0:8, :] = small_in[...]
    def cast_l(n, carry):
        at = pl.ds(pl.multiple_of(small_rows + n * patches_l, 16), patches_l)
        et = ey[at, :].astype(BF)
        tx_l[2 * n] = et[:, :half]
        tx_l[2 * n + 1] = et[:, half:]
        return carry

    def cast_s(n, carry):
        at = pl.ds(pl.multiple_of(n * patches_s, 16), patches_s)
        tx_s[n] = ey[at, :].astype(BF)
        return carry

    lax.fori_loop(0, count_l, cast_l, 0)
    for j in range(per_l):
        for k in range(1, size):
            swap.out("l", j, swap.other(k), me, tx_l, e_l, out_ss_l, out_rs_l).start()
    lax.fori_loop(0, count_s, cast_s, 0)
    for j in range(per_s):
        for k in range(1, size):
            swap.out("s", j, swap.other(k), me, tx_s, e_s, out_ss_s, out_rs_s).start()
    for j in range(per_l):
        e_l[j, swap.rows(me, patches_l)] = tx_l[me * per_l + j]
    for j in range(per_s):
        e_s[j, swap.rows(me, patches_s)] = tx_s[me * per_s + j]
    for copy in inputs:
        copy.wait()
    for n in range(count_s):
        xs[n] = xs_in_v[:, n, :]
    w2_l[...] = w_l[1].T
    w2_s[...] = w_s[1].T
    ones_l = jnp.ones((8, half), BF)
    ones_s = jnp.ones((8, width), BF)
    vec[16:24, 0:patches_l] = lax.fori_loop(
        0, 2 * count_l, lambda n, total: total + matmul_nt(ones_l, tx_l[n]), jnp.zeros((8, patches_l), F32)
    )
    vec[16:24, half:half + patches_s] = lax.fori_loop(
        0, count_s, lambda n, total: total + matmul_nt(ones_s, tx_s[n]), jnp.zeros((8, patches_s), F32)
    )

    def unmix(kind, j, e, w2, w1, slope, ep, eu, outs, tx, rx, bss, brs):
        for k in range(1, size):
            swap.out(kind, j, me, swap.other(k), tx, e, *outs).wait_recv()
        low = (matmul(w2[...], e[j]) * slope[j].astype(F32)).astype(BF)
        ep[j] = low
        eu[j] = matmul(w1, low).astype(BF)
        for k in range(1, size):
            swap.back(kind, j, me, swap.other(k), eu, rx, bss, brs).start()
        patches, per = (patches_l, per_l) if kind == "l" else (patches_s, per_s)
        rx[me * per + j] = eu[j, swap.rows(me, patches)]

    for j in range(per_l):
        tick()
        unmix("l", j, e_l, w2_l, w_l[0], sl_l, ep_l, eu_l, (out_ss_l, out_rs_l), tx_l, rx_l, bk_ss_l, bk_rs_l)
    tick()
    for j in range(per_s):
        unmix("s", j, e_s, w2_s, w_s[0], sl_s, ep_s, eu_s, (out_ss_s, out_rs_s), tx_s, rx_s, bk_ss_s, bk_rs_s)

    vec[8:16, 0:half] = sum(matmul_nt(ones_l, ep_l[j]) for j in range(per_l))
    vec[8:16, half:width] = sum(matmul_nt(ones_s, ep_s[j]) for j in range(per_s))
    top = 2 * patches_l + 2 * patches_s
    begin = 0
    for left, right, per, patches in (
        (u_l, ep_l, per_l, patches_l), (e_l, h_l, per_l, patches_l),
        (u_s, ep_s, per_s, patches_s), (e_s, h_s, per_s, patches_s),
    ):
        value = sum(matmul_nt(left[j], right[j]) for j in range(per))
        for q in range(size):
            grads[q, begin:begin + patches] = value[q * patches:(q + 1) * patches]
        begin += patches
    for p in range(2):
        tok_tx[p] = grads[p * 2 + 1 - peers.core, 0:top].astype(BF)
    t_core = send(tok_tx, tok_rx, tc_ss.at[0], tc_rs.at[0], core_peer)
    t_core.start()
    tick()
    t_core.wait_recv()
    there = 1 - peers.x
    tokx_tx[...] = (grads[there * 2 + peers.core, 0:top] + tok_rx[there].astype(F32)).astype(BF)
    t_x = send(tokx_tx, tokx_rx, tx_ss.at[0], tx_rs.at[0], x_peer)
    t_x.start()
    if SLAB > top:
        tok_sum[top:SLAB, :] = jnp.zeros((SLAB - top, token), F32)
    tok_sum[0:top, :] = grads[me, 0:top] + tok_rx[peers.x].astype(F32)
    tick()
    tick()

    def piece(place, size):
        return pl.ds(pl.multiple_of(place * size, size), size)

    def arrived(kind, unit, eu, rx, bss, brs):
        per = per_l if kind == "l" else per_s
        owner = unit // per

        @pl.when(owner != me)
        def _():
            swap.back(kind, unit - owner * per, owner, me, eu, rx, bss, brs).wait_recv()

    def norm_back(x, eu, at):
        unit, scale = unit_rows(x.astype(F32))
        d = eu * gain
        m1 = jnp.mean(d, axis=-1, keepdims=True)
        m2 = jnp.mean(d * unit, axis=-1, keepdims=True)
        vec[7:8, :] += jnp.sum(eu * unit, axis=0, keepdims=True)
        vec[9:10, :] += jnp.sum(eu, axis=0, keepdims=True)
        return ey[at, :] + scale * (d - m1 - unit * m2)

    def gx_copy(n):
        at = pl.ds(pl.multiple_of(small_rows + n * patches_l, 16), patches_l)
        return pltpu.make_async_copy(ey.at[at], gx_hbm.at[n], gx_sem.at[n])

    def home_l(n, carry):
        arrived("l", 2 * n, eu_l, rx_l, bk_ss_l, bk_rs_l)
        arrived("l", 2 * n + 1, eu_l, rx_l, bk_ss_l, bk_rs_l)
        at = pl.ds(pl.multiple_of(small_rows + n * patches_l, 16), patches_l)
        eu = jnp.concatenate([rx_l[2 * n], rx_l[2 * n + 1]], axis=1).astype(F32)
        ey[at, :] = norm_back(xl[n], eu, at)
        gx_copy(n).start()
        return carry

    def home_s(n, carry):
        arrived("s", n, eu_s, rx_s, bk_ss_s, bk_rs_s)
        at = pl.ds(pl.multiple_of(n * patches_s, 16), real_s)
        gx_s[n] = norm_back(xs[n], rx_s[n, :real_s].astype(F32), at)
        return carry

    vec[9:10, :] = jnp.zeros((1, width), F32)
    lax.fori_loop(0, count_l // 2, home_l, 0)
    tick()
    lax.fori_loop(count_l // 2, count_l, home_l, 0)
    lax.fori_loop(0, count_s, home_s, 0)
    for n in range(count_s):
        gx_out[:, n, :] = gx_s[n]
    both = vec.at[0:16]
    v_core = send(both, vec_rx.at[0], v_ss.at[0], v_rs.at[0], core_peer)
    v_core.start()
    tick()
    t_x.wait_recv()
    tok_sum[0:top, :] += tokx_rx[...].astype(F32)
    part_n = SLAB // near
    part_f = part_n // far
    t_near, t_far, ta_far, ta_near = [], [], [], []
    if far_inside:
        for j, device in near_peers:
            tokn_tx[j - 1] = tok_sum[piece(lax.rem(peers.near + j, near), part_n), :].astype(BF)
            copy = send(tokn_tx.at[j - 1], tokn_rx.at[j - 1], tn_ss.at[j - 1], tn_rs.at[j - 1], device)
            copy.start()
            t_near.append(copy)
    else:
        tok_out[...] = tok_sum[...].astype(BF)
    v_core.wait()
    vec[0:16, :] += vec_rx[0]
    v_x = send(both, vec_rx.at[1], v_ss.at[1], v_rs.at[1], x_peer)
    v_x.start()
    tick()
    v_x.wait()
    vec[0:16, :] += vec_rx[1]
    v_near = [send(vec, vecn_rx.at[j - 1], vn_ss.at[j - 1], vn_rs.at[j - 1], device) for j, device in near_peers]
    for copy in v_near:
        copy.start()
    if far_inside:
        for copy in t_near:
            copy.wait_recv()
        tok_half[...] = tok_sum[piece(peers.near, part_n), :]
        for j in range(near - 1):
            tok_half[...] += tokn_rx[j].astype(F32)
        for j, device in far_peers:
            tokf_tx[j - 1] = tok_half[piece(lax.rem(peers.far + j, far), part_f), :].astype(BF)
            copy = send(tokf_tx.at[j - 1], tokf_rx.at[j - 1], tf_ss.at[j - 1], tf_rs.at[j - 1], device)
            copy.start()
            t_far.append(copy)
    tick()
    for copy in v_near:
        copy.wait()
    for j in range(near - 1):
        vec[...] += vecn_rx[j]
    v_far = [send(vec, vecf_rx.at[j - 1], vf_ss.at[j - 1], vf_rs.at[j - 1], device) for j, device in far_peers]
    for copy in v_far:
        copy.start()
    if far_inside:
        for copy in t_far:
            copy.wait_recv()
        value = tok_half[piece(peers.far, part_f), :]
        for j in range(far - 1):
            value = value + tokf_rx[j].astype(F32)
        span = tok_out.at[piece(peers.near * far + peers.far, part_f)]
        span[...] = value.astype(BF)
        for j, device in far_peers:
            copy = send(span, span, taf_ss.at[j - 1], taf_rs.at[j - 1], device)
            copy.start()
            ta_far.append(copy)
    tick()
    for copy in v_far:
        copy.wait()
    value = vec[...]
    for j in range(far - 1):
        value = value + vecf_rx[j]
    vec_out[...] = value
    if far_inside:
        for copy in ta_far:
            copy.wait_recv()
        span = tok_out.at[piece(peers.near, part_n)]
        for j, device in near_peers:
            copy = send(span, span, tan_ss.at[j - 1], tan_rs.at[j - 1], device)
            copy.start()
            ta_near.append(copy)
    while waiting:
        tick()
    gather.fourth(groups - 1)
    for k in (groups - 2, groups - 1):
        gather.fifth(k)
    for copy in ta_near:
        copy.wait_recv()

    for copy in [t_core, t_x] + t_near + t_far + ta_far + ta_near:
        copy.wait_send()
    for k in range(1, size):
        there = swap.other(k)
        for j in range(per_l):
            swap.out("l", j, there, me, tx_l, e_l, out_ss_l, out_rs_l).wait_send()
            swap.back("l", j, me, there, eu_l, rx_l, bk_ss_l, bk_rs_l).wait_send()
        for j in range(per_s):
            swap.out("s", j, there, me, tx_s, e_s, out_ss_s, out_rs_s).wait_send()
            swap.back("s", j, me, there, eu_s, rx_s, bk_ss_s, bk_rs_s).wait_send()
    for k in range(groups):
        gather.drain(k)
    for n in range(count_l):
        gx_copy(n).wait()


def backward(chunk, begun, ey, xl, xs, saved, small, gain):
    size = lax.axis_size("blk")
    near, far = img_split(lax.axis_size("img"))
    rows, width = ey.shape
    far_inside = width % (near * far * 2 * 16) == 0
    u_l, u_s, h_l, h_s, sl_l, sl_s, w_l, w_s = saved
    count_l, patches_l, _ = xl.shape
    real_s, count_s, _ = xs.shape
    patches_s = real_s + -real_s % 64
    token = w_l.shape[2]
    half = width // 2
    per_l, per_s = u_l.shape[0], u_s.shape[0]
    groups, each, _ = chunk.shape
    vmem = pl.BlockSpec(memory_space=pltpu.VMEM)
    V = pltpu.VMEM
    DMA = pltpu.SemaphoreType.DMA
    n1, f1 = near - 1, far - 1
    top = 2 * patches_l + 2 * patches_s
    part_n = SLAB // near
    part_f = max(part_n // far, 16)
    return pl.pallas_call(
        functools.partial(backward_kernel, near, far, size, far_inside),
        out_shape=(
            jax.ShapeDtypeStruct(begun.shape, BF),
            jax.ShapeDtypeStruct(xl.shape, F32),
            jax.ShapeDtypeStruct((SLAB, token), BF),
            jax.ShapeDtypeStruct((24, width), F32),
            jax.ShapeDtypeStruct(xs.shape, F32),
        ),
        in_specs=[ANY] * 13 + [vmem] * 2,
        out_specs=(ANY, ANY, vmem, vmem, vmem),
        scratch_shapes=[
            V(xl.shape, BF), V(xs.shape, BF), V(u_l.shape, BF), V(u_s.shape, BF), V(h_l.shape, BF), V(h_s.shape, BF),
            V(sl_l.shape, BF), V(sl_s.shape, BF), V(w_l.shape, BF), V(w_s.shape, BF), DMA((10,)),
            V((count_s, real_s, width), BF), V((count_s, real_s, width), F32),
            V((rows, width), F32),
            V((count_l * 2, patches_l, half), BF), V((count_s, patches_s, width), BF),
            V(u_l.shape, BF), V(u_s.shape, BF),
            V((token, size * patches_l), BF), V((token, size * patches_s), BF),
            V(h_l.shape, BF), V(h_s.shape, BF), V(u_l.shape, BF), V(u_s.shape, BF),
            V((count_l * 2, patches_l, half), BF), V((count_s, patches_s, width), BF),
            V((size, top, token), F32), V((2, top, token), BF), V((2, top, token), BF), V((SLAB, token), F32),
            V((n1, part_n, token), BF), V((n1, part_n, token), BF), V((part_n, token), F32),
            V((f1, part_f, token), BF), V((f1, part_f, token), BF), V((top, token), BF), V((top, token), BF),
            V((24, width), F32), V((2, 16, width), F32), V((n1, 24, width), F32), V((f1, 24, width), F32),
            DMA((1,)), DMA((count_l,)),
            DMA((count_l * 2,)), DMA((count_s,)), DMA((per_l, size)), DMA((per_s, size)),
            DMA((per_l, size)), DMA((per_s, size)), DMA((count_l * 2,)), DMA((count_s,)),
            DMA((1,)), DMA((1,)), DMA((1,)), DMA((1,)), DMA((n1,)), DMA((n1,)), DMA((f1,)), DMA((f1,)),
            DMA((f1,)), DMA((f1,)), DMA((n1,)), DMA((n1,)),
            DMA((2,)), DMA((2,)), DMA((n1,)), DMA((n1,)), DMA((f1,)), DMA((f1,)),
        ] + Gather.sems(groups, near, far),
        input_output_aliases={1: 0},
        compiler_params=pltpu.CompilerParams(
            collective_id=1, has_side_effects=True, vmem_limit_bytes=TOP
        ),
    )(chunk, begun, ey, xl, xs, u_l, u_s, h_l, h_s, sl_l, sl_s, w_l, w_s, small, gain)


def widen_kernel(
    first, second, tok, vec, out_l_in, gx_l_in, out_s_in, gx_s_in,
    out_l, gx_l, out_s, gx_s, out_first, out_second, gain1, bias1, w1_s, b1_s, w2_s, b2_s, w1_l, b1_l, w2_l, b2_l, gain2, bias2, b1, b2,
):
    out_l[...] = out_l_in[...]
    gx_l[...] = gx_l_in[...]
    for k in range(first.shape[1]):
        out_first[:, k * TILE:(k + 1) * TILE] = first[0, k].astype(F32)
        out_second[k * TILE:(k + 1) * TILE, :] = second[0, k].astype(F32).T

    @pl.when(pl.program_id(0) == 0)
    def _():
        out_s[...] = out_s_in[...]
        gx_s[...] = gx_s_in[...]
        width = vec.shape[1]
        half = width // 2
        large, small = w1_l.shape[0], w1_s.shape[0]
        wide = small + -small % 64
        at = 2 * large
        w1_l[...] = tok[0:large, :].astype(F32)
        w2_l[...] = tok[large:at, :].astype(F32)
        w1_s[...] = tok[at:at + wide, :].astype(F32)[:small]
        w2_s[...] = tok[at + wide:at + 2 * wide, :].astype(F32)[:small]
        gain1[...] = vec[7, :]
        bias1[...] = vec[9, :]
        b1_l[...] = vec[8, 0:half]
        b1_s[...] = vec[8, half:width]
        b2_l[...] = vec[16, 0:large]
        b2_s[...] = vec[16, half:half + small]
        gain2[...] = vec[5, :]
        bias2[...] = vec[6, :]
        for k in range(b1.shape[0] // width):
            b1[k * width:(k + 1) * width] = vec[k, :]
        b2[...] = vec[4, :]


def widen(full, tok, vec, out_l, gx_l, out_s, gx_s):
    full = full.reshape(full.shape[0], full.shape[1], -1, TILE)
    _, groups, width, _ = full.shape
    count_l, patches_l, _ = out_l.shape
    patches_s = out_s.shape[0]
    hidden = groups * TILE
    token = tok.shape[1]
    step = 2 * TILE
    shapes = (
        (width,), (width,), (patches_s, token), (token,), (patches_s, token), (patches_s,),
        (patches_l, token), (token,), (patches_l, token), (patches_l,), (width,), (width,), (hidden,), (width,),
    )

    def whole(shape):
        return pl.BlockSpec(shape, lambda i: (0,) * len(shape))

    image = pl.BlockSpec((1, patches_l, width), lambda i: (jnp.minimum(i, count_l - 1), 0, 0))
    return pl.pallas_call(
        widen_kernel,
        grid=(hidden // step,),
        out_shape=tuple(jax.ShapeDtypeStruct(a.shape, a.dtype) for a in (out_l, gx_l, out_s, gx_s)) + (
            jax.ShapeDtypeStruct((width, hidden), F32), jax.ShapeDtypeStruct((hidden, width), F32),
        ) + tuple(jax.ShapeDtypeStruct(shape, F32) for shape in shapes),
        in_specs=[
            pl.BlockSpec((1, 2, width, TILE), lambda i: (0, i, 0, 0)),
            pl.BlockSpec((1, 2, width, TILE), lambda i: (1, i, 0, 0)),
            whole(tok.shape), whole(vec.shape), image, image, whole(out_s.shape), whole(gx_s.shape),
        ],
        out_specs=(
            image, image, whole(out_s.shape), whole(gx_s.shape),
            pl.BlockSpec((width, step), lambda i: (0, i)), pl.BlockSpec((step, width), lambda i: (i, 0)),
        ) + tuple(whole(shape) for shape in shapes),
        compiler_params=pltpu.CompilerParams(vmem_limit_bytes=TOP),
    )(full, full, tok, vec, out_l, gx_l, out_s, gx_s)


def local(
    x_small, x_large, live_counts, ln1_gain, ln1_bias,
    tok_w1_small, tok_b1_small, tok_w2_small, tok_b2_small,
    tok_w1_large, tok_b1_large, tok_w2_large, tok_b2_large,
    ln2_gain, ln2_bias, ch_w1, ch_b1, ch_w2, ch_b2, cot_small, cot_large,
):
    width = x_small.shape[2]
    patches_s, patches_l = x_small.shape[1], x_large.shape[1]
    rows = x_small.shape[0] * (patches_s + -patches_s % 64) + x_large.shape[0] * patches_l
    xs = x_small.transpose(1, 0, 2)
    y, *saved = token_forward(
        x_large, xs, tok_w1_large, tok_w1_small, tok_w2_large.T, tok_w2_small.T,
        tok_b1_large, tok_b1_small, tok_b2_large, tok_b2_small, ln1_gain, ln1_bias, rows + -rows % (3 * LANES),
    )
    out_large, ey, chunk, small_grads, out_small, begun = channel(
        y, live_counts, cot_large, cot_small.transpose(1, 0, 2), ch_w1, ch_w2, ch_b1, ln2_gain, ln2_bias, ch_b2
    )
    near, far = img_split(lax.axis_size("img"))
    far_inside = width % (near * far * 2 * 16) == 0
    if not far_inside:
        same = [[a * near + b for a in range(far)] for b in range(near)]
        chunk = lax.psum(chunk.astype(F32), "img", axis_index_groups=same).astype(BF)
    full, gx_large, tok, vec, gx_small = backward(
        chunk, begun, ey, x_large, xs, saved, small_grads, ln1_gain
    )
    if not far_inside:
        tok = lax.psum(tok.astype(F32), "img")
    (
        out_large, gx_large, out_small, gx_small, grad_ch_w1, grad_ch_w2, gain1, bias1, w1_s, b1_s, w2_s, b2_s, w1_l, b1_l, w2_l, b2_l,
        gain2, bias2, grad_b1, grad_b2,
    ) = widen(full, tok, vec, out_large, gx_large, out_small, gx_small)
    return (
        out_small.transpose(1, 0, 2), out_large, gx_small.transpose(1, 0, 2), gx_large, gain1, bias1,
        w1_s, b1_s, w2_s.T, b2_s, w1_l, b1_l, w2_l.T, b2_l,
        gain2, bias2, grad_ch_w1, grad_b1, grad_ch_w2, grad_b2,
    )


def solution(mesh):
    image = P("img", "blk", None)
    whole = P()
    rows = P("blk", None)
    columns = P(None, "blk")
    vector = P("blk")
    in_specs = (
        image, image, P("img", None), whole, whole,
        rows, whole, columns, vector, rows, whole, columns, vector,
        whole, whole, whole, whole, whole, whole, image, image,
    )
    out_specs = (
        image, image, image, image, whole, whole,
        rows, whole, columns, vector, rows, whole, columns, vector,
        whole, whole, whole, whole, whole, whole,
    )
    return jax.shard_map(local, mesh=mesh, in_specs=in_specs, out_specs=out_specs, check_vma=False)
```
